32 devices in a mesh: ctx: 16 (over z, x, core), head: 2 (over y).
Axes of the slice: x: 2, y: 2, z: 4, core: 2. Of those that a mesh axis runs over, the one named last changes fastest.
Arguments:
- tokens: bfloat16 [4096, 3072], P('ctx', 'head'), may hold values from -48 to 48
- block_order: int32 [32], replicated, may hold values from 0 to 31, each once
- block_mask: int32 [32, 32], replicated, may hold values from 0 to 1, as said below
- w_query: bfloat16 [3072, 3072], P(None, 'head'), may hold values from -0.109375 to 0.109375
- w_key: bfloat16 [3072, 3072], P(None, 'head'), may hold values from -0.109375 to 0.109375
- w_value: bfloat16 [3072, 3072], P(None, 'head'), may hold values from -0.109375 to 0.109375
- w_out: bfloat16 [3072, 3072], P('head'), may hold values from -0.109375 to 0.109375
Outputs:
- mixed: bfloat16 [4096, 3072], P('ctx', 'head')
The draws below stay inside these ranges and needn't reach their ends.
Inputs may be any that keep to these rules, and one draw needn't show every extreme that they name: `block_order`: a permutation of the block numbers. block_mask[f, f] = 1 for every block f.
All inputs are finite; a program needn't handle non-finite values.
Results may differ from the reference program's by a relative error of at most 0.02.
The reference program's roundings to bfloat16 on the way count: a program that leaves them out, or rounds other values in their place, can miss the bound.
Values may be sent and summed in bfloat16 or wider, within the bound.
No kernel may reach another device: no remote copies, remote signals or barrier semaphores. Data moves between devices by JAX's collectives and lax.ppermute only.
A program may use at most 128 MiB of HBM per device.

```python
import jax
import jax.numpy as jnp
from jax import lax

D = 3072
HEADS = 24
HEAD_DIM = 128
BLOCK = 128
FRAME_BLOCKS = 8
TOKENS = 4096
NB = 32
N_HEAD = 2


def draw_tokens(key, part):
    return jnp.clip(jax.random.normal(key, (TOKENS, D), jnp.float32), -6.0, 6.0).astype(jnp.bfloat16)


def draw_block_mask(key, part):
    places = jnp.arange(NB, dtype=jnp.int32)
    frame_index = places // FRAME_BLOCKS
    spot_index = places % FRAME_BLOCKS
    distance = jnp.abs(frame_index[:, None] - frame_index[None, :])
    level = jnp.zeros((NB, NB), jnp.int32)
    for power in range(16):
        level = level + (distance >= 2 ** power).astype(jnp.int32)
    band_width = jnp.maximum(jnp.right_shift(jnp.int32(FRAME_BLOCKS), level), 1)
    radial = jnp.abs(spot_index[:, None] - spot_index[None, :]) < band_width
    extra = jax.random.randint(key, (NB, NB), 0, 8) == 0
    diagonal = places[:, None] == places[None, :]
    return (radial | extra | diagonal).astype(jnp.int32)


def steps_of(own_key, dims, shards, least, high):
    factor_of = 1.0
    for dim, shards_of in shards:
        draws = jax.random.uniform(jax.random.fold_in(jax.random.fold_in(own_key, 6), dim), (shards_of,), jnp.float32, least / len(shards), high / len(shards))
        factor_of = factor_of * jnp.repeat(jnp.exp(draws), dims[dim] // shards_of).reshape((-1,) + (1,) * (len(dims) - 1 - dim))
    return factor_of


def normal_values(own_key, extent, scale, most, cuts=(), kind=jnp.bfloat16):
    result = scale * jax.random.normal(own_key, extent, jnp.float32)
    if cuts:
        result = result * steps_of(own_key, extent, cuts, -0.22, 0.18)
    return jnp.clip(result, -most, most).astype(kind)


def setup_inputs(seed: int = 0) -> dict:
    arg_keys = jax.random.split(jax.random.key(seed), 8)
    tokens = draw_tokens(jax.random.fold_in(arg_keys[7], 71), 0)
    block_order = jax.random.permutation(arg_keys[1], NB).astype(jnp.int32)
    block_mask = draw_block_mask(jax.random.fold_in(arg_keys[7], 71), 0)
    w_query = normal_values(arg_keys[3], (D, D), D ** -0.5, 0.109375, ((1, 2),))
    w_key = normal_values(arg_keys[4], (D, D), D ** -0.5, 0.109375, ((1, 2),))
    w_value = normal_values(arg_keys[5], (D, D), D ** -0.5, 0.109375, ((1, 2),))
    w_out = normal_values(arg_keys[6], (D, D), D ** -0.5, 0.109375, ((0, 2),))
    return {"tokens": tokens, "block_order": block_order, "block_mask": block_mask, "w_query": w_query, "w_key": w_key, "w_value": w_value, "w_out": w_out}


def reference(tokens, block_order, block_mask, w_query, w_key, w_value, w_out):
    query_rows = jnp.dot(tokens, w_query, preferred_element_type=jnp.float32).astype(jnp.bfloat16)
    key_rows = jnp.dot(tokens, w_key, preferred_element_type=jnp.float32).astype(jnp.bfloat16)
    value_rows = jnp.dot(tokens, w_value, preferred_element_type=jnp.float32).astype(jnp.bfloat16)
    query_tiles = query_rows.astype(jnp.float32).reshape(TOKENS // BLOCK, BLOCK, HEADS, HEAD_DIM)
    key_all = key_rows.astype(jnp.float32).reshape(TOKENS, HEADS, HEAD_DIM)
    value_all = value_rows.astype(jnp.float32).reshape(TOKENS, HEADS, HEAD_DIM)
    cycle_live = block_mask[block_order][:, block_order]
    inv_root = 1.0 / (HEAD_DIM ** 0.5)

    def one_block(inputs):
        query_tile, live_row = inputs
        key_keep = jnp.repeat(live_row, BLOCK) > 0
        scores = jnp.einsum("qhd,khd->hqk", query_tile, key_all) * inv_root
        allowed = key_keep[None, None, :]
        row_top = jnp.max(jnp.where(allowed, scores, -1e30), axis=-1)
        weights = jnp.where(allowed, jnp.exp(scores - row_top[..., None]), 0.0)
        row_total = jnp.sum(weights, axis=-1)
        rounded = weights.astype(jnp.bfloat16).astype(jnp.float32)
        attended_tile = jnp.einsum("hqk,khd->hqd", rounded, value_all) / row_total[..., None]
        return attended_tile.transpose(1, 0, 2).reshape(BLOCK, D).astype(jnp.bfloat16)

    attended = lax.map(one_block, (query_tiles, cycle_live)).reshape(TOKENS, D)
    group_width = D // N_HEAD
    mixed_sum = jnp.zeros((TOKENS, D), jnp.float32)
    for group in range(N_HEAD):
        group_part = jnp.dot(attended[:, group * group_width:(group + 1) * group_width],
                             w_out[group * group_width:(group + 1) * group_width],
                             preferred_element_type=jnp.float32).astype(jnp.bfloat16)
        mixed_sum = mixed_sum + group_part.astype(jnp.float32)
    return mixed_sum.astype(jnp.bfloat16)
```

```python
import functools
import math

import jax
import jax.numpy as jnp
from jax import lax
from jax.experimental import pallas as pl
from jax.experimental.pallas import tpu as pltpu
from jax.sharding import PartitionSpec as P

HEAD_DIM = 128
BLOCK = 128
Z, X, C = 4, 2, 2
MIB = 1 << 20
BF16, F32 = jnp.bfloat16, jnp.float32


def place(z, x, c):
    return (z * X + x) * C + c


def hop(dz, dx, dc):
    return [
        (place(z, x, c), place(z ^ dz, x ^ dx, c ^ dc))
        for z in range(Z)
        for x in range(X)
        for c in range(C)
    ]


def params(mib):
    return pltpu.CompilerParams(vmem_limit_bytes=mib * MIB)


def project(where, own, other, weights, width, first):
    rows, half = own.shape
    kinds = len(weights)

    def column(i, s):
        return (s[1] ^ i) * first[1] + first[0]

    def body(s, own_ref, other_ref, *refs):
        mine, theirs = refs[:kinds], refs[kinds : 2 * kinds]
        outs = refs[2 * kinds :]
        step = pl.program_id(0)
        w_mine = jnp.concatenate([r[...] for r in mine], axis=1)
        w_theirs = jnp.concatenate([r[...] for r in theirs], axis=1)
        total = jnp.dot(own_ref[...], w_mine, preferred_element_type=F32)
        total += jnp.dot(other_ref[...], w_theirs, preferred_element_type=F32)
        total = total.astype(BF16)
        for i in range(Z):

            @pl.when(step == i)
            def _(i=i):
                for k in range(kinds):
                    outs[i][k] = total[:, k * width : (k + 1) * width]

    row_spec = pl.BlockSpec((rows, half), lambda i, s: (0, 0))
    mine_spec = pl.BlockSpec((half, width), lambda i, s: (s[0], column(i, s)))
    theirs_spec = pl.BlockSpec((half, width), lambda i, s: (1 - s[0], column(i, s)))
    return pl.pallas_call(
        body,
        grid_spec=pltpu.PrefetchScalarGridSpec(
            num_scalar_prefetch=1,
            grid=(Z,),
            in_specs=[row_spec, row_spec] + [mine_spec] * kinds + [theirs_spec] * kinds,
            out_specs=[pl.BlockSpec((kinds, rows, width), lambda i, s: (0, 0, 0))] * Z,
        ),
        out_shape=[jax.ShapeDtypeStruct((kinds, rows, width), BF16)] * Z,
        compiler_params=params(24),
        cost_estimate=pl.CostEstimate(
            flops=2 * rows * 2 * half * width * kinds * Z,
            bytes_accessed=2 * 2 * half * width * kinds * Z,
            transcendentals=0,
        ),
    )(where, own, other, *weights, *weights)


def attend(queries, parts, bias, head):
    rows = queries[0].shape[1]
    tile = parts[0].shape[2]
    tiles = len(parts) * Z
    key_count = tiles * tile
    scale = math.log2(math.e) / math.sqrt(HEAD_DIM)
    per = rows // BLOCK

    def body(*refs):
        q_refs, kv_refs, bias_ref = refs[:Z], refs[Z : Z + len(parts)], refs[Z + len(parts)]
        outs = refs[Z + len(parts) + 1 : Z + len(parts) + 1 + Z]
        s_ref, q_ref = refs[-2:]
        step = pl.program_id(0)
        for i in range(Z):

            @pl.when(step == i)
            def _(i=i):
                q_ref[...] = q_refs[i][0]

        query = q_ref[...]
        top = jnp.full((rows, 1), -jnp.inf, F32)
        for t in range(tiles):
            key = kv_refs[t // Z][t % Z, 0]
            score = lax.dot_general(
                query, key, (((1,), (1,)), ((), ())), preferred_element_type=F32
            )
            keep = [
                jnp.broadcast_to(
                    bias_ref[pl.ds(step * per + r, 1), t * tile : (t + 1) * tile], (BLOCK, tile)
                )
                for r in range(per)
            ]
            score = score + jnp.concatenate(keep, axis=0)
            s_ref[:, t * tile : (t + 1) * tile] = score
            top = jnp.maximum(top, jnp.max(score, axis=1, keepdims=True))
        shift = top * scale
        total = jnp.zeros((rows, 1), F32)
        accum = jnp.zeros((rows, HEAD_DIM), F32)
        for t in range(tiles):
            weight = jnp.exp2(s_ref[:, t * tile : (t + 1) * tile] * scale - shift)
            total += jnp.sum(weight, axis=1, keepdims=True)
            accum += jnp.dot(
                weight.astype(BF16), kv_refs[t // Z][t % Z, 1], preferred_element_type=F32
            )
        result = (accum / total).astype(BF16)
        for i in range(Z):

            @pl.when(step == i)
            def _(i=i):
                outs[i][...] = result

    return pl.pallas_call(
        body,
        grid=(Z,),
        in_specs=[pl.BlockSpec((1, rows, HEAD_DIM), lambda i: (0, 0, head))] * Z
        + [pl.BlockSpec(p.shape, lambda i: (0, 0, 0, 0)) for p in parts]
        + [pl.BlockSpec(bias.shape, lambda i: (0, 0))],
        out_specs=[pl.BlockSpec((rows, HEAD_DIM), lambda i: (0, 0))] * Z,
        out_shape=[jax.ShapeDtypeStruct((rows, HEAD_DIM), BF16)] * Z,
        scratch_shapes=[pltpu.VMEM((rows, key_count), F32), pltpu.VMEM((rows, HEAD_DIM), BF16)],
        compiler_params=params(32),
        cost_estimate=pl.CostEstimate(
            flops=4 * Z * rows * key_count * HEAD_DIM,
            bytes_accessed=4 * key_count * HEAD_DIM,
            transcendentals=Z * rows * key_count,
        ),
    )(*queries, *parts, bias)


def mix(where, attended, w_out, flip, step_width):
    rows = attended[0].shape[0]
    depth = w_out.shape[0] // Z
    half = w_out.shape[1] // 2
    steps = half // step_width
    count = len(attended)

    def body(s, *refs):
        rows_all = jnp.concatenate([r[...] for r in refs[:count]], axis=1)
        weight = jnp.concatenate([r[...] for r in refs[count : count + Z]], axis=0)
        refs[-1][...] = jnp.dot(rows_all, weight, preferred_element_type=F32).astype(BF16)

    def weight_spec(dz):
        return pl.BlockSpec(
            (depth, step_width),
            lambda i, s: (s[1] ^ dz, (1 - s[0] if flip else s[0]) * steps + i),
        )

    return pl.pallas_call(
        body,
        grid_spec=pltpu.PrefetchScalarGridSpec(
            num_scalar_prefetch=1,
            grid=(steps,),
            in_specs=[pl.BlockSpec(a.shape, lambda i, s: (0, 0)) for a in attended]
            + [weight_spec(dz) for dz in range(Z)],
            out_specs=pl.BlockSpec((rows, step_width), lambda i, s: (0, i)),
        ),
        out_shape=jax.ShapeDtypeStruct((rows, half), BF16),
        compiler_params=params(24),
        cost_estimate=pl.CostEstimate(
            flops=2 * rows * Z * depth * half,
            bytes_accessed=2 * Z * depth * half,
            transcendentals=0,
        ),
    )(where, *attended, *([w_out] * Z))


def split_heads(tokens, block_order, block_mask, w_query, w_key, w_value, w_out):
    rows, half = tokens.shape
    group_heads = w_query.shape[1] // HEAD_DIM // Z
    block_count = block_order.shape[0]
    per = rows // BLOCK
    ctx = lax.axis_index("ctx")
    y = lax.axis_index("head")
    z, x, c = ctx // (X * C), (ctx // C) % X, ctx % C
    where = jnp.stack([y, z]).astype(jnp.int32)

    other = lax.ppermute(tokens, "head", [(0, 1), (1, 0)])

    def blocks(pairs):
        first = jnp.stack([place(z ^ dz, x ^ dx, c ^ dc) for dz, dx, dc in pairs]) * per
        return (first[:, None] + jnp.arange(per)[None, :]).reshape(-1)

    query_blocks = blocks([(dz, 0, 0) for dz in range(Z)])
    key_blocks = blocks([(dz, dx, dc) for dc, dx in ((0, 0), (0, 1), (1, 0), (1, 1)) for dz in range(Z)])
    frames = jnp.arange(block_count, dtype=jnp.int32)
    order_hot = (block_order[:, None] == frames[None, :]).astype(F32)

    def pick(wanted):
        place_hot = (wanted[:, None] == frames[None, :]).astype(F32)
        return jnp.dot(place_hot, order_hot)

    live = jnp.dot(
        jnp.dot(pick(query_blocks), block_mask.astype(F32)), pick(key_blocks).T
    )
    bias = jnp.repeat(jnp.where(live > 0.5, 0.0, -1e30).astype(F32), BLOCK, axis=1)

    def share(pieces):
        return [pieces[0]] + [lax.ppermute(pieces[dz], "ctx", hop(dz, 0, 0)) for dz in range(1, Z)]

    gathered = []
    queries = None
    for j in range(group_heads):
        pieces = share(
            project(where, tokens, other, (w_key, w_value), HEAD_DIM, (j, group_heads))
        )
        part = jnp.stack(pieces)
        across = lax.ppermute(part, "ctx", hop(0, 1, 0))
        gathered.append(
            (
                part,
                across,
                lax.ppermute(part, "ctx", hop(0, 0, 1)),
                lax.ppermute(across, "ctx", hop(0, 0, 1)),
            )
        )
        if j == 0:
            queries = share(
                project(where, tokens, other, (w_query,), HEAD_DIM * group_heads, (0, 1))
            )
    results = [share(attend(queries, gathered[j], bias, j)) for j in range(group_heads)]
    attended = [results[j][dz] for dz in range(Z) for j in range(group_heads)]
    away = mix(where, attended, w_out, True, 512)
    arrived = lax.ppermute(away, "head", [(0, 1), (1, 0)])
    home = mix(where, attended, w_out, False, 512)
    return (home.astype(F32) + arrived.astype(F32)).astype(BF16)


def gather_all(tokens, block_order, block_mask, w_query, w_key, w_value, w_out):
    row_count = tokens.shape[0]
    local_width = w_query.shape[1]
    local_heads = local_width // HEAD_DIM
    block_count = block_order.shape[0]
    portion = lax.all_gather(tokens, "head", axis=1, tiled=True)
    query_rows, key_rows, value_rows = [
        jnp.dot(portion, weight, preferred_element_type=F32)
        .astype(BF16)
        .reshape(row_count, local_heads, HEAD_DIM)
        for weight in (w_query, w_key, w_value)
    ]
    cycle_live = block_mask[block_order][:, block_order]
    row_blocks = (
        lax.axis_index("ctx") * row_count + jnp.arange(row_count, dtype=jnp.int32)
    ) // BLOCK
    live_columns = cycle_live[row_blocks].T
    inv_root = 1.0 / HEAD_DIM**0.5

    def advance(state, inputs):
        key_tile, value_tile, offset = inputs
        keep = lax.dynamic_index_in_dim(live_columns, offset, 0, keepdims=False) > 0
        top_now, total_now, accum = state
        scores = (
            jnp.einsum("qhd,khd->hqk", query_rows, key_tile, preferred_element_type=F32)
            * inv_root
        )
        allowed = keep[None, :, None]
        top_next = jnp.maximum(top_now, jnp.max(jnp.where(allowed, scores, -1e30), axis=-1))
        factor = jnp.exp(top_now - top_next)
        weights = jnp.where(allowed, jnp.exp(scores - top_next[..., None]), 0.0)
        total_next = total_now * factor + jnp.sum(weights, axis=-1)
        accum = accum * factor[..., None] + jnp.einsum(
            "hqk,khd->hqd", weights.astype(BF16), value_tile, preferred_element_type=F32
        )
        return (top_next, total_next, accum), None

    initial = (
        jnp.full((local_heads, row_count), -1e30, F32),
        jnp.zeros((local_heads, row_count), F32),
        jnp.zeros((local_heads, row_count, HEAD_DIM), F32),
    )
    tiles = [
        lax.all_gather(part, "ctx", axis=0, tiled=True).reshape(
            block_count, BLOCK, local_heads, HEAD_DIM
        )
        for part in (key_rows, value_rows)
    ]
    (_, total, accum), _ = lax.scan(
        advance, initial, (*tiles, jnp.arange(block_count, dtype=jnp.int32))
    )
    attended = (
        (accum / total[..., None]).transpose(1, 0, 2).reshape(row_count, local_width).astype(BF16)
    )
    partial_out = jnp.dot(attended, w_out, preferred_element_type=F32)
    return lax.psum_scatter(partial_out.astype(BF16), "head", scatter_dimension=1, tiled=True)


def solution(mesh):
    in_specs = (
        P("ctx", "head"),
        P(),
        P(),
        P(None, "head"),
        P(None, "head"),
        P(None, "head"),
        P("head", None),
    )

    def per_device(tokens, block_order, block_mask, w_query, w_key, w_value, w_out):
        args = (tokens, block_order, block_mask, w_query, w_key, w_value, w_out)
        heads = w_query.shape[1] // HEAD_DIM
        fits = mesh.shape["ctx"] == Z * X * C and mesh.shape["head"] == 2 and heads % Z == 0
        return split_heads(*args) if fits else gather_all(*args)

    return jax.shard_map(
        per_device, mesh=mesh, in_specs=in_specs, out_specs=P("ctx", "head"), check_vma=False
    )
```

```python
import functools
import math

import jax
import jax.numpy as jnp
from jax import lax
from jax.experimental import pallas as pl
from jax.experimental.pallas import tpu as pltpu
from jax.sharding import PartitionSpec as P

HEAD_DIM = 128
BLOCK = 128
Z, X, C = 4, 2, 2
MIB = 1 << 20
BF16, F32 = jnp.bfloat16, jnp.float32


def place(z, x, c):
    return (z * X + x) * C + c


def hop(dz, dx, dc):
    return [
        (place(z, x, c), place(z ^ dz, x ^ dx, c ^ dc))
        for z in range(Z)
        for x in range(X)
        for c in range(C)
    ]


def params(mib):
    return pltpu.CompilerParams(vmem_limit_bytes=mib * MIB)


def project(where, own, other, weights, groups, heads, group_heads):
    rows, half = own.shape
    kinds = len(weights)
    count = len(heads)

    def body(s, own_ref, other_ref, *refs):
        mine, theirs = refs[:kinds], refs[kinds : 2 * kinds]
        outs = refs[2 * kinds :]
        w_mine = jnp.concatenate([r[...] for r in mine], axis=1)
        w_theirs = jnp.concatenate([r[...] for r in theirs], axis=1)
        total = jnp.dot(own_ref[...], w_mine, preferred_element_type=F32)
        total += jnp.dot(other_ref[...], w_theirs, preferred_element_type=F32)
        total = total.astype(BF16)
        for i in range(len(groups)):

            @pl.when(pl.program_id(0) == i)
            def _(i=i):
                for k in range(kinds):
                    outs[i][k * count + pl.program_id(1)] = total[:, k * HEAD_DIM : (k + 1) * HEAD_DIM]

    def column(i, h, s):
        flip = groups[0] if len(groups) == 1 else groups[0] ^ (i * (groups[0] ^ groups[1]))
        return (s[1] ^ flip) * group_heads + heads[0] + h

    row_spec = pl.BlockSpec((rows, half), lambda i, h, s: (0, 0))
    mine_spec = pl.BlockSpec((half, HEAD_DIM), lambda i, h, s: (s[0], column(i, h, s)))
    theirs_spec = pl.BlockSpec((half, HEAD_DIM), lambda i, h, s: (1 - s[0], column(i, h, s)))
    out = (kinds * count, rows, HEAD_DIM)
    blocks = kinds * len(groups) * count
    return pl.pallas_call(
        body,
        grid_spec=pltpu.PrefetchScalarGridSpec(
            num_scalar_prefetch=1,
            grid=(len(groups), count),
            in_specs=[row_spec, row_spec] + [mine_spec] * kinds + [theirs_spec] * kinds,
            out_specs=[pl.BlockSpec(out, lambda i, h, s: (0, 0, 0))] * len(groups),
        ),
        out_shape=[jax.ShapeDtypeStruct(out, BF16)] * len(groups),
        compiler_params=params(56),
        cost_estimate=pl.CostEstimate(
            flops=4 * rows * half * HEAD_DIM * blocks,
            bytes_accessed=4 * half * HEAD_DIM * blocks,
            transcendentals=0,
        ),
    )(where, own, other, *weights, *weights)


def attend(queries, parts, bias):
    rows = queries[0][0].shape[1]
    tile = parts[0][0].shape[2]
    where_tile = [(i, b) for i, p in enumerate(parts) for b in range(p[0].shape[0])]
    tiles = len(where_tile)
    key_count = tiles * tile
    scale = math.log2(math.e) / math.sqrt(HEAD_DIM)
    per = rows // BLOCK
    n = len(parts)

    def body(*refs):
        q_refs, k_refs, v_refs = refs[:Z], refs[Z : Z + n], refs[Z + n : Z + 2 * n]
        bias_ref = refs[Z + 2 * n]
        outs = refs[Z + 2 * n + 1 : Z + 2 * n + 1 + Z]
        s_ref, q_ref = refs[-2:]
        step = pl.program_id(0)
        for i in range(Z):

            @pl.when(step == i)
            def _(i=i):
                q_ref[...] = q_refs[i][0]

        query = q_ref[...]
        top = jnp.full((rows, 1), -jnp.inf, F32)
        for t in range(tiles):
            key = k_refs[where_tile[t][0]][where_tile[t][1], 0]
            score = lax.dot_general(
                query, key, (((1,), (1,)), ((), ())), preferred_element_type=F32
            )
            keep = [
                jnp.broadcast_to(
                    bias_ref[pl.ds(step * per + r, 1), t * tile : (t + 1) * tile], (BLOCK, tile)
                )
                for r in range(per)
            ]
            score = score + jnp.concatenate(keep, axis=0)
            s_ref[:, t * tile : (t + 1) * tile] = score
            top = jnp.maximum(top, jnp.max(score, axis=1, keepdims=True))
        shift = top * scale
        total = jnp.zeros((rows, 1), F32)
        accum = jnp.zeros((rows, HEAD_DIM), F32)
        for t in range(tiles):
            weight = jnp.exp2(s_ref[:, t * tile : (t + 1) * tile] * scale - shift)
            total += jnp.sum(weight, axis=1, keepdims=True)
            accum += jnp.dot(
                weight.astype(BF16),
                v_refs[where_tile[t][0]][where_tile[t][1], 0],
                preferred_element_type=F32,
            )
        result = (accum / total).astype(BF16)
        for i in range(Z):

            @pl.when(step == i)
            def _(i=i):
                outs[i][...] = result

    def query_spec(index):
        return pl.BlockSpec((1, rows, HEAD_DIM), lambda i: (index, 0, 0))

    def part_spec(part, index):
        return pl.BlockSpec((part.shape[0], 1, tile, HEAD_DIM), lambda i: (0, index, 0, 0))

    return pl.pallas_call(
        body,
        grid=(Z,),
        in_specs=[query_spec(at) for _, at in queries]
        + [part_spec(p, k) for p, k, _ in parts]
        + [part_spec(p, v) for p, _, v in parts]
        + [pl.BlockSpec(bias.shape, lambda i: (0, 0))],
        out_specs=[pl.BlockSpec((rows, HEAD_DIM), lambda i: (0, 0))] * Z,
        out_shape=[jax.ShapeDtypeStruct((rows, HEAD_DIM), BF16)] * Z,
        scratch_shapes=[pltpu.VMEM((rows, key_count), F32), pltpu.VMEM((rows, HEAD_DIM), BF16)],
        compiler_params=params(32),
        cost_estimate=pl.CostEstimate(
            flops=4 * Z * rows * key_count * HEAD_DIM,
            bytes_accessed=4 * key_count * HEAD_DIM,
            transcendentals=Z * rows * key_count,
        ),
    )(*[q for q, _ in queries], *[p for p, _, _ in parts], *[p for p, _, _ in parts], bias)


def mix(where, attended, w_out, flip, step_width):
    rows = attended[0].shape[0]
    depth = w_out.shape[0] // Z
    half = w_out.shape[1] // 2
    steps = half // step_width
    count = len(attended)

    def body(s, *refs):
        rows_all = jnp.concatenate([r[...] for r in refs[:count]], axis=1)
        weight = jnp.concatenate([r[...] for r in refs[count : count + Z]], axis=0)
        refs[-1][...] = jnp.dot(rows_all, weight, preferred_element_type=F32).astype(BF16)

    def weight_spec(dz):
        return pl.BlockSpec(
            (depth, step_width),
            lambda i, s: (s[1] ^ dz, (1 - s[0] if flip else s[0]) * steps + i),
        )

    return pl.pallas_call(
        body,
        grid_spec=pltpu.PrefetchScalarGridSpec(
            num_scalar_prefetch=1,
            grid=(steps,),
            in_specs=[pl.BlockSpec(a.shape, lambda i, s: (0, 0)) for a in attended]
            + [weight_spec(dz) for dz in range(Z)],
            out_specs=pl.BlockSpec((rows, step_width), lambda i, s: (0, i)),
        ),
        out_shape=jax.ShapeDtypeStruct((rows, half), BF16),
        compiler_params=params(24),
        cost_estimate=pl.CostEstimate(
            flops=2 * rows * Z * depth * half,
            bytes_accessed=2 * Z * depth * half,
            transcendentals=0,
        ),
    )(where, *attended, *([w_out] * Z))


def split_heads(tokens, block_order, block_mask, w_query, w_key, w_value, w_out):
    rows, half = tokens.shape
    group_heads = w_query.shape[1] // HEAD_DIM // Z
    block_count = block_order.shape[0]
    per = rows // BLOCK
    cut = rows // 2
    ctx = lax.axis_index("ctx")
    y = lax.axis_index("head")
    z, x, c = ctx // (X * C), (ctx // C) % X, ctx % C
    where = jnp.stack([y, z]).astype(jnp.int32)
    weights = (w_query, w_key, w_value)

    def over_y(a):
        return lax.ppermute(a, "head", [(0, 1), (1, 0)])

    def over(a, dz, dx, dc):
        return lax.ppermute(a, "ctx", hop(dz, dx, dc))

    other = over_y(tokens)
    far = [over(tokens[i * cut : (i + 1) * cut], 2, 0, 0) for i in range(2)]
    far_other = [over_y(f) for f in far]

    def blocks(pairs):
        first = jnp.stack([place(z ^ dz, x ^ dx, c ^ dc) for dz, dx, dc in pairs]) * per
        return (first[:, None] + jnp.arange(per)[None, :]).reshape(-1)

    sides = ((0, 0), (1, 0), (0, 1), (1, 1))
    query_blocks = blocks([(dz, 0, 0) for dz in range(Z)])
    key_blocks = blocks(
        [(dz + near, dx, dc) for near in (0, 2) for dx, dc in sides for dz in range(2)]
    )
    frames = jnp.arange(block_count, dtype=jnp.int32)
    order_hot = (block_order[:, None] == frames[None, :]).astype(F32)

    def pick(wanted):
        place_hot = (wanted[:, None] == frames[None, :]).astype(F32)
        return jnp.dot(place_hot, order_hot)

    live = jnp.dot(jnp.dot(pick(query_blocks), block_mask.astype(F32)), pick(key_blocks).T)
    bias = jnp.repeat(jnp.where(live > 0.5, 0.0, -1e30).astype(F32), BLOCK, axis=1)

    def spread(part):
        across = over(part, 0, 1, 0)
        return [part, across, over(part, 0, 0, 1), over(across, 0, 0, 1)]

    kept, sent = project(where, tokens, other, weights, (0, 1), range(group_heads), group_heads)
    came = over(sent, 1, 0, 0)
    near = [spread(a[None, group_heads:]) for a in (kept, came)]
    near_queries = [kept, came]

    far = jnp.concatenate(far, axis=0)
    far_other = jnp.concatenate(far_other, axis=0)
    results = []
    far_queries, far_parts = [], []
    for j in range(group_heads):
        kept, sent = project(where, far, far_other, weights, (0, 1), (j,), group_heads)
        came = over(sent, 1, 0, 0)
        far_queries.append((kept, came))
        far_parts.append(spread(jnp.stack([kept[1:], came[1:]])))
    for j in range(group_heads):
        queries = [(a, j) for a in near_queries] + [(a, 0) for a in far_queries[j]]
        parts = [(near[i][side], j, group_heads + j) for side in range(4) for i in range(2)]
        parts += [(a, 0, 1) for a in far_parts[j]]
        results.append(attend(queries, parts, bias))
    results = [
        [r[0]] + [over(r[dz], dz, 0, 0) for dz in range(1, Z)] for r in results
    ]
    attended = [results[j][dz] for dz in range(Z) for j in range(group_heads)]
    arrived = over_y(mix(where, attended, w_out, True, 512))
    home = mix(where, attended, w_out, False, 512)
    return (home.astype(F32) + arrived.astype(F32)).astype(BF16)


def gather_all(tokens, block_order, block_mask, w_query, w_key, w_value, w_out):
    row_count = tokens.shape[0]
    local_width = w_query.shape[1]
    local_heads = local_width // HEAD_DIM
    block_count = block_order.shape[0]
    portion = lax.all_gather(tokens, "head", axis=1, tiled=True)
    query_rows, key_rows, value_rows = [
        jnp.dot(portion, weight, preferred_element_type=F32)
        .astype(BF16)
        .reshape(row_count, local_heads, HEAD_DIM)
        for weight in (w_query, w_key, w_value)
    ]
    cycle_live = block_mask[block_order][:, block_order]
    row_blocks = (
        lax.axis_index("ctx") * row_count + jnp.arange(row_count, dtype=jnp.int32)
    ) // BLOCK
    live_columns = cycle_live[row_blocks].T
    inv_root = 1.0 / HEAD_DIM**0.5

    def advance(state, inputs):
        key_tile, value_tile, offset = inputs
        keep = lax.dynamic_index_in_dim(live_columns, offset, 0, keepdims=False) > 0
        top_now, total_now, accum = state
        scores = (
            jnp.einsum("qhd,khd->hqk", query_rows, key_tile, preferred_element_type=F32)
            * inv_root
        )
        allowed = keep[None, :, None]
        top_next = jnp.maximum(top_now, jnp.max(jnp.where(allowed, scores, -1e30), axis=-1))
        factor = jnp.exp(top_now - top_next)
        weights = jnp.where(allowed, jnp.exp(scores - top_next[..., None]), 0.0)
        total_next = total_now * factor + jnp.sum(weights, axis=-1)
        accum = accum * factor[..., None] + jnp.einsum(
            "hqk,khd->hqd", weights.astype(BF16), value_tile, preferred_element_type=F32
        )
        return (top_next, total_next, accum), None

    initial = (
        jnp.full((local_heads, row_count), -1e30, F32),
        jnp.zeros((local_heads, row_count), F32),
        jnp.zeros((local_heads, row_count, HEAD_DIM), F32),
    )
    tiles = [
        lax.all_gather(part, "ctx", axis=0, tiled=True).reshape(
            block_count, BLOCK, local_heads, HEAD_DIM
        )
        for part in (key_rows, value_rows)
    ]
    (_, total, accum), _ = lax.scan(
        advance, initial, (*tiles, jnp.arange(block_count, dtype=jnp.int32))
    )
    attended = (
        (accum / total[..., None]).transpose(1, 0, 2).reshape(row_count, local_width).astype(BF16)
    )
    partial_out = jnp.dot(attended, w_out, preferred_element_type=F32)
    return lax.psum_scatter(partial_out.astype(BF16), "head", scatter_dimension=1, tiled=True)


def solution(mesh):
    in_specs = (
        P("ctx", "head"),
        P(),
        P(),
        P(None, "head"),
        P(None, "head"),
        P(None, "head"),
        P("head", None),
    )

    def per_device(tokens, block_order, block_mask, w_query, w_key, w_value, w_out):
        args = (tokens, block_order, block_mask, w_query, w_key, w_value, w_out)
        heads = w_query.shape[1] // HEAD_DIM
        fits = mesh.shape["ctx"] == Z * X * C and mesh.shape["head"] == 2 and heads % Z == 0
        return split_heads(*args) if fits else gather_all(*args)

    return jax.shard_map(
        per_device, mesh=mesh, in_specs=in_specs, out_specs=P("ctx", "head"), check_vma=False
    )
```

```python
import functools
import math

import jax
import jax.numpy as jnp
from jax import lax
from jax.experimental import pallas as pl
from jax.experimental.pallas import tpu as pltpu
from jax.sharding import PartitionSpec as P

HEAD_DIM = 128
BLOCK = 128
Z, X, C = 4, 2, 2
MIB = 1 << 20
BF16, F32 = jnp.bfloat16, jnp.float32
LIGHT = pl.CostEstimate(flops=1024, bytes_accessed=1024, transcendentals=0)


def place(z, x, c):
    return (z * X + x) * C + c


def hop(dz, dx, dc):
    return [
        (place(z, x, c), place(z ^ dz, x ^ dx, c ^ dc))
        for z in range(Z)
        for x in range(X)
        for c in range(C)
    ]


def params(mib):
    return pltpu.CompilerParams(vmem_limit_bytes=mib * MIB)


def after(value, *others):
    return lax.optimization_barrier((value, *others))[0]


def whole(count):
    return [pl.BlockSpec(memory_space=pltpu.VMEM)] * count


def fetch(where, weights, width):
    depth = weights[0].shape[0]
    half = depth // 2
    kinds = len(weights)

    def body(s, *refs):
        out, sems = refs[kinds], refs[kinds + 1]
        copies = []
        for g in range(2):
            columns = pl.ds(pl.multiple_of((s[1] ^ g) * width, width), width)
            for k in range(kinds):
                for part in range(2):
                    rows = pl.ds(pl.multiple_of((s[0] ^ part) * half, half), half)
                    copies.append(
                        pltpu.make_async_copy(
                            refs[k].at[rows, columns],
                            out.at[g * kinds + k, pl.ds(part * half, half)],
                            sems.at[len(copies)],
                        )
                    )
        for copy in copies:
            copy.start()
        for copy in copies:
            copy.wait()

    return pl.pallas_call(
        body,
        grid_spec=pltpu.PrefetchScalarGridSpec(
            num_scalar_prefetch=1,
            grid=(),
            in_specs=[pl.BlockSpec(memory_space=pl.ANY)] * kinds,
            out_specs=pl.BlockSpec(memory_space=pltpu.VMEM),
            scratch_shapes=[pltpu.SemaphoreType.DMA((4 * kinds,))],
        ),
        out_shape=pltpu.VMEM((2 * kinds, depth, width), BF16),
        compiler_params=params(4),
        cost_estimate=LIGHT,
    )(where, *weights)


def project(own, other, held, outputs):
    rows = own.shape[0]
    kinds = held.shape[0] // 2
    flat = [block for blocks in outputs for block in blocks]

    def body(own_ref, other_ref, held_ref, *outs):
        tokens = jnp.concatenate([own_ref[...], other_ref[...]], axis=1)
        at = [(o, i) for o, blocks in enumerate(outputs) for i in range(len(blocks))]
        for start in range(0, len(flat), 2):
            pair = flat[start : start + 2]
            weight = [
                held_ref[g * kinds + k, :, h * HEAD_DIM : (h + 1) * HEAD_DIM] for g, k, h in pair
            ]
            total = jnp.dot(
                tokens, jnp.concatenate(weight, axis=1), preferred_element_type=F32
            ).astype(BF16)
            for i in range(len(pair)):
                o, place_in = at[start + i]
                outs[o][place_in] = total[:, i * HEAD_DIM : (i + 1) * HEAD_DIM]

    return pl.pallas_call(
        body,
        in_specs=whole(3),
        out_specs=whole(len(outputs)),
        out_shape=[jax.ShapeDtypeStruct((len(b), rows, HEAD_DIM), BF16) for b in outputs],
        compiler_params=params(16),
        cost_estimate=LIGHT,
    )(own, other, held)


def attend(queries, parts, bias, fence):
    rows = queries[0][0].shape[1]
    tile = parts[0][0].shape[1]
    n = len(parts)
    group = 4
    scale = math.log2(math.e) / math.sqrt(HEAD_DIM)
    per = rows // BLOCK
    both = 2 * rows

    def body(*refs):
        q_refs, k_refs, v_refs = refs[:Z], refs[Z : Z + n], refs[Z + n : Z + 2 * n]
        bias_ref = refs[Z + 2 * n]
        outs = refs[Z + 2 * n + 2 : Z + 2 * n + 2 + Z]
        q_ref = refs[-1]
        step = pl.program_id(0)
        for i in range(Z // 2):

            @pl.when(step == i)
            def _(i=i):
                q_ref[:rows] = q_refs[2 * i][0]
                q_ref[rows:] = q_refs[2 * i + 1][0]

        query = q_ref[...]
        top = jnp.full((both, 1), -1e30, F32)
        total = jnp.zeros((both, HEAD_DIM), F32)
        accum = jnp.zeros((both, HEAD_DIM), F32)
        for t in range(0, n, group):
            key = jnp.concatenate([k_refs[u][0] for u in range(t, t + group)], axis=0)
            value = jnp.concatenate([v_refs[u][0] for u in range(t, t + group)], axis=0)
            width = group * tile
            score = lax.dot_general(
                query, key, (((1,), (1,)), ((), ())), preferred_element_type=F32
            )
            keep = [
                jnp.broadcast_to(
                    bias_ref[pl.ds(step * 2 * per + r, 1), t * tile : t * tile + width],
                    (BLOCK, width),
                )
                for r in range(2 * per)
            ]
            score = score + jnp.concatenate(keep, axis=0)
            best = score[:, :HEAD_DIM]
            for u in range(HEAD_DIM, width, HEAD_DIM):
                best = jnp.maximum(best, score[:, u : u + HEAD_DIM])
            top_next = jnp.maximum(top, jnp.max(best, axis=1, keepdims=True))
            factor = jnp.exp2((top - top_next) * scale)
            top = top_next
            weight = jnp.exp2(score * scale - top * scale)
            add = weight[:, :HEAD_DIM]
            for u in range(HEAD_DIM, width, HEAD_DIM):
                add = add + weight[:, u : u + HEAD_DIM]
            total = total * factor + add
            accum = accum * factor + jnp.dot(
                weight.astype(BF16), value, preferred_element_type=F32
            )
        result = (accum / jnp.sum(total, axis=1, keepdims=True)).astype(BF16)
        for i in range(Z // 2):

            @pl.when(step == i)
            def _(i=i):
                outs[2 * i][...] = result[:rows]
                outs[2 * i + 1][...] = result[rows:]

    def block_spec(index):
        return pl.BlockSpec((1, rows, HEAD_DIM), lambda i: (index, 0, 0))

    return pl.pallas_call(
        body,
        grid=(Z // 2,),
        in_specs=[block_spec(at) for _, at in queries]
        + [block_spec(k) for _, k, _ in parts]
        + [block_spec(v) for _, _, v in parts]
        + [pl.BlockSpec(bias.shape, lambda i: (0, 0)), pl.BlockSpec(memory_space=pl.ANY)],
        out_specs=[pl.BlockSpec((rows, HEAD_DIM), lambda i: (0, 0))] * Z,
        out_shape=[jax.ShapeDtypeStruct((rows, HEAD_DIM), BF16)] * Z,
        scratch_shapes=[pltpu.VMEM((both, HEAD_DIM), BF16)],
        compiler_params=params(24),
        cost_estimate=LIGHT,
    )(*[q for q, _ in queries], *[p for p, _, _ in parts], *[p for p, _, _ in parts], bias, fence)


def mix(where, attended, w_out, flip, step_width):
    rows = attended[0].shape[0]
    depth = w_out.shape[0] // Z
    half = w_out.shape[1] // 2
    steps = half // step_width
    count = len(attended)

    def body(s, *refs):
        rows_all = jnp.concatenate([r[...] for r in refs[:count]], axis=1)
        weight = jnp.concatenate([r[...] for r in refs[count : count + Z]], axis=0)
        refs[-1][...] = jnp.dot(rows_all, weight, preferred_element_type=F32).astype(BF16)

    def weight_spec(dz):
        return pl.BlockSpec(
            (depth, step_width),
            lambda i, s: (s[1] ^ dz, (1 - s[0] if flip else s[0]) * steps + i),
        )

    return pl.pallas_call(
        body,
        grid_spec=pltpu.PrefetchScalarGridSpec(
            num_scalar_prefetch=1,
            grid=(steps,),
            in_specs=[pl.BlockSpec(a.shape, lambda i, s: (0, 0)) for a in attended]
            + [weight_spec(dz) for dz in range(Z)],
            out_specs=pl.BlockSpec((rows, step_width), lambda i, s: (0, i)),
        ),
        out_shape=jax.ShapeDtypeStruct((rows, half), BF16),
        compiler_params=params(24),
        cost_estimate=LIGHT,
    )(where, *attended, *([w_out] * Z))


def split_heads(tokens, block_order, block_mask, w_query, w_key, w_value, w_out):
    rows, half = tokens.shape
    group_heads = w_query.shape[1] // HEAD_DIM // Z
    block_count = block_order.shape[0]
    per = rows // BLOCK
    cut = rows // 2
    ctx = lax.axis_index("ctx")
    y = lax.axis_index("head")
    z, x, c = ctx // (X * C), (ctx // C) % X, ctx % C
    where = jnp.stack([y, z]).astype(jnp.int32)
    weights = (w_query, w_key, w_value)

    def over_y(a):
        return lax.ppermute(a, "head", [(0, 1), (1, 0)])

    def over(a, dz, dx, dc):
        return lax.ppermute(a, "ctx", hop(dz, dx, dc))

    held = [pltpu.with_memory_space_constraint(w, pltpu.HBM) for w in weights]
    other = over_y(tokens)
    far = [over(tokens[i * cut : (i + 1) * cut], 2, 0, 0) for i in range(2)]

    def blocks(pairs):
        first = jnp.stack([place(z ^ dz, x ^ dx, c ^ dc) for dz, dx, dc in pairs]) * per
        return (first[:, None] + jnp.arange(per)[None, :]).reshape(-1)

    sides = ((0, 0), (1, 0), (0, 1), (1, 1))
    query_blocks = blocks([(dz, 0, 0) for dz in range(Z)])
    key_blocks = blocks([(dz, dx, dc) for dz in range(Z) for dx, dc in sides])
    frames = jnp.arange(block_count, dtype=jnp.int32)
    order_hot = (block_order[:, None] == frames[None, :]).astype(F32)

    def pick(wanted):
        place_hot = (wanted[:, None] == frames[None, :]).astype(F32)
        return jnp.dot(place_hot, order_hot)

    live = jnp.dot(jnp.dot(pick(query_blocks), block_mask.astype(F32)), pick(key_blocks).T)
    bias = jnp.repeat(jnp.where(live > 0.5, 0.0, -1e30).astype(F32), BLOCK, axis=1)

    heads = range(group_heads)
    span = group_heads * HEAD_DIM

    def pairs(group, wanted):
        return [(group, kind, h) for kind in (1, 2) for h in wanted]

    def singles(group):
        return [(group, 0, h) for h in heads]

    held = fetch(where, held, span)

    far_other = [over_y(far[0])]
    own_q, own_kv, sent_q, sent_kv = project(
        after(tokens, far[0]),
        other,
        held,
        [singles(0), pairs(0, heads), singles(1), pairs(1, heads)],
    )
    came_kv = over(sent_kv, 1, 0, 0)
    came_q = over(sent_q, 1, 0, 0)
    own_across = over(own_kv, 0, 1, 0)
    own_core = over(own_kv, 0, 0, 1)
    far_other.append(over_y(after(far[1], own_kv)))
    came_kv = after(came_kv, far[1])
    came_across = over(came_kv, 0, 1, 0)
    came_core = over(came_kv, 0, 0, 1)
    own_across_core = over(after(own_across, came_kv), 0, 0, 1)

    far = after(jnp.concatenate(far, axis=0), came_kv, own_across)
    far_other = jnp.concatenate(far_other, axis=0)
    first, rest = (0,), tuple(heads)[1:]
    far_sent_kv, far_sent_q = project(far, far_other, held, [pairs(1, first), singles(1)])
    far_came_kv = over(far_sent_kv, 1, 0, 0)
    far_came_q = over(far_sent_q, 1, 0, 0)
    (far_sent_kv2,) = project(after(far, far_sent_kv), far_other, held, [pairs(1, rest)])
    far_came_kv2 = over(far_sent_kv2, 1, 0, 0)
    far_q, far_kv = project(
        after(far, far_sent_kv2), far_other, held, [singles(0), pairs(0, heads)]
    )

    def spread(part):
        across = over(part, 0, 1, 0)
        return [part, across, over(part, 0, 0, 1), over(across, 0, 0, 1)]

    far_kept = spread(far_kv)
    came_across_core = over(came_across, 0, 0, 1)
    far_first = spread(after(far_came_kv, far_kv))
    far_rest = spread(after(far_came_kv2, far_first[0]))
    near = [[own_kv, own_across, own_core, own_across_core]]
    near.append([came_kv, came_across, came_core, came_across_core])

    results = []
    for j in heads:
        queries = [(own_q, j), (came_q, j), (far_q, j), (far_came_q, j)]
        parts = [(a, j, group_heads + j) for a in near[0] + near[1] + far_kept]
        if j == 0:
            parts += [(a, 0, 1) for a in far_first]
        else:
            parts += [(a, j - 1, group_heads - 1 + j - 1) for a in far_rest]
        results.append(attend(queries, parts, bias, results[-1][0] if j else far_rest[1]))
    results = [[r[0]] + [over(r[dz], dz, 0, 0) for dz in range(1, Z)] for r in results]
    attended = [results[j][dz] for dz in range(Z) for j in range(group_heads)]
    arrived = over_y(mix(where, attended, w_out, True, 512))
    home = mix(where, attended, w_out, False, 512)
    return (home.astype(F32) + arrived.astype(F32)).astype(BF16)


def gather_all(tokens, block_order, block_mask, w_query, w_key, w_value, w_out):
    row_count = tokens.shape[0]
    local_width = w_query.shape[1]
    local_heads = local_width // HEAD_DIM
    block_count = block_order.shape[0]
    portion = lax.all_gather(tokens, "head", axis=1, tiled=True)
    query_rows, key_rows, value_rows = [
        jnp.dot(portion, weight, preferred_element_type=F32)
        .astype(BF16)
        .reshape(row_count, local_heads, HEAD_DIM)
        for weight in (w_query, w_key, w_value)
    ]
    cycle_live = block_mask[block_order][:, block_order]
    row_blocks = (
        lax.axis_index("ctx") * row_count + jnp.arange(row_count, dtype=jnp.int32)
    ) // BLOCK
    live_columns = cycle_live[row_blocks].T
    inv_root = 1.0 / HEAD_DIM**0.5

    def advance(state, inputs):
        key_tile, value_tile, offset = inputs
        keep = lax.dynamic_index_in_dim(live_columns, offset, 0, keepdims=False) > 0
        top_now, total_now, accum = state
        scores = (
            jnp.einsum("qhd,khd->hqk", query_rows, key_tile, preferred_element_type=F32)
            * inv_root
        )
        allowed = keep[None, :, None]
        top_next = jnp.maximum(top_now, jnp.max(jnp.where(allowed, scores, -1e30), axis=-1))
        factor = jnp.exp(top_now - top_next)
        weights = jnp.where(allowed, jnp.exp(scores - top_next[..., None]), 0.0)
        total_next = total_now * factor + jnp.sum(weights, axis=-1)
        accum = accum * factor[..., None] + jnp.einsum(
            "hqk,khd->hqd", weights.astype(BF16), value_tile, preferred_element_type=F32
        )
        return (top_next, total_next, accum), None

    initial = (
        jnp.full((local_heads, row_count), -1e30, F32),
        jnp.zeros((local_heads, row_count), F32),
        jnp.zeros((local_heads, row_count, HEAD_DIM), F32),
    )
    tiles = [
        lax.all_gather(part, "ctx", axis=0, tiled=True).reshape(
            block_count, BLOCK, local_heads, HEAD_DIM
        )
        for part in (key_rows, value_rows)
    ]
    (_, total, accum), _ = lax.scan(
        advance, initial, (*tiles, jnp.arange(block_count, dtype=jnp.int32))
    )
    attended = (
        (accum / total[..., None]).transpose(1, 0, 2).reshape(row_count, local_width).astype(BF16)
    )
    partial_out = jnp.dot(attended, w_out, preferred_element_type=F32)
    return lax.psum_scatter(partial_out.astype(BF16), "head", scatter_dimension=1, tiled=True)


def solution(mesh):
    in_specs = (
        P("ctx", "head"),
        P(),
        P(),
        P(None, "head"),
        P(None, "head"),
        P(None, "head"),
        P("head", None),
    )

    def per_device(tokens, block_order, block_mask, w_query, w_key, w_value, w_out):
        args = (tokens, block_order, block_mask, w_query, w_key, w_value, w_out)
        heads = w_query.shape[1] // HEAD_DIM
        fits = mesh.shape["ctx"] == Z * X * C and mesh.shape["head"] == 2 and heads % Z == 0
        return split_heads(*args) if fits else gather_all(*args)

    return jax.shard_map(
        per_device, mesh=mesh, in_specs=in_specs, out_specs=P("ctx", "head"), check_vma=False
    )
```

```python
import functools
import math

import jax
import jax.numpy as jnp
from jax import lax
from jax.experimental import pallas as pl
from jax.experimental.pallas import tpu as pltpu
from jax.sharding import PartitionSpec as P

HEAD_DIM = 128
BLOCK = 128
Z, X, C = 4, 2, 2
MIB = 1 << 20
BF16, F32 = jnp.bfloat16, jnp.float32
LIGHT = pl.CostEstimate(flops=1024, bytes_accessed=1024, transcendentals=0)


def place(z, x, c):
    return (z * X + x) * C + c


def hop(dz, dx, dc):
    return [
        (place(z, x, c), place(z ^ dz, x ^ dx, c ^ dc))
        for z in range(Z)
        for x in range(X)
        for c in range(C)
    ]


def params(mib):
    return pltpu.CompilerParams(vmem_limit_bytes=mib * MIB)


def after(value, *others):
    return lax.optimization_barrier((value, *others))[0]


def whole(count):
    return [pl.BlockSpec(memory_space=pltpu.VMEM)] * count


def fetch(where, weights, width, fence):
    depth = weights[0].shape[0]
    half = depth // 2
    kinds = len(weights)

    def body(s, *refs):
        out, sems = refs[kinds + 1], refs[kinds + 2]
        copies = []
        for g in range(2):
            columns = pl.ds(pl.multiple_of((s[1] ^ g) * width, width), width)
            for k in range(kinds):
                for part in range(2):
                    rows = pl.ds(pl.multiple_of((s[0] ^ part) * half, half), half)
                    copies.append(
                        pltpu.make_async_copy(
                            refs[k].at[rows, columns],
                            out.at[g * kinds + k, pl.ds(part * half, half)],
                            sems.at[len(copies)],
                        )
                    )
        for copy in copies:
            copy.start()
        for copy in copies:
            copy.wait()

    return pl.pallas_call(
        body,
        grid_spec=pltpu.PrefetchScalarGridSpec(
            num_scalar_prefetch=1,
            grid=(),
            in_specs=[pl.BlockSpec(memory_space=pl.ANY)] * (kinds + 1),
            out_specs=pl.BlockSpec(memory_space=pltpu.VMEM),
            scratch_shapes=[pltpu.SemaphoreType.DMA((4 * kinds,))],
        ),
        out_shape=pltpu.VMEM((2 * kinds, depth, width), BF16),
        compiler_params=params(4),
        cost_estimate=LIGHT,
    )(where, *weights, fence)


def project(own, other, held, outputs):
    pieces = len(own)
    rows = sum(a.shape[0] for a in own)
    kinds = held.shape[0] // 2
    flat = [block for blocks in outputs for block in blocks]

    def body(*refs):
        held_ref, outs = refs[2 * pieces], refs[2 * pieces + 1 :]
        tokens = jnp.concatenate(
            [
                jnp.concatenate([r[...] for r in refs[:pieces]], axis=0),
                jnp.concatenate([r[...] for r in refs[pieces : 2 * pieces]], axis=0),
            ],
            axis=1,
        )
        at = [(o, i) for o, blocks in enumerate(outputs) for i in range(len(blocks))]
        for start in range(0, len(flat), 2):
            pair = flat[start : start + 2]
            weight = [
                held_ref[g * kinds + k, :, h * HEAD_DIM : (h + 1) * HEAD_DIM] for g, k, h in pair
            ]
            total = jnp.dot(
                tokens, jnp.concatenate(weight, axis=1), preferred_element_type=F32
            ).astype(BF16)
            for i in range(len(pair)):
                o, place_in = at[start + i]
                outs[o][place_in] = total[:, i * HEAD_DIM : (i + 1) * HEAD_DIM]

    return pl.pallas_call(
        body,
        in_specs=whole(2 * pieces + 1),
        out_specs=whole(len(outputs)),
        out_shape=[jax.ShapeDtypeStruct((len(b), rows, HEAD_DIM), BF16) for b in outputs],
        compiler_params=params(16),
        cost_estimate=LIGHT,
    )(*own, *other, held)


def mask_rows(where, block_order, block_mask, rows):
    blocks = block_order.shape[0]
    per = rows // BLOCK
    keys = blocks * BLOCK

    def body(s, order_ref, mask_ref, out_ref):
        def ids(shape, axis, shift):
            at = lax.broadcasted_iota(jnp.int32, shape, axis) >> shift
            piece = at >> (per.bit_length() - 1)
            return at & (per - 1), piece

        hot = (order_ref[...] == lax.broadcasted_iota(jnp.int32, (blocks, blocks), 0)).astype(F32)
        low, piece = ids((Z * per, blocks), 0, 0)
        want = (place(s[1] ^ piece, s[2], s[3])) * per + low
        query = (want == lax.broadcasted_iota(jnp.int32, (Z * per, blocks), 1)).astype(F32)
        low, piece = ids((blocks, keys), 1, BLOCK.bit_length() - 1)
        want = place(s[1] ^ (piece >> 2), s[2] ^ (piece & 1), s[3] ^ ((piece >> 1) & 1)) * per + low
        key = (want == lax.broadcasted_iota(jnp.int32, (blocks, keys), 0)).astype(F32)
        frames = lax.dot_general(query, hot, (((1,), (1,)), ((), ())), preferred_element_type=F32)
        live = jnp.dot(frames, mask_ref[...].astype(F32), preferred_element_type=F32)
        live = jnp.dot(live, hot, preferred_element_type=F32)
        live = jnp.dot(live, key, preferred_element_type=F32)
        out_ref[...] = jnp.where(live > 0.5, 0.0, -1e30)

    return pl.pallas_call(
        body,
        grid_spec=pltpu.PrefetchScalarGridSpec(
            num_scalar_prefetch=1, grid=(), in_specs=whole(2), out_specs=whole(1)[0]
        ),
        out_shape=jax.ShapeDtypeStruct((Z * per, keys), F32),
        compiler_params=params(8),
        cost_estimate=LIGHT,
    )(where, block_order[None, :], block_mask)


def attend(queries, parts, states, bias, query_at, key_at, last, fences):
    rows = queries[0][0][0].shape[1]
    tile = parts[0][0][0].shape[1]
    n = len(parts[0])
    group = 4
    scale = math.log2(math.e) / math.sqrt(HEAD_DIM)
    per = rows // BLOCK
    both = 2 * rows
    steps = len(queries)
    same_parts = len(parts) == 1

    def body(*refs):
        refs = list(refs)

        def take(count):
            got = refs[:count]
            del refs[:count]
            return got

        q_refs = take(2 * steps)
        k_refs, v_refs = take(n), take(n)
        state_refs = [take(3) for _ in states]
        (bias_ref,) = take(1)
        take(len(fences))
        outs = take(2 * steps if last else 3)
        q_ref = refs[0]
        step = pl.program_id(0)
        for i in range(steps):

            @pl.when(step == i)
            def _(i=i):
                q_ref[:rows] = q_refs[2 * i][0]
                q_ref[rows:] = q_refs[2 * i + 1][0]
                if states:
                    for held, ref in zip(refs[1:], state_refs[i]):
                        held[...] = ref[0]

        query = q_ref[...]
        if states:
            top, total, accum = refs[1][:, :1], refs[2][...], refs[3][...]
        else:
            top = jnp.full((both, 1), -1e30, F32)
            total = jnp.zeros((both, HEAD_DIM), F32)
            accum = jnp.zeros((both, HEAD_DIM), F32)
        first_row = (query_at[0] + step * query_at[1]) * per
        for t in range(0, n, group):
            key = jnp.concatenate([k_refs[u][0] for u in range(t, t + group)], axis=0)
            value = jnp.concatenate([v_refs[u][0] for u in range(t, t + group)], axis=0)
            width = group * tile
            at = (key_at + t) * tile
            score = lax.dot_general(
                query, key, (((1,), (1,)), ((), ())), preferred_element_type=F32
            )
            keep = [
                jnp.broadcast_to(bias_ref[pl.ds(first_row + r, 1), at : at + width], (BLOCK, width))
                for r in range(2 * per)
            ]
            score = score + jnp.concatenate(keep, axis=0)
            best = score[:, :HEAD_DIM]
            for u in range(HEAD_DIM, width, HEAD_DIM):
                best = jnp.maximum(best, score[:, u : u + HEAD_DIM])
            top_next = jnp.maximum(top, jnp.max(best, axis=1, keepdims=True))
            factor = jnp.exp2((top - top_next) * scale)
            top = top_next
            weight = jnp.exp2(score * scale - top * scale)
            add = weight[:, :HEAD_DIM]
            for u in range(HEAD_DIM, width, HEAD_DIM):
                add = add + weight[:, u : u + HEAD_DIM]
            total = total * factor + add
            accum = accum * factor + jnp.dot(
                weight.astype(BF16), value, preferred_element_type=F32
            )
        if last:
            result = (accum / jnp.sum(total, axis=1, keepdims=True)).astype(BF16)
            for i in range(steps):

                @pl.when(step == i)
                def _(i=i):
                    outs[2 * i][...] = result[:rows]
                    outs[2 * i + 1][...] = result[rows:]

        else:
            outs[0][0] = jnp.broadcast_to(top, (both, HEAD_DIM))
            outs[1][0] = total
            outs[2][0] = accum

    def fixed(block, index):
        return pl.BlockSpec(block, lambda i: (index,) + (0,) * (len(block) - 1))

    def part_spec(kind):
        def one(u):
            base = parts[0][u][kind]
            stride = 0 if same_parts else 1
            return pl.BlockSpec((1, tile, HEAD_DIM), lambda i: (base + i * stride, 0, 0))

        return [one(u) for u in range(n)]

    arrays = [p[0] for p in parts[0]]
    state_block = (1, both, HEAD_DIM)
    if last:
        out_specs = [pl.BlockSpec((rows, HEAD_DIM), lambda i: (0, 0))] * (2 * steps)
        out_shape = [jax.ShapeDtypeStruct((rows, HEAD_DIM), BF16)] * (2 * steps)
    else:
        out_specs = [pl.BlockSpec(state_block, lambda i: (i, 0, 0))] * 3
        out_shape = [jax.ShapeDtypeStruct((steps, both, HEAD_DIM), F32)] * 3
    return pl.pallas_call(
        body,
        grid=(steps,),
        in_specs=[fixed((1, rows, HEAD_DIM), at) for row in queries for _, at in row]
        + part_spec(1)
        + part_spec(2)
        + [fixed(state_block, at) for _, at in states for _ in range(3)]
        + [pl.BlockSpec(bias.shape, lambda i: (0, 0))]
        + [pl.BlockSpec(memory_space=pl.ANY)] * len(fences),
        out_specs=out_specs,
        out_shape=out_shape,
        scratch_shapes=[pltpu.VMEM((both, HEAD_DIM), BF16)]
        + [pltpu.VMEM((both, HEAD_DIM), F32)] * (3 if states else 0),
        compiler_params=params(24),
        cost_estimate=LIGHT,
    )(
        *[a for row in queries for a, _ in row],
        *arrays,
        *arrays,
        *[a for held, _ in states for a in held],
        bias,
        *fences,
    )


def mix(where, attended, w_out, flip, step_width):
    rows = attended[0].shape[0]
    depth = w_out.shape[0] // Z
    half = w_out.shape[1] // 2
    steps = half // step_width
    count = len(attended)

    def body(s, *refs):
        rows_all = jnp.concatenate([r[...] for r in refs[:count]], axis=1)
        weight = jnp.concatenate([r[...] for r in refs[count : count + Z]], axis=0)
        refs[-1][...] = jnp.dot(rows_all, weight, preferred_element_type=F32).astype(BF16)

    def weight_spec(dz):
        return pl.BlockSpec(
            (depth, step_width),
            lambda i, s: (s[1] ^ dz, (1 - s[0] if flip else s[0]) * steps + i),
        )

    return pl.pallas_call(
        body,
        grid_spec=pltpu.PrefetchScalarGridSpec(
            num_scalar_prefetch=1,
            grid=(steps,),
            in_specs=[pl.BlockSpec(a.shape, lambda i, s: (0, 0)) for a in attended]
            + [weight_spec(dz) for dz in range(Z)],
            out_specs=pl.BlockSpec((rows, step_width), lambda i, s: (0, i)),
        ),
        out_shape=jax.ShapeDtypeStruct((rows, half), BF16),
        compiler_params=params(24),
        cost_estimate=LIGHT,
    )(where, *attended, *([w_out] * Z))


def split_heads(tokens, block_order, block_mask, w_query, w_key, w_value, w_out):
    rows, half = tokens.shape
    group_heads = w_query.shape[1] // HEAD_DIM // Z
    cut = rows // 2
    ctx = lax.axis_index("ctx")
    y = lax.axis_index("head")
    where = jnp.stack([y, ctx // (X * C), (ctx // C) % X, ctx % C]).astype(jnp.int32)
    weights = [pltpu.with_memory_space_constraint(w, pltpu.HBM) for w in (w_query, w_key, w_value)]
    w_out = pltpu.with_memory_space_constraint(w_out, pltpu.HBM)
    heads = range(group_heads)
    span = group_heads * HEAD_DIM

    def over_y(a):
        return lax.ppermute(a, "head", [(0, 1), (1, 0)])

    def over(a, dz, dx, dc):
        return lax.ppermute(a, "ctx", hop(dz, dx, dc))

    def pairs(group, wanted):
        return [(group, kind, h) for kind in (1, 2) for h in wanted]

    def singles(group):
        return [(group, 0, h) for h in heads]

    other = over_y(tokens)
    far = [over(tokens[:cut], 2, 0, 0)]
    bias = mask_rows(where, block_order, block_mask, rows)
    held = fetch(where, weights, span, bias)

    other = after(other, held)
    far[0] = after(far[0], held)
    far.append(over(after(tokens[cut:], far[0]), 2, 0, 0))
    far_other = [over_y(far[0])]
    own_kv, sent_kv = project(
        [after(tokens, far[0])], [other], held, [pairs(0, heads), pairs(1, heads)]
    )
    came_kv = over(sent_kv, 1, 0, 0)
    own_across = over(own_kv, 0, 1, 0)
    own_core = over(own_kv, 0, 0, 1)
    own_q, sent_q = project(
        [after(tokens, sent_kv)], [other], held, [singles(0), singles(1)]
    )
    came_q = over(sent_q, 1, 0, 0)
    far[1] = after(far[1], sent_q)
    far_other.append(over_y(after(far[1], far_other[0])))
    own_across_core = over(own_across, 0, 0, 1)
    came_kv = after(came_kv, own_across)
    came_across = over(came_kv, 0, 1, 0)
    came_core = over(came_kv, 0, 0, 1)

    far[1] = after(far[1], came_kv)
    far_other[1] = after(far_other[1], came_kv)
    first, rest = (0,), tuple(heads)[1:]
    far_sent_kv, far_sent_q = project(far, far_other, held, [pairs(1, first), singles(1)])
    far_came_kv = over(far_sent_kv, 1, 0, 0)
    far_came_q = over(far_sent_q, 1, 0, 0)
    (far_kv,) = project(
        [far[0], after(far[1], far_sent_kv)], far_other, held, [pairs(0, heads)]
    )
    far_across = over(far_kv, 0, 1, 0)
    far_core = over(far_kv, 0, 0, 1)
    far_sent_kv2, far_q = project(
        [far[0], after(far[1], far_kv)], far_other, held, [pairs(1, rest), singles(0)]
    )
    far_came_kv2 = over(far_sent_kv2, 1, 0, 0)
    came_across = after(came_across, far_q)
    came_across_core = over(came_across, 0, 0, 1)

    near = [own_kv, own_across, own_core, own_across_core]
    near += [came_kv, came_across, came_core, came_across_core]
    near_parts = [[(a, 0, group_heads) for a in near], None]
    state_near = attend(
        [[(own_q, j), (came_q, j)] for j in heads], near_parts, [], bias, (0, 0), 0, False, []
    )
    far_came_kv = after(far_came_kv, state_near[0])
    first_across = over(far_came_kv, 0, 1, 0)
    first_core = over(far_came_kv, 0, 0, 1)
    far_came_kv2 = after(far_came_kv2, far_came_kv)
    rest_across = over(far_came_kv2, 0, 1, 0)
    rest_core = over(far_came_kv2, 0, 0, 1)
    far_across = after(far_across, far_came_kv2)
    far_across_core = over(far_across, 0, 0, 1)
    state_far = attend(
        [[(far_q, j), (far_came_q, j)] for j in heads],
        near_parts,
        [],
        bias,
        (2, 0),
        0,
        False,
        [far_across, far_came_kv2],
    )
    first_across = after(first_across, state_far[0])
    first_across_core = over(first_across, 0, 0, 1)
    rest_across = after(rest_across, first_across_core)
    rest_across_core = over(rest_across, 0, 0, 1)
    kept = [far_kv, far_across, far_core, far_across_core]
    far_first = [far_came_kv, first_across, first_core, first_across_core]
    far_rest = [far_came_kv2, rest_across, rest_core, rest_across_core]

    results = []
    for j in heads:
        parts = [(a, j, group_heads + j) for a in kept]
        if j == 0:
            parts += [(a, 0, 1) for a in far_first]
        else:
            parts += [(a, j - 1, group_heads - 1 + j - 1) for a in far_rest]
        results.append(
            attend(
                [[(own_q, j), (came_q, j)], [(far_q, j), (far_came_q, j)]],
                [parts],
                [(state_near, j), (state_far, j)],
                bias,
                (0, 2),
                len(near),
                True,
                [results[-1][0]] if j else [],
            )
        )
    results = [[r[0]] + [over(r[dz], dz, 0, 0) for dz in range(1, Z)] for r in results]
    attended = [results[j][dz] for dz in range(Z) for j in heads]
    arrived = over_y(mix(where, attended, w_out, True, 512))
    home = mix(where, attended, w_out, False, 512)
    return (home.astype(F32) + arrived.astype(F32)).astype(BF16)


def gather_all(tokens, block_order, block_mask, w_query, w_key, w_value, w_out):
    row_count = tokens.shape[0]
    local_width = w_query.shape[1]
    local_heads = local_width // HEAD_DIM
    block_count = block_order.shape[0]
    portion = lax.all_gather(tokens, "head", axis=1, tiled=True)
    query_rows, key_rows, value_rows = [
        jnp.dot(portion, weight, preferred_element_type=F32)
        .astype(BF16)
        .reshape(row_count, local_heads, HEAD_DIM)
        for weight in (w_query, w_key, w_value)
    ]
    cycle_live = block_mask[block_order][:, block_order]
    row_blocks = (
        lax.axis_index("ctx") * row_count + jnp.arange(row_count, dtype=jnp.int32)
    ) // BLOCK
    live_columns = cycle_live[row_blocks].T
    inv_root = 1.0 / HEAD_DIM**0.5

    def advance(state, inputs):
        key_tile, value_tile, offset = inputs
        keep = lax.dynamic_index_in_dim(live_columns, offset, 0, keepdims=False) > 0
        top_now, total_now, accum = state
        scores = (
            jnp.einsum("qhd,khd->hqk", query_rows, key_tile, preferred_element_type=F32)
            * inv_root
        )
        allowed = keep[None, :, None]
        top_next = jnp.maximum(top_now, jnp.max(jnp.where(allowed, scores, -1e30), axis=-1))
        factor = jnp.exp(top_now - top_next)
        weights = jnp.where(allowed, jnp.exp(scores - top_next[..., None]), 0.0)
        total_next = total_now * factor + jnp.sum(weights, axis=-1)
        accum = accum * factor[..., None] + jnp.einsum(
            "hqk,khd->hqd", weights.astype(BF16), value_tile, preferred_element_type=F32
        )
        return (top_next, total_next, accum), None

    initial = (
        jnp.full((local_heads, row_count), -1e30, F32),
        jnp.zeros((local_heads, row_count), F32),
        jnp.zeros((local_heads, row_count, HEAD_DIM), F32),
    )
    tiles = [
        lax.all_gather(part, "ctx", axis=0, tiled=True).reshape(
            block_count, BLOCK, local_heads, HEAD_DIM
        )
        for part in (key_rows, value_rows)
    ]
    (_, total, accum), _ = lax.scan(
        advance, initial, (*tiles, jnp.arange(block_count, dtype=jnp.int32))
    )
    attended = (
        (accum / total[..., None]).transpose(1, 0, 2).reshape(row_count, local_width).astype(BF16)
    )
    partial_out = jnp.dot(attended, w_out, preferred_element_type=F32)
    return lax.psum_scatter(partial_out.astype(BF16), "head", scatter_dimension=1, tiled=True)


def solution(mesh):
    in_specs = (
        P("ctx", "head"),
        P(),
        P(),
        P(None, "head"),
        P(None, "head"),
        P(None, "head"),
        P("head", None),
    )

    def per_device(tokens, block_order, block_mask, w_query, w_key, w_value, w_out):
        args = (tokens, block_order, block_mask, w_query, w_key, w_value, w_out)
        heads = w_query.shape[1] // HEAD_DIM
        fits = mesh.shape["ctx"] == Z * X * C and mesh.shape["head"] == 2 and heads % Z == 0
        return split_heads(*args) if fits else gather_all(*args)

    return jax.shard_map(
        per_device, mesh=mesh, in_specs=in_specs, out_specs=P("ctx", "head"), check_vma=False
    )
```

```python
import functools
import math

import jax
import jax.numpy as jnp
from jax import lax
from jax.experimental import pallas as pl
from jax.experimental.pallas import tpu as pltpu
from jax.sharding import PartitionSpec as P

HEAD_DIM = 128
BLOCK = 128
Z, X, C = 4, 2, 2
MIB = 1 << 20
BF16, F32 = jnp.bfloat16, jnp.float32
LIGHT = pl.CostEstimate(flops=1024, bytes_accessed=1024, transcendentals=0)


def place(z, x, c):
    return (z * X + x) * C + c


def hop(dz, dx, dc):
    return [
        (place(z, x, c), place(z ^ dz, x ^ dx, c ^ dc))
        for z in range(Z)
        for x in range(X)
        for c in range(C)
    ]


def params(mib):
    return pltpu.CompilerParams(vmem_limit_bytes=mib * MIB)


def after(value, *others):
    return lax.optimization_barrier((value, *others))[0]


def whole(count):
    return [pl.BlockSpec(memory_space=pltpu.VMEM)] * count


def fetch(where, weights, width, groups, fence):
    depth = weights[0].shape[0]
    half = depth // 2
    kinds = len(weights)

    def body(s, *refs):
        out, sems = refs[kinds + 1], refs[kinds + 2]
        copies = []
        for g in range(2):
            columns = pl.ds(pl.multiple_of((s[1] ^ groups[g]) * width, width), width)
            for k in range(kinds):
                for part in range(2):
                    rows = pl.ds(pl.multiple_of((s[0] ^ part) * half, half), half)
                    copies.append(
                        pltpu.make_async_copy(
                            refs[k].at[rows, columns],
                            out.at[g * kinds + k, pl.ds(part * half, half)],
                            sems.at[len(copies)],
                        )
                    )
        for copy in copies:
            copy.start()
        for copy in copies:
            copy.wait()

    return pl.pallas_call(
        body,
        grid_spec=pltpu.PrefetchScalarGridSpec(
            num_scalar_prefetch=1,
            grid=(),
            in_specs=[pl.BlockSpec(memory_space=pl.ANY)] * (kinds + 1),
            out_specs=pl.BlockSpec(memory_space=pltpu.VMEM),
            scratch_shapes=[pltpu.SemaphoreType.DMA((4 * kinds,))],
        ),
        out_shape=pltpu.VMEM((2 * kinds, depth, width), BF16),
        compiler_params=params(4),
        cost_estimate=LIGHT,
    )(where, *weights, fence)


def project(own, other, held, outputs, start=0):
    rows = own.shape[0] - start
    kinds = held.shape[0] // 2
    flat = [block for blocks in outputs for block in blocks]

    def body(*refs):
        held_ref, outs = refs[2], refs[3:]
        tokens = jnp.concatenate([refs[0][start:], refs[1][start:]], axis=1)
        at = [(o, i) for o, blocks in enumerate(outputs) for i in range(len(blocks))]
        for first in range(0, len(flat), 2):
            pair = flat[first : first + 2]
            weight = [
                held_ref[g * kinds + k, :, h * HEAD_DIM : (h + 1) * HEAD_DIM] for g, k, h in pair
            ]
            total = jnp.dot(
                tokens, jnp.concatenate(weight, axis=1), preferred_element_type=F32
            ).astype(BF16)
            for i in range(len(pair)):
                o, place_in = at[first + i]
                outs[o][place_in] = total[:, i * HEAD_DIM : (i + 1) * HEAD_DIM]

    return pl.pallas_call(
        body,
        in_specs=whole(3),
        out_specs=whole(len(outputs)),
        out_shape=[jax.ShapeDtypeStruct((len(b), rows, HEAD_DIM), BF16) for b in outputs],
        compiler_params=params(8),
        cost_estimate=LIGHT,
    )(own, other, held)


def take(array, ranges):
    def body(in_ref, *outs):
        for out, (first, last) in zip(outs, ranges):
            out[...] = in_ref[first:last]

    return pl.pallas_call(
        body,
        in_specs=whole(1),
        out_specs=whole(len(ranges)),
        out_shape=[
            jax.ShapeDtypeStruct((last - first,) + array.shape[1:], array.dtype)
            for first, last in ranges
        ],
        compiler_params=params(4),
        cost_estimate=LIGHT,
    )(array)


def pack(sides, picks):
    arrays = [a for side in sides for half in side for a in half]
    rows = sum(half[0].shape[1] for half in sides[0])

    def body(*refs):
        ins, outs = list(refs[: len(arrays)]), refs[len(arrays) :]
        blocks = []
        for side in sides:
            for half in side:
                blocks.append([])
                for a in half:
                    ref = ins.pop(0)
                    blocks[-1] += [(ref, b) for b in range(a.shape[0])]
        for out, wanted in zip(outs, picks):
            for n, (side, upper, lower) in enumerate(wanted):
                ref, b = blocks[2 * side][upper]
                size = ref.shape[1]
                out[n, :size] = ref[b]
                ref, b = blocks[2 * side + 1][lower]
                out[n, size:] = ref[b]

    return pl.pallas_call(
        body,
        in_specs=whole(len(arrays)),
        out_specs=whole(len(picks)),
        out_shape=[jax.ShapeDtypeStruct((len(p), rows, HEAD_DIM), BF16) for p in picks],
        compiler_params=params(4),
        cost_estimate=LIGHT,
    )(*arrays)


def mask_rows(where, block_order, block_mask, rows):
    blocks = block_order.shape[0]
    per = rows // BLOCK
    keys = blocks * BLOCK

    def body(s, order_ref, mask_ref, out_ref):
        def ids(shape, axis, shift):
            at = lax.broadcasted_iota(jnp.int32, shape, axis) >> shift
            piece = at >> (per.bit_length() - 1)
            return at & (per - 1), piece

        hot = (order_ref[...] == lax.broadcasted_iota(jnp.int32, (blocks, blocks), 0)).astype(F32)
        low, piece = ids((Z * per, blocks), 0, 0)
        want = (place(s[1] ^ piece, s[2], s[3])) * per + low
        query = (want == lax.broadcasted_iota(jnp.int32, (Z * per, blocks), 1)).astype(F32)
        low, piece = ids((blocks, keys), 1, BLOCK.bit_length() - 1)
        want = place(s[1] ^ (piece >> 2), s[2] ^ (piece & 1), s[3] ^ ((piece >> 1) & 1)) * per + low
        key = (want == lax.broadcasted_iota(jnp.int32, (blocks, keys), 0)).astype(F32)
        frames = lax.dot_general(query, hot, (((1,), (1,)), ((), ())), preferred_element_type=F32)
        live = jnp.dot(frames, mask_ref[...].astype(F32), preferred_element_type=F32)
        live = jnp.dot(live, hot, preferred_element_type=F32)
        live = jnp.dot(live, key, preferred_element_type=F32)
        out_ref[...] = jnp.where(live > 0.5, 0.0, -1e30)

    return pl.pallas_call(
        body,
        grid_spec=pltpu.PrefetchScalarGridSpec(
            num_scalar_prefetch=1, grid=(), in_specs=whole(2), out_specs=whole(1)[0]
        ),
        out_shape=jax.ShapeDtypeStruct((Z * per, keys), F32),
        compiler_params=params(8),
        cost_estimate=LIGHT,
    )(where, block_order[None, :], block_mask)


def attend(queries, parts, states, bias, query_at, key_at, last, fences, earlier=()):
    rows = queries[0][0][0].shape[1]
    tile = parts[0][0][0].shape[1]
    n = len(parts[0])
    group = 4
    scale = math.log2(math.e) / math.sqrt(HEAD_DIM)
    per = rows // BLOCK
    both = 2 * rows
    steps = len(queries)
    same_parts = len(parts) == 1

    def body(*refs):
        refs = list(refs)

        def take(count):
            got = refs[:count]
            del refs[:count]
            return got

        q_refs = take(2 * steps)
        k_refs, v_refs = take(n), take(n)
        state_refs = [take(3) for _ in states]
        (bias_ref,) = take(1)
        take(len(fences))
        earlier_refs = take(len(earlier))
        outs = take(2 * steps if last else 3)
        q_ref = refs[0]
        step = pl.program_id(0)
        for i in range(steps):

            @pl.when(step == i)
            def _(i=i):
                q_ref[:rows] = q_refs[2 * i][0]
                q_ref[rows:] = q_refs[2 * i + 1][0]
                if states:
                    for held, ref in zip(refs[1:], state_refs[i]):
                        held[...] = ref[0]

        query = q_ref[...]
        if states:
            top, total, accum = refs[1][:, :1], refs[2][...], refs[3][...]
        else:
            top = jnp.full((both, 1), -1e30, F32)
            total = jnp.zeros((both, HEAD_DIM), F32)
            accum = jnp.zeros((both, HEAD_DIM), F32)
        first_row = (query_at[0] + step * query_at[1]) * per
        for t in range(0, n, group):
            key = jnp.concatenate([k_refs[u][0] for u in range(t, t + group)], axis=0)
            value = jnp.concatenate([v_refs[u][0] for u in range(t, t + group)], axis=0)
            width = group * tile
            at = (key_at + t) * tile
            score = lax.dot_general(
                query, key, (((1,), (1,)), ((), ())), preferred_element_type=F32
            )
            keep = [
                jnp.broadcast_to(bias_ref[pl.ds(first_row + r, 1), at : at + width], (BLOCK, width))
                for r in range(2 * per)
            ]
            score = score + jnp.concatenate(keep, axis=0)
            best = score[:, :HEAD_DIM]
            for u in range(HEAD_DIM, width, HEAD_DIM):
                best = jnp.maximum(best, score[:, u : u + HEAD_DIM])
            top_next = jnp.maximum(top, jnp.max(best, axis=1, keepdims=True))
            factor = jnp.exp2((top - top_next) * scale)
            top = top_next
            weight = jnp.exp2(score * scale - top * scale)
            add = weight[:, :HEAD_DIM]
            for u in range(HEAD_DIM, width, HEAD_DIM):
                add = add + weight[:, u : u + HEAD_DIM]
            total = total * factor + add
            accum = accum * factor + jnp.dot(
                weight.astype(BF16), value, preferred_element_type=F32
            )
        if last:
            result = (accum / jnp.sum(total, axis=1, keepdims=True)).astype(BF16)
            for i in range(steps):

                @pl.when(step == i)
                def _(i=i):
                    for half in range(2):
                        out, piece = outs[2 * i + half], result[half * rows : (half + 1) * rows]
                        if earlier:
                            before = earlier_refs[2 * i + half][...]
                            piece = jnp.concatenate([before, piece], axis=1)
                        out[...] = piece

        else:
            outs[0][0] = jnp.broadcast_to(top, (both, HEAD_DIM))
            outs[1][0] = total
            outs[2][0] = accum

    def fixed(block, index):
        return pl.BlockSpec(block, lambda i: (index,) + (0,) * (len(block) - 1))

    def part_spec(kind):
        def one(u):
            base = parts[0][u][2 * kind + 1]
            stride = 0 if same_parts else 1
            return pl.BlockSpec((1, tile, HEAD_DIM), lambda i: (base + i * stride, 0, 0))

        return [one(u) for u in range(n)]

    arrays = [p[2 * kind] for kind in range(2) for p in parts[0]]
    state_block = (1, both, HEAD_DIM)
    if last:
        out_width = HEAD_DIM + (earlier[0].shape[1] if earlier else 0)
        out_specs = [pl.BlockSpec((rows, out_width), lambda i: (0, 0))] * (2 * steps)
        out_shape = [jax.ShapeDtypeStruct((rows, out_width), BF16)] * (2 * steps)
    else:
        out_specs = [pl.BlockSpec(state_block, lambda i: (i, 0, 0))] * 3
        out_shape = [jax.ShapeDtypeStruct((steps, both, HEAD_DIM), F32)] * 3
    return pl.pallas_call(
        body,
        grid=(steps,),
        in_specs=[fixed((1, rows, HEAD_DIM), at) for row in queries for _, at in row]
        + part_spec(0)
        + part_spec(1)
        + [fixed(state_block, at) for _, at in states for _ in range(3)]
        + [pl.BlockSpec(bias.shape, lambda i: (0, 0))]
        + [pl.BlockSpec(memory_space=pl.ANY)] * len(fences)
        + [pl.BlockSpec(e.shape, lambda i: (0, 0)) for e in earlier],
        out_specs=out_specs,
        out_shape=out_shape,
        scratch_shapes=[pltpu.VMEM((both, HEAD_DIM), BF16)]
        + [pltpu.VMEM((both, HEAD_DIM), F32)] * (3 if states else 0),
        compiler_params=params(24),
        cost_estimate=LIGHT,
    )(
        *[a for row in queries for a, _ in row],
        *arrays,
        *[a for held, _ in states for a in held],
        bias,
        *fences,
        *earlier,
    )


def fetch_out(where, w_out, fence):
    depth, width = w_out.shape
    group, half = depth // Z, width // 2

    def body(s, w_ref, fence_ref, out, sems):
        copies = []
        for dz in range(Z):
            rows = pl.ds(pl.multiple_of((s[1] ^ dz) * group, group), group)
            for part in range(2):
                columns = pl.ds(pl.multiple_of((1 - s[0] if part == 0 else s[0]) * half, half), half)
                copies.append(
                    pltpu.make_async_copy(
                        w_ref.at[rows, columns],
                        out.at[pl.ds(dz * group, group), pl.ds(part * half, half)],
                        sems.at[len(copies)],
                    )
                )
        for copy in copies:
            copy.start()
        for copy in copies:
            copy.wait()

    return pl.pallas_call(
        body,
        grid_spec=pltpu.PrefetchScalarGridSpec(
            num_scalar_prefetch=1,
            grid=(),
            in_specs=[pl.BlockSpec(memory_space=pl.ANY)] * 2,
            out_specs=whole(1)[0],
            scratch_shapes=[pltpu.SemaphoreType.DMA((2 * Z,))],
        ),
        out_shape=pltpu.VMEM((depth, width), BF16),
        compiler_params=params(4),
        cost_estimate=LIGHT,
    )(where, w_out, fence)


def mix(attended, held, skip, columns, earlier, out_type):
    rows, width = attended[0].shape
    depth = held.shape[0] // Z
    count = len(attended)
    first, last = columns
    step = (last - first) // 3

    def body(*refs):
        rows_all = jnp.concatenate([r[...] for r in refs[:count]], axis=1)
        for i in range(3):
            at = slice(first + i * step, first + (i + 1) * step)
            weight = jnp.concatenate(
                [
                    refs[count][g * depth + skip : g * depth + skip + width, at]
                    for g in range(count)
                ],
                axis=0,
            )
            total = jnp.dot(rows_all, weight, preferred_element_type=F32)
            if earlier is not None:
                total += refs[count + 1][:, at]
            refs[-1][:, i * step : (i + 1) * step] = total.astype(out_type)

    more = [] if earlier is None else [earlier]
    return pl.pallas_call(
        body,
        in_specs=whole(count + 1 + len(more)),
        out_specs=whole(1)[0],
        out_shape=jax.ShapeDtypeStruct((rows, last - first), out_type),
        compiler_params=params(16),
        cost_estimate=LIGHT,
    )(*attended, held, *more)


def split_heads(tokens, block_order, block_mask, w_query, w_key, w_value, w_out):
    rows, half = tokens.shape
    group_heads = w_query.shape[1] // HEAD_DIM // Z
    cut = rows * 9 // 16
    ctx = lax.axis_index("ctx")
    y = lax.axis_index("head")
    where = jnp.stack([y, ctx // (X * C), (ctx // C) % X, ctx % C]).astype(jnp.int32)
    weights = [pltpu.with_memory_space_constraint(w, pltpu.HBM) for w in (w_query, w_key, w_value)]
    w_out = pltpu.with_memory_space_constraint(w_out, pltpu.HBM)
    heads = range(group_heads)
    span = group_heads * HEAD_DIM

    def over_y(a):
        return lax.ppermute(a, "head", [(0, 1), (1, 0)])

    def over(a, dz, dx, dc):
        return lax.ppermute(a, "ctx", hop(dz, dx, dc))

    def pairs(group, wanted):
        return [(group, kind, h) for kind in (1, 2) for h in wanted]

    def singles(group):
        return [(group, 0, h) for h in heads]

    other = over_y(tokens)
    far = over(tokens[:cut], 2, 0, 0)
    bias = mask_rows(where, block_order, block_mask, rows)
    held = fetch(where, weights, span, (0, 1), bias)
    held_far = fetch(where, weights, span, (2, 3), held)

    other = after(other, held_far)
    own_kv, sent = project(
        tokens, other, held, [pairs(0, heads), singles(1) + pairs(1, heads)]
    )
    came = over(sent, 1, 0, 0)
    own_across = over(own_kv, 0, 1, 0)
    own_core = over(own_kv, 0, 0, 1)
    far = after(far, sent)
    far_other = over_y(far)
    low2, low3 = project(
        after(tokens, far),
        other,
        held_far,
        [singles(0) + pairs(0, heads), singles(1) + pairs(1, heads)],
        cut,
    )
    (own_q,) = project(after(tokens, own_core, low2), other, held, [singles(0)])
    low2 = over(low2, 2, 0, 0)
    low3 = over(low3, 3, 0, 0)
    out_held = fetch_out(where, w_out, own_q)
    own_across = after(own_across, out_held)
    own_across_core = over(own_across, 0, 0, 1)

    far_sent_q, far_sent, far_kept = project(
        far,
        after(far_other, out_held),
        held,
        [singles(1), pairs(1, heads), singles(0) + pairs(0, heads)],
    )
    far_came_q = over(far_sent_q, 1, 0, 0)
    far_came = over(far_sent, 1, 0, 0)
    came = after(came, far_sent, own_across)
    n = group_heads
    came_kv, came_k, came_v = take(came, [(n, 3 * n), (n, 2 * n), (2 * n, 3 * n)])
    across_k = over(came_k, 0, 1, 0)
    across_v = over(came_v, 0, 1, 0)
    came_core = over(came_kv, 0, 0, 1)
    across_core_k = over(across_k, 0, 0, 1)
    across_core_v = over(across_v, 0, 0, 1)

    first, rest = (0,), tuple(heads)[1:]
    far_came = after(far_came, across_k, across_v, low2, low3)
    sides = [[[far_kept], [low2]], [[far_came], [low3]]]

    def picks(chunk):
        kept = [(0, k * n + h, k * n + h) for k in (1, 2) for h in chunk]
        return kept + [(1, (k - 1) * n + h, k * n + h) for k in (1, 2) for h in chunk]

    far_first, far_rest, far_q = pack(
        sides, [picks(first), picks(rest), [(0, h, h) for h in heads]]
    )
    first_across = over(far_first, 0, 1, 0)
    first_core = over(far_first, 0, 0, 1)
    rest_across = over(far_rest, 0, 1, 0)
    rest_core = over(far_rest, 0, 0, 1)

    near = [(a, 0, a, n) for a in (own_kv, own_across, own_core, own_across_core)]
    near += [
        (came_kv, 0, came_kv, n),
        (across_k, 0, across_v, 0),
        (came_core, 0, came_core, n),
        (across_core_k, 0, across_core_v, 0),
    ]
    near_parts = [near, None]
    state_near = attend(
        [[(own_q, j), (came, j)] for j in heads], near_parts, [], bias, (0, 0), 0, False, [far_first]
    )
    (far_came_q,) = pack(
        [[[after(far_came_q, state_near[0])], [low3]]], [[(0, h, h) for h in heads]]
    )
    state_far = attend(
        [[(far_q, j), (far_came_q, j)] for j in heads],
        near_parts,
        [],
        bias,
        (2, 0),
        0,
        False,
        [state_near[0]],
    )
    first_across = after(first_across, state_far[0])
    first_across_core = over(first_across, 0, 0, 1)

    results = []
    for j in heads:
        if j == 0:
            arrays, size, at = [far_first, first_across, first_core, first_across_core], 1, 0
            fences = []
        else:
            if j == 1:
                rest_across = after(rest_across, results[0][0])
                rest_across_core = over(rest_across, 0, 0, 1)
            arrays, size, at = [far_rest, rest_across, rest_core, rest_across_core], len(rest), j - 1
            fences = [results[-1][0]]
        parts = [
            (a, 2 * i * size + at, a, (2 * i + 1) * size + at) for i in range(2) for a in arrays
        ]
        rows_out = attend(
            [[(own_q, j), (came, j)], [(far_q, j), (far_came_q, j)]],
            [parts],
            [(state_near, j), (state_far, j)],
            bias,
            (0, 2),
            len(near),
            True,
            fences,
            results.pop() if j == 1 else (),
        )
        results.append(rows_out)
    results = [[r[0]] + [over(r[dz], dz, 0, 0) for dz in range(1, Z)] for r in results]
    width = w_out.shape[1]
    skip = results[0][0].shape[1]
    partial = mix(results[0], out_held, 0, (0, width), None, F32)
    rest = results[1][:-1] + [after(results[1][-1], partial)]
    away = mix(rest, out_held, skip, (0, width // 2), partial, BF16)
    arrived = over_y(away)
    rest = rest[:-1] + [after(rest[-1], away)]
    home = mix(rest, out_held, skip, (width // 2, width), partial, BF16)
    return (home.astype(F32) + arrived.astype(F32)).astype(BF16)


def gather_all(tokens, block_order, block_mask, w_query, w_key, w_value, w_out):
    row_count = tokens.shape[0]
    local_width = w_query.shape[1]
    local_heads = local_width // HEAD_DIM
    block_count = block_order.shape[0]
    portion = lax.all_gather(tokens, "head", axis=1, tiled=True)
    query_rows, key_rows, value_rows = [
        jnp.dot(portion, weight, preferred_element_type=F32)
        .astype(BF16)
        .reshape(row_count, local_heads, HEAD_DIM)
        for weight in (w_query, w_key, w_value)
    ]
    cycle_live = block_mask[block_order][:, block_order]
    row_blocks = (
        lax.axis_index("ctx") * row_count + jnp.arange(row_count, dtype=jnp.int32)
    ) // BLOCK
    live_columns = cycle_live[row_blocks].T
    inv_root = 1.0 / HEAD_DIM**0.5

    def advance(state, inputs):
        key_tile, value_tile, offset = inputs
        keep = lax.dynamic_index_in_dim(live_columns, offset, 0, keepdims=False) > 0
        top_now, total_now, accum = state
        scores = (
            jnp.einsum("qhd,khd->hqk", query_rows, key_tile, preferred_element_type=F32)
            * inv_root
        )
        allowed = keep[None, :, None]
        top_next = jnp.maximum(top_now, jnp.max(jnp.where(allowed, scores, -1e30), axis=-1))
        factor = jnp.exp(top_now - top_next)
        weights = jnp.where(allowed, jnp.exp(scores - top_next[..., None]), 0.0)
        total_next = total_now * factor + jnp.sum(weights, axis=-1)
        accum = accum * factor[..., None] + jnp.einsum(
            "hqk,khd->hqd", weights.astype(BF16), value_tile, preferred_element_type=F32
        )
        return (top_next, total_next, accum), None

    initial = (
        jnp.full((local_heads, row_count), -1e30, F32),
        jnp.zeros((local_heads, row_count), F32),
        jnp.zeros((local_heads, row_count, HEAD_DIM), F32),
    )
    tiles = [
        lax.all_gather(part, "ctx", axis=0, tiled=True).reshape(
            block_count, BLOCK, local_heads, HEAD_DIM
        )
        for part in (key_rows, value_rows)
    ]
    (_, total, accum), _ = lax.scan(
        advance, initial, (*tiles, jnp.arange(block_count, dtype=jnp.int32))
    )
    attended = (
        (accum / total[..., None]).transpose(1, 0, 2).reshape(row_count, local_width).astype(BF16)
    )
    partial_out = jnp.dot(attended, w_out, preferred_element_type=F32)
    return lax.psum_scatter(partial_out.astype(BF16), "head", scatter_dimension=1, tiled=True)


def solution(mesh):
    in_specs = (
        P("ctx", "head"),
        P(),
        P(),
        P(None, "head"),
        P(None, "head"),
        P(None, "head"),
        P("head", None),
    )

    def per_device(tokens, block_order, block_mask, w_query, w_key, w_value, w_out):
        args = (tokens, block_order, block_mask, w_query, w_key, w_value, w_out)
        heads = w_query.shape[1] // HEAD_DIM
        fits = mesh.shape["ctx"] == Z * X * C and mesh.shape["head"] == 2 and heads % Z == 0
        return split_heads(*args) if fits else gather_all(*args)

    return jax.shard_map(
        per_device, mesh=mesh, in_specs=in_specs, out_specs=P("ctx", "head"), check_vma=False
    )
```

```python
import functools
import math

import jax
import jax.numpy as jnp
from jax import lax
from jax.experimental import pallas as pl
from jax.experimental.pallas import tpu as pltpu
from jax.sharding import PartitionSpec as P

HEAD_DIM = 128
BLOCK = 128
Z, X, C = 4, 2, 2
MIB = 1 << 20
BF16, F32 = jnp.bfloat16, jnp.float32
LIGHT = pl.CostEstimate(flops=1024, bytes_accessed=1024, transcendentals=0)
SOME = pl.CostEstimate(flops=1024, bytes_accessed=1 << 20, transcendentals=0)


def place(z, x, c):
    return (z * X + x) * C + c


def hop(dz, dx, dc):
    return [
        (place(z, x, c), place(z ^ dz, x ^ dx, c ^ dc))
        for z in range(Z)
        for x in range(X)
        for c in range(C)
    ]


def params(mib):
    return pltpu.CompilerParams(vmem_limit_bytes=mib * MIB)


def after(value, *others):
    return lax.optimization_barrier((value, *others))[0]


def whole(count):
    return [pl.BlockSpec(memory_space=pltpu.VMEM)] * count


def fetch(where, weights, width, groups, fence):
    depth = weights[0].shape[0]
    half = depth // 2
    kinds = len(weights)

    def body(s, *refs):
        out, sems = refs[kinds + 1], refs[kinds + 2]
        copies = []
        for g in range(2):
            columns = pl.ds(pl.multiple_of((s[1] ^ groups[g]) * width, width), width)
            for k in range(kinds):
                for part in range(2):
                    rows = pl.ds(pl.multiple_of((s[0] ^ part) * half, half), half)
                    copies.append(
                        pltpu.make_async_copy(
                            refs[k].at[rows, columns],
                            out.at[g * kinds + k, pl.ds(part * half, half)],
                            sems.at[len(copies)],
                        )
                    )
        for copy in copies:
            copy.start()
        for copy in copies:
            copy.wait()

    return pl.pallas_call(
        body,
        grid_spec=pltpu.PrefetchScalarGridSpec(
            num_scalar_prefetch=1,
            grid=(),
            in_specs=[pl.BlockSpec(memory_space=pl.ANY)] * (kinds + 1),
            out_specs=pl.BlockSpec(memory_space=pltpu.VMEM),
            scratch_shapes=[pltpu.SemaphoreType.DMA((4 * kinds,))],
        ),
        out_shape=pltpu.VMEM((2 * kinds, depth, width), BF16),
        compiler_params=params(4),
        cost_estimate=LIGHT,
    )(where, *weights, fence)


def project(own, other, held, outputs, start=0):
    rows = own.shape[0] - start
    kinds = held.shape[0] // 2
    flat = [block for blocks in outputs for block in blocks]

    def body(*refs):
        held_ref, outs = refs[2], refs[3:]
        tokens = jnp.concatenate([refs[0][start:], refs[1][start:]], axis=1)
        at = [(o, i) for o, blocks in enumerate(outputs) for i in range(len(blocks))]
        for first in range(0, len(flat), 2):
            pair = flat[first : first + 2]
            weight = [
                held_ref[g * kinds + k, :, h * HEAD_DIM : (h + 1) * HEAD_DIM] for g, k, h in pair
            ]
            total = jnp.dot(
                tokens, jnp.concatenate(weight, axis=1), preferred_element_type=F32
            ).astype(BF16)
            for i in range(len(pair)):
                o, place_in = at[first + i]
                outs[o][place_in] = total[:, i * HEAD_DIM : (i + 1) * HEAD_DIM]

    return pl.pallas_call(
        body,
        in_specs=whole(3),
        out_specs=whole(len(outputs)),
        out_shape=[jax.ShapeDtypeStruct((len(b), rows, HEAD_DIM), BF16) for b in outputs],
        compiler_params=params(8),
        cost_estimate=LIGHT,
    )(own, other, held)


def take(array, ranges):
    def body(in_ref, *outs):
        for out, (first, last) in zip(outs, ranges):
            out[...] = in_ref[first:last]

    return pl.pallas_call(
        body,
        in_specs=whole(1),
        out_specs=whole(len(ranges)),
        out_shape=[
            jax.ShapeDtypeStruct((last - first,) + array.shape[1:], array.dtype)
            for first, last in ranges
        ],
        compiler_params=params(4),
        cost_estimate=LIGHT,
    )(array)


def pack(sides, picks):
    arrays = [a for side in sides for half in side for a in half]
    rows = sum(half[0].shape[1] for half in sides[0])

    def body(*refs):
        ins, outs = list(refs[: len(arrays)]), refs[len(arrays) :]
        blocks = []
        for side in sides:
            for half in side:
                blocks.append([])
                for a in half:
                    ref = ins.pop(0)
                    blocks[-1] += [(ref, b) for b in range(a.shape[0])]
        for out, wanted in zip(outs, picks):
            for n, (side, upper, lower) in enumerate(wanted):
                ref, b = blocks[2 * side][upper]
                size = ref.shape[1]
                out[n, :size] = ref[b]
                ref, b = blocks[2 * side + 1][lower]
                out[n, size:] = ref[b]

    return pl.pallas_call(
        body,
        in_specs=whole(len(arrays)),
        out_specs=whole(len(picks)),
        out_shape=[jax.ShapeDtypeStruct((len(p), rows, HEAD_DIM), BF16) for p in picks],
        compiler_params=params(4),
        cost_estimate=LIGHT,
    )(*arrays)


def mask_rows(where, block_order, block_mask, rows):
    blocks = block_order.shape[0]
    per = rows // BLOCK
    keys = blocks * BLOCK

    def body(s, order_ref, mask_ref, out_ref):
        def ids(shape, axis, shift):
            at = lax.broadcasted_iota(jnp.int32, shape, axis) >> shift
            piece = at >> (per.bit_length() - 1)
            return at & (per - 1), piece

        hot = (order_ref[...] == lax.broadcasted_iota(jnp.int32, (blocks, blocks), 0)).astype(F32)
        low, piece = ids((Z * per, blocks), 0, 0)
        want = (place(s[1] ^ piece, s[2], s[3])) * per + low
        query = (want == lax.broadcasted_iota(jnp.int32, (Z * per, blocks), 1)).astype(F32)
        low, piece = ids((blocks, keys), 1, BLOCK.bit_length() - 1)
        want = place(s[1] ^ (piece >> 2), s[2] ^ (piece & 1), s[3] ^ ((piece >> 1) & 1)) * per + low
        key = (want == lax.broadcasted_iota(jnp.int32, (blocks, keys), 0)).astype(F32)
        frames = lax.dot_general(query, hot, (((1,), (1,)), ((), ())), preferred_element_type=F32)
        live = jnp.dot(frames, mask_ref[...].astype(F32), preferred_element_type=F32)
        live = jnp.dot(live, hot, preferred_element_type=F32)
        live = jnp.dot(live, key, preferred_element_type=F32)
        out_ref[...] = jnp.where(live > 0.5, 0.0, -1e30)

    return pl.pallas_call(
        body,
        grid_spec=pltpu.PrefetchScalarGridSpec(
            num_scalar_prefetch=1, grid=(), in_specs=whole(2), out_specs=whole(1)[0]
        ),
        out_shape=jax.ShapeDtypeStruct((Z * per, keys), F32),
        compiler_params=params(8),
        cost_estimate=LIGHT,
    )(where, block_order[None, :], block_mask)


def attend(steps, parts, stride, bias, mask_at, mask_stride, key_at, outputs, earlier, fences):
    tile = parts[0][0].shape[1]
    n, count = len(parts), len(steps)
    scale = math.log2(math.e) / math.sqrt(HEAD_DIM)
    every = sum(q[3] for q in steps[0][0])
    width = n * tile
    carried = bool(steps[0][1])
    arrays = []

    def index_of(array):
        for i, known in enumerate(arrays):
            if known is array:
                return i
        arrays.append(array)
        return len(arrays) - 1

    plan = [
        (
            [(index_of(q), *rest) for q, *rest in queries],
            [([index_of(a) for a in held], *rest) for held, *rest in states],
            results,
        )
        for queries, states, results in steps
    ]
    part_plan = [(index_of(p[0]), p[1], index_of(p[2]), p[3]) for p in parts]
    earlier_plan = [(index_of(a), low, out) for a, low, out in earlier]
    bias_index = index_of(bias)
    total_arrays = len(arrays)

    def body(*refs):
        ins = refs[:total_arrays]
        outs = refs[total_arrays + len(fences) :]
        q_ref = outs[-1 - (3 if carried else 0)]
        held_refs = outs[len(outs) - 3 :]
        step = pl.program_id(0)
        for i, (queries, states, _) in enumerate(plan):

            @pl.when(step == i)
            def _(i=i, queries=queries, states=states):
                at = 0
                for q, block, low, size in queries:
                    q_ref[at : at + size] = ins[q][block, low : low + size]
                    at += size
                at = 0
                for held, block, low, size in states:
                    for k in range(3):
                        held_refs[k][at : at + size] = ins[held[k]][block, low : low + size]
                    at += size
                if i == 0:
                    for a, low, out in earlier_plan:
                        outs[out][:, :HEAD_DIM] = ins[a][low : low + outs[out].shape[0]]

        shift = step * stride
        key = jnp.concatenate([ins[k][at + shift] for k, at, _, _ in part_plan], axis=0)
        value = jnp.concatenate([ins[v][at + shift] for _, _, v, at in part_plan], axis=0)
        if carried:
            top, total, accum = held_refs[0][:, :1], held_refs[1][...], held_refs[2][...]
        else:
            top = jnp.full((every, 1), -1e30, F32)
            total = jnp.zeros((every, HEAD_DIM), F32)
            accum = jnp.zeros((every, HEAD_DIM), F32)
        score = lax.dot_general(
            q_ref[...], key, (((1,), (1,)), ((), ())), preferred_element_type=F32
        )
        columns = slice(key_at * tile, key_at * tile + width)
        keep = [
            jnp.broadcast_to(
                ins[bias_index][pl.ds(row + step * mask_stride, 1), columns], (BLOCK, width)
            )
            for row in mask_at
        ]
        score = score + jnp.concatenate(keep, axis=0)
        best = score[:, :HEAD_DIM]
        for u in range(HEAD_DIM, width, HEAD_DIM):
            best = jnp.maximum(best, score[:, u : u + HEAD_DIM])
        top_next = jnp.maximum(top, jnp.max(best, axis=1, keepdims=True))
        factor = jnp.exp2((top - top_next) * scale)
        weight = jnp.exp2(score * scale - top_next * scale)
        add = weight[:, :HEAD_DIM]
        for u in range(HEAD_DIM, width, HEAD_DIM):
            add = add + weight[:, u : u + HEAD_DIM]
        total = total * factor + add
        accum = accum * factor + jnp.dot(weight.astype(BF16), value, preferred_element_type=F32)
        if outputs is None:
            outs[0][step] = jnp.broadcast_to(top_next, (every, HEAD_DIM))
            outs[1][step] = total
            outs[2][step] = accum
            return
        result = (accum / jnp.sum(total, axis=1, keepdims=True)).astype(BF16)
        for i, (queries, _, results) in enumerate(plan):

            @pl.when(step == i)
            def _(queries=queries, results=results):
                at = 0
                for (_, _, _, size), (out, head) in zip(queries, results):
                    lanes = slice(head * HEAD_DIM, (head + 1) * HEAD_DIM)
                    outs[out][:, lanes] = result[at : at + size]
                    at += size

    if outputs is None:
        out_shape = [jax.ShapeDtypeStruct((count, every, HEAD_DIM), F32)] * 3
    else:
        out_shape = [jax.ShapeDtypeStruct(shape, BF16) for shape in outputs]
    return pl.pallas_call(
        body,
        grid=(count,),
        in_specs=whole(total_arrays) + [pl.BlockSpec(memory_space=pl.ANY)] * len(fences),
        out_specs=whole(len(out_shape)),
        out_shape=out_shape,
        scratch_shapes=[pltpu.VMEM((every, HEAD_DIM), BF16)]
        + [pltpu.VMEM((every, HEAD_DIM), F32)] * (3 if carried else 0),
        compiler_params=params(24),
        cost_estimate=LIGHT,
    )(*arrays, *fences)


def fetch_out(where, w_out, fence):
    depth, width = w_out.shape
    group, half = depth // Z, width // 2

    def body(s, w_ref, fence_ref, out, sems):
        copies = []
        for dz in range(Z):
            rows = pl.ds(pl.multiple_of((s[1] ^ dz) * group, group), group)
            for part in range(2):
                columns = pl.ds(pl.multiple_of((1 - s[0] if part == 0 else s[0]) * half, half), half)
                copies.append(
                    pltpu.make_async_copy(
                        w_ref.at[rows, columns],
                        out.at[pl.ds(dz * group, group), pl.ds(part * half, half)],
                        sems.at[len(copies)],
                    )
                )
        for copy in copies:
            copy.start()
        for copy in copies:
            copy.wait()

    return pl.pallas_call(
        body,
        grid_spec=pltpu.PrefetchScalarGridSpec(
            num_scalar_prefetch=1,
            grid=(),
            in_specs=[pl.BlockSpec(memory_space=pl.ANY)] * 2,
            out_specs=whole(1)[0],
            scratch_shapes=[pltpu.SemaphoreType.DMA((2 * Z,))],
        ),
        out_shape=pltpu.VMEM((depth, width), BF16),
        compiler_params=params(4),
        cost_estimate=LIGHT,
    )(where, w_out, fence)


def mix(attended, held, part):
    rows = attended[0].shape[0]
    half = held.shape[1] // 2
    count = len(attended)
    step = half // 3

    def body(*refs):
        rows_all = jnp.concatenate([r[...] for r in refs[:count]], axis=1)
        for i in range(3):
            weight = refs[count][:, part * half + i * step : part * half + (i + 1) * step]
            refs[-1][:, i * step : (i + 1) * step] = jnp.dot(
                rows_all, weight, preferred_element_type=F32
            ).astype(BF16)

    return pl.pallas_call(
        body,
        in_specs=whole(count + 1),
        out_specs=whole(1)[0],
        out_shape=jax.ShapeDtypeStruct((rows, half), BF16),
        compiler_params=params(16),
        cost_estimate=LIGHT,
    )(*attended, held)


def finish(home, arrived, above, cost):
    rows, width = home.shape
    first = 0 if above is None else above.shape[0]

    def body(*refs):
        total = refs[0][...].astype(F32) + refs[1][...].astype(F32)
        if above is not None:
            refs[-1][:first] = refs[2][...]
        refs[-1][first:] = total.astype(BF16)

    more = [] if above is None else [above]
    return pl.pallas_call(
        body,
        in_specs=whole(2 + len(more)),
        out_specs=whole(1)[0],
        out_shape=jax.ShapeDtypeStruct((first + rows, width), BF16),
        compiler_params=params(8),
        cost_estimate=cost,
    )(home, arrived, *more)


def split_heads(tokens, block_order, block_mask, w_query, w_key, w_value, w_out):
    rows, half = tokens.shape
    group_heads = w_query.shape[1] // HEAD_DIM // Z
    per = rows // BLOCK
    cut = rows * 9 // 16
    ctx = lax.axis_index("ctx")
    y = lax.axis_index("head")
    where = jnp.stack([y, ctx // (X * C), (ctx // C) % X, ctx % C]).astype(jnp.int32)
    weights = [pltpu.with_memory_space_constraint(w, pltpu.HBM) for w in (w_query, w_key, w_value)]
    w_out = pltpu.with_memory_space_constraint(w_out, pltpu.HBM)
    heads = range(group_heads)
    span = group_heads * HEAD_DIM

    def over_y(a):
        return lax.ppermute(a, "head", [(0, 1), (1, 0)])

    def over(a, dz, dx, dc):
        return lax.ppermute(a, "ctx", hop(dz, dx, dc))

    def pairs(group, wanted):
        return [(group, kind, h) for kind in (1, 2) for h in wanted]

    def singles(group):
        return [(group, 0, h) for h in heads]

    other = over_y(tokens)
    far = over(tokens[:cut], 2, 0, 0)
    bias = mask_rows(where, block_order, block_mask, rows)
    held = fetch(where, weights, span, (0, 1), bias)
    held_far = fetch(where, weights, span, (2, 3), held)

    other = after(other, held_far)
    own_kv, sent = project(
        tokens, other, held, [pairs(0, heads), singles(1) + pairs(1, heads)]
    )
    came = over(sent, 1, 0, 0)
    own_across = over(own_kv, 0, 1, 0)
    own_core = over(own_kv, 0, 0, 1)
    far = after(far, sent)
    far_other = over_y(far)
    low2, low3 = project(
        after(tokens, far),
        other,
        held_far,
        [singles(0) + pairs(0, heads), singles(1) + pairs(1, heads)],
        cut,
    )
    (own_q,) = project(after(tokens, own_core, low2), other, held, [singles(0)])
    low2 = over(low2, 2, 0, 0)
    low3 = over(low3, 3, 0, 0)
    out_held = fetch_out(where, w_out, own_q)
    own_across = after(own_across, out_held)
    own_across_core = over(own_across, 0, 0, 1)

    far_sent_q, far_sent, far_kept = project(
        far,
        after(far_other, out_held),
        held,
        [singles(1), pairs(1, heads), singles(0) + pairs(0, heads)],
    )
    far_came_q = over(far_sent_q, 1, 0, 0)
    far_came = over(far_sent, 1, 0, 0)
    came = after(came, far_sent, own_across)
    n = group_heads
    came_kv, came_k, came_v = take(came, [(n, 3 * n), (n, 2 * n), (2 * n, 3 * n)])
    across_k = over(came_k, 0, 1, 0)
    across_v = over(came_v, 0, 1, 0)
    came_core = over(came_kv, 0, 0, 1)
    across_core_k = over(across_k, 0, 0, 1)
    across_core_v = over(across_v, 0, 0, 1)

    first, rest = (0,), tuple(heads)[1:]
    far_came = after(far_came, across_k, across_v, low2, low3)
    sides = [[[far_kept], [low2]], [[far_came], [low3]]]

    def picks(chunk):
        kept = [(0, k * n + h, k * n + h) for k in (1, 2) for h in chunk]
        return kept + [(1, (k - 1) * n + h, k * n + h) for k in (1, 2) for h in chunk]

    far_first, far_rest, far_q = pack(
        sides, [picks(first), picks(rest), [(0, h, h) for h in heads]]
    )
    first_across = over(far_first, 0, 1, 0)
    first_core = over(far_first, 0, 0, 1)
    rest_across = over(far_rest, 0, 1, 0)
    rest_core = over(far_rest, 0, 0, 1)

    near = [(a, 0, a, n) for a in (own_kv, own_across, own_core, own_across_core)]
    near += [
        (came_kv, 0, came_kv, n),
        (across_k, 0, across_v, 0),
        (came_core, 0, came_core, n),
        (across_core_k, 0, across_core_v, 0),
    ]

    def whole_rows(arrays, j):
        return [(a, j, 0, rows) for a in arrays]

    state_near = attend(
        [(whole_rows([own_q, came], j), [], []) for j in heads],
        near,
        1,
        bias,
        range(2 * per),
        0,
        0,
        None,
        [],
        [far_first],
    )
    (far_came_q,) = pack(
        [[[after(far_came_q, state_near[0])], [low3]]], [[(0, h, h) for h in heads]]
    )
    state_far = attend(
        [(whole_rows([far_q, far_came_q], j), [], []) for j in heads],
        near,
        1,
        bias,
        range(2 * per, 4 * per),
        0,
        0,
        None,
        [],
        [state_near[0]],
    )
    first_across = after(first_across, state_far[0])
    first_across_core = over(first_across, 0, 0, 1)

    def far_parts(arrays, size):
        return [(a, 2 * i * size, a, (2 * i + 1) * size) for i in range(2) for a in arrays]

    first_rows = attend(
        [
            (whole_rows([own_q, came], 0), [(state_near, 0, 0, 2 * rows)], [(0, 0), (1, 0)]),
            (whole_rows([far_q, far_came_q], 0), [(state_far, 0, 0, 2 * rows)], [(2, 0), (3, 0)]),
        ],
        far_parts([far_first, first_across, first_core, first_across_core], 1),
        0,
        bias,
        range(2 * per),
        2 * per,
        len(near),
        [(rows, HEAD_DIM)] * Z,
        [],
        [],
    )
    rest_across = after(rest_across, first_rows[0])
    rest_across_core = over(rest_across, 0, 0, 1)
    rest_parts = far_parts([far_rest, rest_across, rest_core, rest_across_core], len(rest))
    homes, arrived, fences = [], [], []
    for low in range(0, rows, BLOCK):
        steps = [
            (
                [(a, j, low, BLOCK) for a in (own_q, came, far_q, far_came_q)],
                [(s, j, i * rows + low, BLOCK) for s in (state_near, state_far) for i in range(2)],
                [(i, j) for i in range(Z)],
            )
            for j in rest
        ]
        done = attend(
            steps,
            rest_parts,
            1,
            bias,
            [i * per + low // BLOCK for i in range(Z)],
            0,
            len(near),
            [(BLOCK, span)] * Z,
            [(first_rows[i], low, i) for i in range(Z)],
            fences,
        )
        fences = [done[0]]
        back = [done[0]] + [over(done[dz], dz, 0, 0) for dz in range(1, Z)]
        if arrived:
            back[-1] = after(back[-1], homes[0])
        away = mix(back, out_held, 0)
        arrived.append(over_y(away))
        homes.append(mix(back[:-1] + [after(back[-1], away)], out_held, 1))
    upper = finish(homes[0], arrived[0], None, SOME)
    return finish(homes[1], after(arrived[1], upper), upper, LIGHT)


def gather_all(tokens, block_order, block_mask, w_query, w_key, w_value, w_out):
    row_count = tokens.shape[0]
    local_width = w_query.shape[1]
    local_heads = local_width // HEAD_DIM
    block_count = block_order.shape[0]
    portion = lax.all_gather(tokens, "head", axis=1, tiled=True)
    query_rows, key_rows, value_rows = [
        jnp.dot(portion, weight, preferred_element_type=F32)
        .astype(BF16)
        .reshape(row_count, local_heads, HEAD_DIM)
        for weight in (w_query, w_key, w_value)
    ]
    cycle_live = block_mask[block_order][:, block_order]
    row_blocks = (
        lax.axis_index("ctx") * row_count + jnp.arange(row_count, dtype=jnp.int32)
    ) // BLOCK
    live_columns = cycle_live[row_blocks].T
    inv_root = 1.0 / HEAD_DIM**0.5

    def advance(state, inputs):
        key_tile, value_tile, offset = inputs
        keep = lax.dynamic_index_in_dim(live_columns, offset, 0, keepdims=False) > 0
        top_now, total_now, accum = state
        scores = (
            jnp.einsum("qhd,khd->hqk", query_rows, key_tile, preferred_element_type=F32)
            * inv_root
        )
        allowed = keep[None, :, None]
        top_next = jnp.maximum(top_now, jnp.max(jnp.where(allowed, scores, -1e30), axis=-1))
        factor = jnp.exp(top_now - top_next)
        weights = jnp.where(allowed, jnp.exp(scores - top_next[..., None]), 0.0)
        total_next = total_now * factor + jnp.sum(weights, axis=-1)
        accum = accum * factor[..., None] + jnp.einsum(
            "hqk,khd->hqd", weights.astype(BF16), value_tile, preferred_element_type=F32
        )
        return (top_next, total_next, accum), None

    initial = (
        jnp.full((local_heads, row_count), -1e30, F32),
        jnp.zeros((local_heads, row_count), F32),
        jnp.zeros((local_heads, row_count, HEAD_DIM), F32),
    )
    tiles = [
        lax.all_gather(part, "ctx", axis=0, tiled=True).reshape(
            block_count, BLOCK, local_heads, HEAD_DIM
        )
        for part in (key_rows, value_rows)
    ]
    (_, total, accum), _ = lax.scan(
        advance, initial, (*tiles, jnp.arange(block_count, dtype=jnp.int32))
    )
    attended = (
        (accum / total[..., None]).transpose(1, 0, 2).reshape(row_count, local_width).astype(BF16)
    )
    partial_out = jnp.dot(attended, w_out, preferred_element_type=F32)
    return lax.psum_scatter(partial_out.astype(BF16), "head", scatter_dimension=1, tiled=True)


def solution(mesh):
    in_specs = (
        P("ctx", "head"),
        P(),
        P(),
        P(None, "head"),
        P(None, "head"),
        P(None, "head"),
        P("head", None),
    )

    def per_device(tokens, block_order, block_mask, w_query, w_key, w_value, w_out):
        args = (tokens, block_order, block_mask, w_query, w_key, w_value, w_out)
        heads = w_query.shape[1] // HEAD_DIM
        fits = mesh.shape["ctx"] == Z * X * C and mesh.shape["head"] == 2 and heads % Z == 0
        return split_heads(*args) if fits else gather_all(*args)

    return jax.shard_map(
        per_device, mesh=mesh, in_specs=in_specs, out_specs=P("ctx", "head"), check_vma=False
    )
```

```python
import functools
import math

import jax
import jax.numpy as jnp
from jax import lax
from jax.experimental import pallas as pl
from jax.experimental.pallas import tpu as pltpu
from jax.sharding import PartitionSpec as P

HEAD_DIM = 128
BLOCK = 128
Z, X, C = 4, 2, 2
MIB = 1 << 20
BF16, F32 = jnp.bfloat16, jnp.float32
LIGHT = pl.CostEstimate(flops=1024, bytes_accessed=1024, transcendentals=0)
SOME = pl.CostEstimate(flops=1024, bytes_accessed=1 << 20, transcendentals=0)


def place(z, x, c):
    return (z * X + x) * C + c


def hop(dz, dx, dc):
    return [
        (place(z, x, c), place(z ^ dz, x ^ dx, c ^ dc))
        for z in range(Z)
        for x in range(X)
        for c in range(C)
    ]


def params(mib):
    return pltpu.CompilerParams(vmem_limit_bytes=mib * MIB)


def after(value, *others):
    return lax.optimization_barrier((value, *others))[0]


def whole(count):
    return [pl.BlockSpec(memory_space=pltpu.VMEM)] * count


def fetch(where, weights, width, groups, fence, beside=None):
    depth = weights[0].shape[0]
    half = depth // 2
    kinds = len(weights)
    extra = list(beside or ())

    def body(s, *refs):
        out, sems = refs[kinds + 1 + len(extra)], refs[-1]
        copies = []
        for g in range(2):
            columns = pl.ds(pl.multiple_of((s[1] ^ groups[g]) * width, width), width)
            for k in range(kinds):
                for part in range(2):
                    rows = pl.ds(pl.multiple_of((s[0] ^ part) * half, half), half)
                    copies.append(
                        pltpu.make_async_copy(
                            refs[k].at[rows, columns],
                            out.at[g * kinds + k, pl.ds(part * half, half)],
                            sems.at[len(copies)],
                        )
                    )
        for copy in copies:
            copy.start()
        if extra:
            tokens_ref, held_ref = refs[kinds + 1 : kinds + 3]
            for i in range(2 * kinds):
                refs[-2][i] = jnp.dot(
                    tokens_ref[...], held_ref[i, :half], preferred_element_type=F32
                )
        for copy in copies:
            copy.wait()

    out_shape = [pltpu.VMEM((2 * kinds, depth, width), BF16)]
    if extra:
        out_shape.append(pltpu.VMEM((2 * kinds, extra[0].shape[0], width), F32))
    return pl.pallas_call(
        body,
        grid_spec=pltpu.PrefetchScalarGridSpec(
            num_scalar_prefetch=1,
            grid=(),
            in_specs=[pl.BlockSpec(memory_space=pl.ANY)] * (kinds + 1) + whole(len(extra)),
            out_specs=whole(len(out_shape)),
            scratch_shapes=[pltpu.SemaphoreType.DMA((4 * kinds,))],
        ),
        out_shape=out_shape,
        compiler_params=params(4),
        cost_estimate=LIGHT,
    )(where, *weights, fence, *extra)


def project(own, other, held, outputs, start=0, partial=None):
    rows = own.shape[0] - start
    kinds = held.shape[0] // 2
    flat = [block for blocks in outputs for block in blocks]

    def body(*refs):
        held_ref, outs = refs[2], refs[3:]
        tokens, low = jnp.concatenate([refs[0][start:], refs[1][start:]], axis=1), 0
        if partial is not None:
            tokens, low, outs = refs[1][start:], own.shape[1], refs[4:]
        at = [(o, i) for o, blocks in enumerate(outputs) for i in range(len(blocks))]
        for first in range(0, len(flat), 2):
            pair = flat[first : first + 2]
            weight = [
                held_ref[g * kinds + k, low:, h * HEAD_DIM : (h + 1) * HEAD_DIM] for g, k, h in pair
            ]
            total = jnp.dot(
                tokens, jnp.concatenate(weight, axis=1), preferred_element_type=F32
            )
            if partial is not None:
                done = [
                    refs[3][g * kinds + k, :, h * HEAD_DIM : (h + 1) * HEAD_DIM] for g, k, h in pair
                ]
                total = total + jnp.concatenate(done, axis=1)
            total = total.astype(BF16)
            for i in range(len(pair)):
                o, place_in = at[first + i]
                outs[o][place_in] = total[:, i * HEAD_DIM : (i + 1) * HEAD_DIM]

    more = [] if partial is None else [partial]
    return pl.pallas_call(
        body,
        in_specs=whole(3 + len(more)),
        out_specs=whole(len(outputs)),
        out_shape=[jax.ShapeDtypeStruct((len(b), rows, HEAD_DIM), BF16) for b in outputs],
        compiler_params=params(8),
        cost_estimate=LIGHT,
    )(own, other, held, *more)


def take(array, ranges):
    def body(in_ref, *outs):
        for out, (first, last) in zip(outs, ranges):
            out[...] = in_ref[first:last]

    return pl.pallas_call(
        body,
        in_specs=whole(1),
        out_specs=whole(len(ranges)),
        out_shape=[
            jax.ShapeDtypeStruct((last - first,) + array.shape[1:], array.dtype)
            for first, last in ranges
        ],
        compiler_params=params(4),
        cost_estimate=LIGHT,
    )(array)


def pack(sides, picks):
    arrays = [a for side in sides for half in side for a in half]
    rows = sum(half[0].shape[1] for half in sides[0])

    def body(*refs):
        ins, outs = list(refs[: len(arrays)]), refs[len(arrays) :]
        blocks = []
        for side in sides:
            for half in side:
                blocks.append([])
                for a in half:
                    ref = ins.pop(0)
                    blocks[-1] += [(ref, b) for b in range(a.shape[0])]
        for out, wanted in zip(outs, picks):
            for n, (side, upper, lower) in enumerate(wanted):
                ref, b = blocks[2 * side][upper]
                size = ref.shape[1]
                out[n, :size] = ref[b]
                ref, b = blocks[2 * side + 1][lower]
                out[n, size:] = ref[b]

    return pl.pallas_call(
        body,
        in_specs=whole(len(arrays)),
        out_specs=whole(len(picks)),
        out_shape=[jax.ShapeDtypeStruct((len(p), rows, HEAD_DIM), BF16) for p in picks],
        compiler_params=params(4),
        cost_estimate=LIGHT,
    )(*arrays)


def mask_rows(where, block_order, block_mask, rows):
    blocks = block_order.shape[0]
    per = rows // BLOCK
    keys = blocks * BLOCK

    def body(s, order_ref, mask_ref, out_ref):
        def ids(shape, axis, shift):
            at = lax.broadcasted_iota(jnp.int32, shape, axis) >> shift
            piece = at >> (per.bit_length() - 1)
            return at & (per - 1), piece

        hot = (order_ref[...] == lax.broadcasted_iota(jnp.int32, (blocks, blocks), 0)).astype(F32)
        low, piece = ids((Z * per, blocks), 0, 0)
        want = (place(s[1] ^ piece, s[2], s[3])) * per + low
        query = (want == lax.broadcasted_iota(jnp.int32, (Z * per, blocks), 1)).astype(F32)
        low, piece = ids((blocks, keys), 1, BLOCK.bit_length() - 1)
        want = place(s[1] ^ (piece >> 2), s[2] ^ (piece & 1), s[3] ^ ((piece >> 1) & 1)) * per + low
        key = (want == lax.broadcasted_iota(jnp.int32, (blocks, keys), 0)).astype(F32)
        frames = lax.dot_general(query, hot, (((1,), (1,)), ((), ())), preferred_element_type=F32)
        live = jnp.dot(frames, mask_ref[...].astype(F32), preferred_element_type=F32)
        live = jnp.dot(live, hot, preferred_element_type=F32)
        live = jnp.dot(live, key, preferred_element_type=F32)
        out_ref[...] = jnp.where(live > 0.5, 0.0, -1e30)

    return pl.pallas_call(
        body,
        grid_spec=pltpu.PrefetchScalarGridSpec(
            num_scalar_prefetch=1, grid=(), in_specs=whole(2), out_specs=whole(1)[0]
        ),
        out_shape=jax.ShapeDtypeStruct((Z * per, keys), F32),
        compiler_params=params(8),
        cost_estimate=LIGHT,
    )(where, block_order[None, :], block_mask)


def attend(steps, parts, stride, bias, mask_at, mask_stride, key_at, outputs, earlier, fences):
    tile = parts[0][0].shape[1]
    n, count = len(parts), len(steps)
    scale = math.log2(math.e) / math.sqrt(HEAD_DIM)
    every = sum(q[3] for q in steps[0][0])
    width = n * tile
    carried = bool(steps[0][1])
    arrays = []

    def index_of(array):
        for i, known in enumerate(arrays):
            if known is array:
                return i
        arrays.append(array)
        return len(arrays) - 1

    plan = [
        (
            [(index_of(q), *rest) for q, *rest in queries],
            [([index_of(a) for a in held], *rest) for held, *rest in states],
            results,
        )
        for queries, states, results in steps
    ]
    part_plan = [(index_of(p[0]), p[1], index_of(p[2]), p[3]) for p in parts]
    earlier_plan = [(index_of(a), low, out) for a, low, out in earlier]
    bias_index = index_of(bias)
    total_arrays = len(arrays)

    def body(*refs):
        ins = refs[:total_arrays]
        outs = refs[total_arrays + len(fences) :]
        q_ref = outs[-1 - (3 if carried else 0)]
        held_refs = outs[len(outs) - 3 :]
        step = pl.program_id(0)
        for i, (queries, states, _) in enumerate(plan):

            @pl.when(step == i)
            def _(i=i, queries=queries, states=states):
                at = 0
                for q, block, low, size in queries:
                    q_ref[at : at + size] = ins[q][block, low : low + size]
                    at += size
                at = 0
                for held, block, low, size in states:
                    for k in range(3):
                        held_refs[k][at : at + size] = ins[held[k]][block, low : low + size]
                    at += size
                if i == 0:
                    for a, low, out in earlier_plan:
                        outs[out][:, :HEAD_DIM] = ins[a][low : low + outs[out].shape[0]]

        shift = step * stride
        key = jnp.concatenate([ins[k][at + shift] for k, at, _, _ in part_plan], axis=0)
        value = jnp.concatenate([ins[v][at + shift] for _, _, v, at in part_plan], axis=0)
        if carried:
            top, total, accum = held_refs[0][:, :1], held_refs[1][...], held_refs[2][...]
        else:
            top = jnp.full((every, 1), -1e30, F32)
            total = jnp.zeros((every, HEAD_DIM), F32)
            accum = jnp.zeros((every, HEAD_DIM), F32)
        score = lax.dot_general(
            q_ref[...], key, (((1,), (1,)), ((), ())), preferred_element_type=F32
        )
        columns = slice(key_at * tile, key_at * tile + width)
        keep = [
            jnp.broadcast_to(
                ins[bias_index][pl.ds(row + step * mask_stride, 1), columns], (BLOCK, width)
            )
            for row in mask_at
        ]
        score = score + jnp.concatenate(keep, axis=0)
        best = score[:, :HEAD_DIM]
        for u in range(HEAD_DIM, width, HEAD_DIM):
            best = jnp.maximum(best, score[:, u : u + HEAD_DIM])
        top_next = jnp.maximum(top, jnp.max(best, axis=1, keepdims=True))
        factor = jnp.exp2((top - top_next) * scale)
        weight = jnp.exp2(score * scale - top_next * scale)
        add = weight[:, :HEAD_DIM]
        for u in range(HEAD_DIM, width, HEAD_DIM):
            add = add + weight[:, u : u + HEAD_DIM]
        total = total * factor + add
        accum = accum * factor + jnp.dot(weight.astype(BF16), value, preferred_element_type=F32)
        if outputs is None:
            outs[0][step] = jnp.broadcast_to(top_next, (every, HEAD_DIM))
            outs[1][step] = total
            outs[2][step] = accum
            return
        result = (accum / jnp.sum(total, axis=1, keepdims=True)).astype(BF16)
        for i, (queries, _, results) in enumerate(plan):

            @pl.when(step == i)
            def _(queries=queries, results=results):
                at = 0
                for (_, _, _, size), (out, head) in zip(queries, results):
                    lanes = slice(head * HEAD_DIM, (head + 1) * HEAD_DIM)
                    outs[out][:, lanes] = result[at : at + size]
                    at += size

    if outputs is None:
        out_shape = [jax.ShapeDtypeStruct((count, every, HEAD_DIM), F32)] * 3
    else:
        out_shape = [jax.ShapeDtypeStruct(shape, BF16) for shape in outputs]
    return pl.pallas_call(
        body,
        grid=(count,),
        in_specs=whole(total_arrays) + [pl.BlockSpec(memory_space=pl.ANY)] * len(fences),
        out_specs=whole(len(out_shape)),
        out_shape=out_shape,
        scratch_shapes=[pltpu.VMEM((every, HEAD_DIM), BF16)]
        + [pltpu.VMEM((every, HEAD_DIM), F32)] * (3 if carried else 0),
        compiler_params=params(24),
        cost_estimate=LIGHT,
    )(*arrays, *fences)


def fetch_out(where, w_out, fence):
    depth, width = w_out.shape
    group, half = depth // Z, width // 2

    def body(s, w_ref, fence_ref, out, sems):
        copies = []
        for dz in range(Z):
            rows = pl.ds(pl.multiple_of((s[1] ^ dz) * group, group), group)
            for part in range(2):
                columns = pl.ds(pl.multiple_of((1 - s[0] if part == 0 else s[0]) * half, half), half)
                copies.append(
                    pltpu.make_async_copy(
                        w_ref.at[rows, columns],
                        out.at[pl.ds(dz * group, group), pl.ds(part * half, half)],
                        sems.at[len(copies)],
                    )
                )
        for copy in copies:
            copy.start()
        for copy in copies:
            copy.wait()

    return pl.pallas_call(
        body,
        grid_spec=pltpu.PrefetchScalarGridSpec(
            num_scalar_prefetch=1,
            grid=(),
            in_specs=[pl.BlockSpec(memory_space=pl.ANY)] * 2,
            out_specs=whole(1)[0],
            scratch_shapes=[pltpu.SemaphoreType.DMA((2 * Z,))],
        ),
        out_shape=pltpu.VMEM((depth, width), BF16),
        compiler_params=params(4),
        cost_estimate=LIGHT,
    )(where, w_out, fence)


def mix(attended, held, part):
    rows = attended[0].shape[0]
    half = held.shape[1] // 2
    count = len(attended)
    step = half // 3

    def body(*refs):
        rows_all = jnp.concatenate([r[...] for r in refs[:count]], axis=1)
        for i in range(3):
            weight = refs[count][:, part * half + i * step : part * half + (i + 1) * step]
            refs[-1][:, i * step : (i + 1) * step] = jnp.dot(
                rows_all, weight, preferred_element_type=F32
            ).astype(BF16)

    return pl.pallas_call(
        body,
        in_specs=whole(count + 1),
        out_specs=whole(1)[0],
        out_shape=jax.ShapeDtypeStruct((rows, half), BF16),
        compiler_params=params(16),
        cost_estimate=LIGHT,
    )(*attended, held)


def finish(home, arrived, above, cost):
    rows, width = home.shape
    first = 0 if above is None else above.shape[0]

    def body(*refs):
        total = refs[0][...].astype(F32) + refs[1][...].astype(F32)
        if above is not None:
            refs[-1][:first] = refs[2][...]
        refs[-1][first:] = total.astype(BF16)

    more = [] if above is None else [above]
    return pl.pallas_call(
        body,
        in_specs=whole(2 + len(more)),
        out_specs=whole(1)[0],
        out_shape=jax.ShapeDtypeStruct((first + rows, width), BF16),
        compiler_params=params(8),
        cost_estimate=cost,
    )(home, arrived, *more)


def split_heads(tokens, block_order, block_mask, w_query, w_key, w_value, w_out):
    rows, half = tokens.shape
    group_heads = w_query.shape[1] // HEAD_DIM // Z
    per = rows // BLOCK
    cut = rows * 9 // 16
    ctx = lax.axis_index("ctx")
    y = lax.axis_index("head")
    where = jnp.stack([y, ctx // (X * C), (ctx // C) % X, ctx % C]).astype(jnp.int32)
    weights = [pltpu.with_memory_space_constraint(w, pltpu.HBM) for w in (w_query, w_key, w_value)]
    w_out = pltpu.with_memory_space_constraint(w_out, pltpu.HBM)
    heads = range(group_heads)
    span = group_heads * HEAD_DIM

    def over_y(a):
        return lax.ppermute(a, "head", [(0, 1), (1, 0)])

    def over(a, dz, dx, dc):
        return lax.ppermute(a, "ctx", hop(dz, dx, dc))

    def pairs(group, wanted):
        return [(group, kind, h) for kind in (1, 2) for h in wanted]

    def singles(group):
        return [(group, 0, h) for h in heads]

    other = over_y(tokens)
    far = over(tokens[:cut], 2, 0, 0)
    (held,) = fetch(where, weights, span, (0, 1), where)
    held_far, partial = fetch(where, weights, span, (2, 3), where, (tokens, held))

    other = after(other, held_far)
    own_kv, sent = project(
        tokens,
        other,
        held,
        [pairs(0, heads), singles(1) + pairs(1, heads)],
        partial=partial,
    )
    came = over(sent, 1, 0, 0)
    own_across = over(own_kv, 0, 1, 0)
    own_core = over(own_kv, 0, 0, 1)
    far = after(far, sent)
    far_other = over_y(far)
    low2, low3 = project(
        after(tokens, far),
        other,
        held_far,
        [singles(0) + pairs(0, heads), singles(1) + pairs(1, heads)],
        cut,
    )
    (own_q,) = project(
        after(tokens, own_core, low2), other, held, [singles(0)], partial=partial
    )
    low2 = over(low2, 2, 0, 0)
    low3 = over(low3, 3, 0, 0)
    bias = mask_rows(after(where, own_q), block_order, block_mask, rows)
    out_held = fetch_out(where, w_out, bias)
    own_across = after(own_across, out_held)
    own_across_core = over(own_across, 0, 0, 1)

    far_sent_q, far_sent, far_kept = project(
        far,
        after(far_other, out_held),
        held,
        [singles(1), pairs(1, heads), singles(0) + pairs(0, heads)],
    )
    far_came_q = over(far_sent_q, 1, 0, 0)
    far_came = over(far_sent, 1, 0, 0)
    came = after(came, far_sent, own_across)
    n = group_heads
    came_kv, came_k, came_v = take(came, [(n, 3 * n), (n, 2 * n), (2 * n, 3 * n)])
    across_k = over(came_k, 0, 1, 0)
    across_v = over(came_v, 0, 1, 0)
    came_core = over(came_kv, 0, 0, 1)
    far_came = after(far_came, low2, low3)
    across_k, across_v = after(across_k, far_came), after(across_v, far_came)
    across_core_k = over(across_k, 0, 0, 1)
    across_core_v = over(across_v, 0, 0, 1)

    first, rest = (0,), tuple(heads)[1:]
    sides = [[[far_kept], [low2]], [[far_came], [low3]]]

    def picks(chunk):
        kept = [(0, k * n + h, k * n + h) for k in (1, 2) for h in chunk]
        return kept + [(1, (k - 1) * n + h, k * n + h) for k in (1, 2) for h in chunk]

    far_first, far_rest, far_q = pack(
        sides, [picks(first), picks(rest), [(0, h, h) for h in heads]]
    )
    first_across = over(far_first, 0, 1, 0)
    first_core = over(far_first, 0, 0, 1)
    rest_across = over(far_rest, 0, 1, 0)
    rest_core = over(far_rest, 0, 0, 1)

    near = [(a, 0, a, n) for a in (own_kv, own_across, own_core, own_across_core)]
    near += [
        (came_kv, 0, came_kv, n),
        (across_k, 0, across_v, 0),
        (came_core, 0, came_core, n),
        (across_core_k, 0, across_core_v, 0),
    ]

    def whole_rows(arrays, j):
        return [(a, j, 0, rows) for a in arrays]

    state_near = attend(
        [(whole_rows([own_q, came], j), [], []) for j in heads],
        near,
        1,
        bias,
        range(2 * per),
        0,
        0,
        None,
        [],
        [far_first],
    )
    (far_came_q,) = pack(
        [[[after(far_came_q, state_near[0])], [low3]]], [[(0, h, h) for h in heads]]
    )
    state_far = attend(
        [(whole_rows([far_q, far_came_q], j), [], []) for j in heads],
        near,
        1,
        bias,
        range(2 * per, 4 * per),
        0,
        0,
        None,
        [],
        [state_near[0]],
    )
    first_across = after(first_across, state_far[0])
    first_across_core = over(first_across, 0, 0, 1)

    def far_parts(arrays, size):
        return [(a, 2 * i * size, a, (2 * i + 1) * size) for i in range(2) for a in arrays]

    first_rows = attend(
        [
            (whole_rows([own_q, came], 0), [(state_near, 0, 0, 2 * rows)], [(0, 0), (1, 0)]),
            (whole_rows([far_q, far_came_q], 0), [(state_far, 0, 0, 2 * rows)], [(2, 0), (3, 0)]),
        ],
        far_parts([far_first, first_across, first_core, first_across_core], 1),
        0,
        bias,
        range(2 * per),
        2 * per,
        len(near),
        [(rows, HEAD_DIM)] * Z,
        [],
        [],
    )
    rest_across = after(rest_across, first_rows[0])
    rest_across_core = over(rest_across, 0, 0, 1)
    rest_parts = far_parts([far_rest, rest_across, rest_core, rest_across_core], len(rest))
    homes, arrived, fences = [], [], []
    for low in range(0, rows, BLOCK):
        steps = [
            (
                [(a, j, low, BLOCK) for a in (own_q, came, far_q, far_came_q)],
                [(s, j, i * rows + low, BLOCK) for s in (state_near, state_far) for i in range(2)],
                [(i, j) for i in range(Z)],
            )
            for j in rest
        ]
        done = attend(
            steps,
            rest_parts,
            1,
            bias,
            [i * per + low // BLOCK for i in range(Z)],
            0,
            len(near),
            [(BLOCK, span)] * Z,
            [(first_rows[i], low, i) for i in range(Z)],
            fences,
        )
        fences = [done[0]]
        back = [done[0]] + [over(done[dz], dz, 0, 0) for dz in range(1, Z)]
        if arrived:
            back[-1] = after(back[-1], homes[0])
        away = mix(back, out_held, 0)
        arrived.append(over_y(away))
        homes.append(mix(back[:-1] + [after(back[-1], away)], out_held, 1))
    upper = finish(homes[0], arrived[0], None, SOME)
    return finish(homes[1], after(arrived[1], upper), upper, LIGHT)


def gather_all(tokens, block_order, block_mask, w_query, w_key, w_value, w_out):
    row_count = tokens.shape[0]
    local_width = w_query.shape[1]
    local_heads = local_width // HEAD_DIM
    block_count = block_order.shape[0]
    portion = lax.all_gather(tokens, "head", axis=1, tiled=True)
    query_rows, key_rows, value_rows = [
        jnp.dot(portion, weight, preferred_element_type=F32)
        .astype(BF16)
        .reshape(row_count, local_heads, HEAD_DIM)
        for weight in (w_query, w_key, w_value)
    ]
    cycle_live = block_mask[block_order][:, block_order]
    row_blocks = (
        lax.axis_index("ctx") * row_count + jnp.arange(row_count, dtype=jnp.int32)
    ) // BLOCK
    live_columns = cycle_live[row_blocks].T
    inv_root = 1.0 / HEAD_DIM**0.5

    def advance(state, inputs):
        key_tile, value_tile, offset = inputs
        keep = lax.dynamic_index_in_dim(live_columns, offset, 0, keepdims=False) > 0
        top_now, total_now, accum = state
        scores = (
            jnp.einsum("qhd,khd->hqk", query_rows, key_tile, preferred_element_type=F32)
            * inv_root
        )
        allowed = keep[None, :, None]
        top_next = jnp.maximum(top_now, jnp.max(jnp.where(allowed, scores, -1e30), axis=-1))
        factor = jnp.exp(top_now - top_next)
        weights = jnp.where(allowed, jnp.exp(scores - top_next[..., None]), 0.0)
        total_next = total_now * factor + jnp.sum(weights, axis=-1)
        accum = accum * factor[..., None] + jnp.einsum(
            "hqk,khd->hqd", weights.astype(BF16), value_tile, preferred_element_type=F32
        )
        return (top_next, total_next, accum), None

    initial = (
        jnp.full((local_heads, row_count), -1e30, F32),
        jnp.zeros((local_heads, row_count), F32),
        jnp.zeros((local_heads, row_count, HEAD_DIM), F32),
    )
    tiles = [
        lax.all_gather(part, "ctx", axis=0, tiled=True).reshape(
            block_count, BLOCK, local_heads, HEAD_DIM
        )
        for part in (key_rows, value_rows)
    ]
    (_, total, accum), _ = lax.scan(
        advance, initial, (*tiles, jnp.arange(block_count, dtype=jnp.int32))
    )
    attended = (
        (accum / total[..., None]).transpose(1, 0, 2).reshape(row_count, local_width).astype(BF16)
    )
    partial_out = jnp.dot(attended, w_out, preferred_element_type=F32)
    return lax.psum_scatter(partial_out.astype(BF16), "head", scatter_dimension=1, tiled=True)


def solution(mesh):
    in_specs = (
        P("ctx", "head"),
        P(),
        P(),
        P(None, "head"),
        P(None, "head"),
        P(None, "head"),
        P("head", None),
    )

    def per_device(tokens, block_order, block_mask, w_query, w_key, w_value, w_out):
        args = (tokens, block_order, block_mask, w_query, w_key, w_value, w_out)
        heads = w_query.shape[1] // HEAD_DIM
        fits = mesh.shape["ctx"] == Z * X * C and mesh.shape["head"] == 2 and heads % Z == 0
        return split_heads(*args) if fits else gather_all(*args)

    return jax.shard_map(
        per_device, mesh=mesh, in_specs=in_specs, out_specs=P("ctx", "head"), check_vma=False
    )
```

```python
import functools
import math

import jax
import jax.numpy as jnp
from jax import lax
from jax.experimental import pallas as pl
from jax.experimental.pallas import tpu as pltpu
from jax.sharding import PartitionSpec as P

HEAD_DIM = 128
BLOCK = 128
Z, X, C = 4, 2, 2
MIB = 1 << 20
BF16, F32 = jnp.bfloat16, jnp.float32
LIGHT = pl.CostEstimate(flops=1024, bytes_accessed=1024, transcendentals=0)
SOME = pl.CostEstimate(flops=1024, bytes_accessed=1 << 20, transcendentals=0)


def place(z, x, c):
    return (z * X + x) * C + c


def hop(dz, dx, dc):
    return [
        (place(z, x, c), place(z ^ dz, x ^ dx, c ^ dc))
        for z in range(Z)
        for x in range(X)
        for c in range(C)
    ]


def params(mib):
    return pltpu.CompilerParams(vmem_limit_bytes=mib * MIB)


def after(value, *others):
    return lax.optimization_barrier((value, *others))[0]


def whole(count):
    return [pl.BlockSpec(memory_space=pltpu.VMEM)] * count


def fetch(where, weights, width, groups, fence, beside=None):
    depth = weights[0].shape[0]
    half = depth // 2
    kinds = len(weights)
    extra = list(beside or ())

    def body(s, *refs):
        out, sems = refs[kinds + 1 + len(extra)], refs[-1]
        copies = []
        for g in range(2):
            columns = pl.ds(pl.multiple_of((s[1] ^ groups[g]) * width, width), width)
            for k in range(kinds):
                for part in range(2):
                    rows = pl.ds(pl.multiple_of((s[0] ^ part) * half, half), half)
                    copies.append(
                        pltpu.make_async_copy(
                            refs[k].at[rows, columns],
                            out.at[g * kinds + k, pl.ds(part * half, half)],
                            sems.at[len(copies)],
                        )
                    )
        for copy in copies:
            copy.start()
        if extra:
            tokens_ref, held_ref = refs[kinds + 1 : kinds + 3]
            for i in range(2 * kinds):
                refs[-2][i] = jnp.dot(
                    tokens_ref[...], held_ref[i, :half], preferred_element_type=F32
                )
        for copy in copies:
            copy.wait()

    out_shape = [pltpu.VMEM((2 * kinds, depth, width), BF16)]
    if extra:
        out_shape.append(pltpu.VMEM((2 * kinds, extra[0].shape[0], width), F32))
    return pl.pallas_call(
        body,
        grid_spec=pltpu.PrefetchScalarGridSpec(
            num_scalar_prefetch=1,
            grid=(),
            in_specs=[pl.BlockSpec(memory_space=pl.ANY)] * (kinds + 1) + whole(len(extra)),
            out_specs=whole(len(out_shape)),
            scratch_shapes=[pltpu.SemaphoreType.DMA((4 * kinds,))],
        ),
        out_shape=out_shape,
        compiler_params=params(4),
        cost_estimate=LIGHT,
    )(where, *weights, fence, *extra)


def project(own, other, held, outputs, start=0, partial=None):
    rows = own.shape[0] - start
    kinds = held.shape[0] // 2
    flat = [block for blocks in outputs for block in blocks]

    def body(*refs):
        held_ref, outs = refs[2], refs[3:]
        tokens, low = jnp.concatenate([refs[0][start:], refs[1][start:]], axis=1), 0
        if partial is not None:
            tokens, low, outs = refs[1][start:], own.shape[1], refs[4:]
        at = [(o, i) for o, blocks in enumerate(outputs) for i in range(len(blocks))]
        for first in range(0, len(flat), 2):
            pair = flat[first : first + 2]
            weight = [
                held_ref[g * kinds + k, low:, h * HEAD_DIM : (h + 1) * HEAD_DIM] for g, k, h in pair
            ]
            total = jnp.dot(
                tokens, jnp.concatenate(weight, axis=1), preferred_element_type=F32
            )
            if partial is not None:
                done = [
                    refs[3][g * kinds + k, :, h * HEAD_DIM : (h + 1) * HEAD_DIM] for g, k, h in pair
                ]
                total = total + jnp.concatenate(done, axis=1)
            total = total.astype(BF16)
            for i in range(len(pair)):
                o, place_in = at[first + i]
                outs[o][place_in] = total[:, i * HEAD_DIM : (i + 1) * HEAD_DIM]

    more = [] if partial is None else [partial]
    return pl.pallas_call(
        body,
        in_specs=whole(3 + len(more)),
        out_specs=whole(len(outputs)),
        out_shape=[jax.ShapeDtypeStruct((len(b), rows, HEAD_DIM), BF16) for b in outputs],
        compiler_params=params(8),
        cost_estimate=LIGHT,
    )(own, other, held, *more)


def take(array, ranges):
    def body(in_ref, *outs):
        for out, (first, last) in zip(outs, ranges):
            out[...] = in_ref[first:last]

    return pl.pallas_call(
        body,
        in_specs=whole(1),
        out_specs=whole(len(ranges)),
        out_shape=[
            jax.ShapeDtypeStruct((last - first,) + array.shape[1:], array.dtype)
            for first, last in ranges
        ],
        compiler_params=params(4),
        cost_estimate=LIGHT,
    )(array)


def pack(sides, picks):
    arrays = [a for side in sides for half in side for a in half]
    rows = sum(half[0].shape[1] for half in sides[0])

    def body(*refs):
        ins, outs = list(refs[: len(arrays)]), refs[len(arrays) :]
        blocks = []
        for side in sides:
            for half in side:
                blocks.append([])
                for a in half:
                    ref = ins.pop(0)
                    blocks[-1] += [(ref, b) for b in range(a.shape[0])]
        for out, wanted in zip(outs, picks):
            for n, (side, upper, lower) in enumerate(wanted):
                ref, b = blocks[2 * side][upper]
                size = ref.shape[1]
                out[n, :size] = ref[b]
                ref, b = blocks[2 * side + 1][lower]
                out[n, size:] = ref[b]

    return pl.pallas_call(
        body,
        in_specs=whole(len(arrays)),
        out_specs=whole(len(picks)),
        out_shape=[jax.ShapeDtypeStruct((len(p), rows, HEAD_DIM), BF16) for p in picks],
        compiler_params=params(4),
        cost_estimate=LIGHT,
    )(*arrays)


def mask_rows(where, block_order, block_mask, rows):
    blocks = block_order.shape[0]
    per = rows // BLOCK
    keys = blocks * BLOCK

    def body(s, order_ref, mask_ref, out_ref):
        def ids(shape, axis, shift):
            at = lax.broadcasted_iota(jnp.int32, shape, axis) >> shift
            piece = at >> (per.bit_length() - 1)
            return at & (per - 1), piece

        hot = (order_ref[...] == lax.broadcasted_iota(jnp.int32, (blocks, blocks), 0)).astype(F32)
        low, piece = ids((Z * per, blocks), 0, 0)
        want = (place(s[1] ^ piece, s[2], s[3])) * per + low
        query = (want == lax.broadcasted_iota(jnp.int32, (Z * per, blocks), 1)).astype(F32)
        low, piece = ids((blocks, keys), 1, BLOCK.bit_length() - 1)
        want = place(s[1] ^ (piece >> 2), s[2] ^ (piece & 1), s[3] ^ ((piece >> 1) & 1)) * per + low
        key = (want == lax.broadcasted_iota(jnp.int32, (blocks, keys), 0)).astype(F32)
        frames = lax.dot_general(query, hot, (((1,), (1,)), ((), ())), preferred_element_type=F32)
        live = jnp.dot(frames, mask_ref[...].astype(F32), preferred_element_type=F32)
        live = jnp.dot(live, hot, preferred_element_type=F32)
        live = jnp.dot(live, key, preferred_element_type=F32)
        out_ref[...] = jnp.where(live > 0.5, 0.0, -1e30)

    return pl.pallas_call(
        body,
        grid_spec=pltpu.PrefetchScalarGridSpec(
            num_scalar_prefetch=1, grid=(), in_specs=whole(2), out_specs=whole(1)[0]
        ),
        out_shape=jax.ShapeDtypeStruct((Z * per, keys), F32),
        compiler_params=params(8),
        cost_estimate=LIGHT,
    )(where, block_order[None, :], block_mask)


def attend(steps, parts, stride, bias, mask_at, mask_stride, key_at, outputs, earlier, fences):
    tile = parts[0][0].shape[1]
    n, count = len(parts), len(steps)
    scale = math.log2(math.e) / math.sqrt(HEAD_DIM)
    every = sum(q[3] for q in steps[0][0])
    width = n * tile
    carried = bool(steps[0][1])
    arrays = []

    def index_of(array):
        for i, known in enumerate(arrays):
            if known is array:
                return i
        arrays.append(array)
        return len(arrays) - 1

    plan = [
        (
            [(index_of(q), *rest) for q, *rest in queries],
            [([index_of(a) for a in held], *rest) for held, *rest in states],
            results,
        )
        for queries, states, results in steps
    ]
    part_plan = [(index_of(p[0]), p[1], index_of(p[2]), p[3]) for p in parts]
    earlier_plan = [(index_of(a), low, out) for a, low, out in earlier]
    bias_index = index_of(bias)
    total_arrays = len(arrays)

    def body(*refs):
        ins = refs[:total_arrays]
        outs = refs[total_arrays + len(fences) :]
        q_ref = outs[-1 - (3 if carried else 0)]
        held_refs = outs[len(outs) - 3 :]
        step = pl.program_id(0)
        for i, (queries, states, _) in enumerate(plan):

            @pl.when(step == i)
            def _(i=i, queries=queries, states=states):
                at = 0
                for q, block, low, size in queries:
                    q_ref[at : at + size] = ins[q][block, low : low + size]
                    at += size
                at = 0
                for held, block, low, size in states:
                    for k in range(3):
                        held_refs[k][at : at + size] = ins[held[k]][block, low : low + size]
                    at += size
                if i == 0:
                    for a, low, out in earlier_plan:
                        outs[out][:, :HEAD_DIM] = ins[a][low : low + outs[out].shape[0]]

        shift = step * stride
        key = jnp.concatenate([ins[k][at + shift] for k, at, _, _ in part_plan], axis=0)
        value = jnp.concatenate([ins[v][at + shift] for _, _, v, at in part_plan], axis=0)
        if carried:
            top, total, accum = held_refs[0][:, :1], held_refs[1][...], held_refs[2][...]
        else:
            top = jnp.full((every, 1), -1e30, F32)
            total = jnp.zeros((every, HEAD_DIM), F32)
            accum = jnp.zeros((every, HEAD_DIM), F32)
        score = lax.dot_general(
            q_ref[...], key, (((1,), (1,)), ((), ())), preferred_element_type=F32
        )
        columns = slice(key_at * tile, key_at * tile + width)
        keep = [
            jnp.broadcast_to(
                ins[bias_index][pl.ds(row + step * mask_stride, 1), columns], (BLOCK, width)
            )
            for row in mask_at
        ]
        score = score + jnp.concatenate(keep, axis=0)
        best = score[:, :HEAD_DIM]
        for u in range(HEAD_DIM, width, HEAD_DIM):
            best = jnp.maximum(best, score[:, u : u + HEAD_DIM])
        top_next = jnp.maximum(top, jnp.max(best, axis=1, keepdims=True))
        factor = jnp.exp2((top - top_next) * scale)
        weight = jnp.exp2((score - top_next) * scale)
        add = weight[:, :HEAD_DIM]
        for u in range(HEAD_DIM, width, HEAD_DIM):
            add = add + weight[:, u : u + HEAD_DIM]
        total = total * factor + add
        accum = accum * factor + jnp.dot(weight.astype(BF16), value, preferred_element_type=F32)
        if outputs is None:
            outs[0][step] = jnp.broadcast_to(top_next, (every, HEAD_DIM))
            outs[1][step] = total
            outs[2][step] = accum
            return
        result = (accum / jnp.sum(total, axis=1, keepdims=True)).astype(BF16)
        for i, (queries, _, results) in enumerate(plan):

            @pl.when(step == i)
            def _(queries=queries, results=results):
                at = 0
                for (_, _, _, size), (out, head) in zip(queries, results):
                    lanes = slice(head * HEAD_DIM, (head + 1) * HEAD_DIM)
                    outs[out][:, lanes] = result[at : at + size]
                    at += size

    if outputs is None:
        out_shape = [jax.ShapeDtypeStruct((count, every, HEAD_DIM), F32)] * 3
    else:
        out_shape = [jax.ShapeDtypeStruct(shape, BF16) for shape in outputs]
    return pl.pallas_call(
        body,
        grid=(count,),
        in_specs=whole(total_arrays) + [pl.BlockSpec(memory_space=pl.ANY)] * len(fences),
        out_specs=whole(len(out_shape)),
        out_shape=out_shape,
        scratch_shapes=[pltpu.VMEM((every, HEAD_DIM), BF16)]
        + [pltpu.VMEM((every, HEAD_DIM), F32)] * (3 if carried else 0),
        compiler_params=params(24),
        cost_estimate=LIGHT,
    )(*arrays, *fences)


def fetch_out(where, w_out, fence):
    depth, width = w_out.shape
    group, half = depth // Z, width // 2

    def body(s, w_ref, fence_ref, out, sems):
        copies = []
        for dz in range(Z):
            rows = pl.ds(pl.multiple_of((s[1] ^ dz) * group, group), group)
            for part in range(2):
                columns = pl.ds(pl.multiple_of((1 - s[0] if part == 0 else s[0]) * half, half), half)
                copies.append(
                    pltpu.make_async_copy(
                        w_ref.at[rows, columns],
                        out.at[pl.ds(dz * group, group), pl.ds(part * half, half)],
                        sems.at[len(copies)],
                    )
                )
        for copy in copies:
            copy.start()
        for copy in copies:
            copy.wait()

    return pl.pallas_call(
        body,
        grid_spec=pltpu.PrefetchScalarGridSpec(
            num_scalar_prefetch=1,
            grid=(),
            in_specs=[pl.BlockSpec(memory_space=pl.ANY)] * 2,
            out_specs=whole(1)[0],
            scratch_shapes=[pltpu.SemaphoreType.DMA((2 * Z,))],
        ),
        out_shape=pltpu.VMEM((depth, width), BF16),
        compiler_params=params(4),
        cost_estimate=LIGHT,
    )(where, w_out, fence)


def mix(attended, held, part):
    rows = attended[0].shape[0]
    half = held.shape[1] // 2
    count = len(attended)
    step = half // 3

    def body(*refs):
        rows_all = jnp.concatenate([r[...] for r in refs[:count]], axis=1)
        for i in range(3):
            weight = refs[count][:, part * half + i * step : part * half + (i + 1) * step]
            refs[-1][:, i * step : (i + 1) * step] = jnp.dot(
                rows_all, weight, preferred_element_type=F32
            ).astype(BF16)

    return pl.pallas_call(
        body,
        in_specs=whole(count + 1),
        out_specs=whole(1)[0],
        out_shape=jax.ShapeDtypeStruct((rows, half), BF16),
        compiler_params=params(16),
        cost_estimate=LIGHT,
    )(*attended, held)


def finish(home, arrived, above, cost):
    rows, width = home.shape
    first = 0 if above is None else above.shape[0]

    def body(*refs):
        total = refs[0][...].astype(F32) + refs[1][...].astype(F32)
        if above is not None:
            refs[-1][:first] = refs[2][...]
        refs[-1][first:] = total.astype(BF16)

    more = [] if above is None else [above]
    return pl.pallas_call(
        body,
        in_specs=whole(2 + len(more)),
        out_specs=whole(1)[0],
        out_shape=jax.ShapeDtypeStruct((first + rows, width), BF16),
        compiler_params=params(8),
        cost_estimate=cost,
    )(home, arrived, *more)


def split_heads(tokens, block_order, block_mask, w_query, w_key, w_value, w_out):
    rows, half = tokens.shape
    group_heads = w_query.shape[1] // HEAD_DIM // Z
    per = rows // BLOCK
    cut = rows * 9 // 16
    ctx = lax.axis_index("ctx")
    y = lax.axis_index("head")
    where = jnp.stack([y, ctx // (X * C), (ctx // C) % X, ctx % C]).astype(jnp.int32)
    weights = [pltpu.with_memory_space_constraint(w, pltpu.HBM) for w in (w_query, w_key, w_value)]
    w_out = pltpu.with_memory_space_constraint(w_out, pltpu.HBM)
    heads = range(group_heads)
    span = group_heads * HEAD_DIM

    def over_y(a):
        return lax.ppermute(a, "head", [(0, 1), (1, 0)])

    def over(a, dz, dx, dc):
        return lax.ppermute(a, "ctx", hop(dz, dx, dc))

    def pairs(group, wanted):
        return [(group, kind, h) for kind in (1, 2) for h in wanted]

    def singles(group):
        return [(group, 0, h) for h in heads]

    other = over_y(tokens)
    far = over(tokens[:cut], 2, 0, 0)
    (held,) = fetch(where, weights, span, (0, 1), where)
    held_far, partial = fetch(where, weights, span, (2, 3), where, (tokens, held))

    other = after(other, held_far)
    own_kv, sent = project(
        tokens,
        other,
        held,
        [pairs(0, heads), singles(1) + pairs(1, heads)],
        partial=partial,
    )
    came = over(sent, 1, 0, 0)
    own_across = over(own_kv, 0, 1, 0)
    own_core = over(own_kv, 0, 0, 1)
    far = after(far, sent)
    far_other = over_y(far)
    low2, low3 = project(
        after(tokens, far),
        other,
        held_far,
        [singles(0) + pairs(0, heads), singles(1) + pairs(1, heads)],
        cut,
    )
    (own_q,) = project(
        after(tokens, own_core, low2), other, held, [singles(0)], partial=partial
    )
    low2 = over(low2, 2, 0, 0)
    low3 = over(low3, 3, 0, 0)
    bias = mask_rows(after(where, own_q), block_order, block_mask, rows)
    out_held = fetch_out(where, w_out, bias)
    own_across = after(own_across, out_held)
    own_across_core = over(own_across, 0, 0, 1)

    far_sent_q, far_sent, far_kept = project(
        far,
        after(far_other, out_held),
        held,
        [singles(1), pairs(1, heads), singles(0) + pairs(0, heads)],
    )
    far_came_q = over(far_sent_q, 1, 0, 0)
    far_came = over(far_sent, 1, 0, 0)
    came = after(came, far_sent, own_across)
    n = group_heads
    came_kv, came_k, came_v = take(came, [(n, 3 * n), (n, 2 * n), (2 * n, 3 * n)])
    across_k = over(came_k, 0, 1, 0)
    across_v = over(came_v, 0, 1, 0)
    came_core = over(came_kv, 0, 0, 1)
    far_came = after(far_came, low2, low3)
    across_k, across_v = after(across_k, far_came), after(across_v, far_came)
    across_core_k = over(across_k, 0, 0, 1)
    across_core_v = over(across_v, 0, 0, 1)

    first, rest = (0,), tuple(heads)[1:]
    sides = [[[far_kept], [low2]], [[far_came], [low3]]]

    def picks(chunk):
        kept = [(0, k * n + h, k * n + h) for k in (1, 2) for h in chunk]
        return kept + [(1, (k - 1) * n + h, k * n + h) for k in (1, 2) for h in chunk]

    far_first, far_rest, far_q = pack(
        sides, [picks(first), picks(rest), [(0, h, h) for h in heads]]
    )
    first_across = over(far_first, 0, 1, 0)
    first_core = over(far_first, 0, 0, 1)
    rest_across = over(far_rest, 0, 1, 0)
    rest_core = over(far_rest, 0, 0, 1)

    near = [(a, 0, a, n) for a in (own_kv, own_across, own_core, own_across_core)]
    near += [
        (came_kv, 0, came_kv, n),
        (across_k, 0, across_v, 0),
        (came_core, 0, came_core, n),
        (across_core_k, 0, across_core_v, 0),
    ]

    def whole_rows(arrays, j):
        return [(a, j, 0, rows) for a in arrays]

    state_near = attend(
        [(whole_rows([own_q, came], j), [], []) for j in heads],
        near,
        1,
        bias,
        range(2 * per),
        0,
        0,
        None,
        [],
        [far_first],
    )
    (far_came_q,) = pack(
        [[[after(far_came_q, state_near[0])], [low3]]], [[(0, h, h) for h in heads]]
    )
    state_far = attend(
        [(whole_rows([far_q, far_came_q], j), [], []) for j in heads],
        near,
        1,
        bias,
        range(2 * per, 4 * per),
        0,
        0,
        None,
        [],
        [state_near[0]],
    )
    first_across = after(first_across, state_far[0])
    first_across_core = over(first_across, 0, 0, 1)

    def far_parts(arrays, size):
        return [(a, 2 * i * size, a, (2 * i + 1) * size) for i in range(2) for a in arrays]

    first_rows = attend(
        [
            (whole_rows([own_q, came], 0), [(state_near, 0, 0, 2 * rows)], [(0, 0), (1, 0)]),
            (whole_rows([far_q, far_came_q], 0), [(state_far, 0, 0, 2 * rows)], [(2, 0), (3, 0)]),
        ],
        far_parts([far_first, first_across, first_core, first_across_core], 1),
        0,
        bias,
        range(2 * per),
        2 * per,
        len(near),
        [(rows, HEAD_DIM)] * Z,
        [],
        [],
    )
    rest_across = after(rest_across, first_rows[0])
    rest_across_core = over(rest_across, 0, 0, 1)
    rest_parts = far_parts([far_rest, rest_across, rest_core, rest_across_core], len(rest))
    homes, arrived, fences = [], [], []
    for low in range(0, rows, BLOCK):
        steps = [
            (
                [(a, j, low, BLOCK) for a in (own_q, came, far_q, far_came_q)],
                [(s, j, i * rows + low, BLOCK) for s in (state_near, state_far) for i in range(2)],
                [(i, j) for i in range(Z)],
            )
            for j in rest
        ]
        done = attend(
            steps,
            rest_parts,
            1,
            bias,
            [i * per + low // BLOCK for i in range(Z)],
            0,
            len(near),
            [(BLOCK, span)] * Z,
            [(first_rows[i], low, i) for i in range(Z)],
            fences,
        )
        fences = [done[0]]
        back = [done[0]] + [over(done[dz], dz, 0, 0) for dz in range(1, Z)]
        if arrived:
            back[-1] = after(back[-1], homes[0])
        away = mix(back, out_held, 0)
        arrived.append(over_y(away))
        homes.append(mix(back[:-1] + [after(back[-1], away)], out_held, 1))
    upper = finish(homes[0], arrived[0], None, SOME)
    return finish(homes[1], after(arrived[1], upper), upper, LIGHT)


def gather_all(tokens, block_order, block_mask, w_query, w_key, w_value, w_out):
    row_count = tokens.shape[0]
    local_width = w_query.shape[1]
    local_heads = local_width // HEAD_DIM
    block_count = block_order.shape[0]
    portion = lax.all_gather(tokens, "head", axis=1, tiled=True)
    query_rows, key_rows, value_rows = [
        jnp.dot(portion, weight, preferred_element_type=F32)
        .astype(BF16)
        .reshape(row_count, local_heads, HEAD_DIM)
        for weight in (w_query, w_key, w_value)
    ]
    cycle_live = block_mask[block_order][:, block_order]
    row_blocks = (
        lax.axis_index("ctx") * row_count + jnp.arange(row_count, dtype=jnp.int32)
    ) // BLOCK
    live_columns = cycle_live[row_blocks].T
    inv_root = 1.0 / HEAD_DIM**0.5

    def advance(state, inputs):
        key_tile, value_tile, offset = inputs
        keep = lax.dynamic_index_in_dim(live_columns, offset, 0, keepdims=False) > 0
        top_now, total_now, accum = state
        scores = (
            jnp.einsum("qhd,khd->hqk", query_rows, key_tile, preferred_element_type=F32)
            * inv_root
        )
        allowed = keep[None, :, None]
        top_next = jnp.maximum(top_now, jnp.max(jnp.where(allowed, scores, -1e30), axis=-1))
        factor = jnp.exp(top_now - top_next)
        weights = jnp.where(allowed, jnp.exp(scores - top_next[..., None]), 0.0)
        total_next = total_now * factor + jnp.sum(weights, axis=-1)
        accum = accum * factor[..., None] + jnp.einsum(
            "hqk,khd->hqd", weights.astype(BF16), value_tile, preferred_element_type=F32
        )
        return (top_next, total_next, accum), None

    initial = (
        jnp.full((local_heads, row_count), -1e30, F32),
        jnp.zeros((local_heads, row_count), F32),
        jnp.zeros((local_heads, row_count, HEAD_DIM), F32),
    )
    tiles = [
        lax.all_gather(part, "ctx", axis=0, tiled=True).reshape(
            block_count, BLOCK, local_heads, HEAD_DIM
        )
        for part in (key_rows, value_rows)
    ]
    (_, total, accum), _ = lax.scan(
        advance, initial, (*tiles, jnp.arange(block_count, dtype=jnp.int32))
    )
    attended = (
        (accum / total[..., None]).transpose(1, 0, 2).reshape(row_count, local_width).astype(BF16)
    )
    partial_out = jnp.dot(attended, w_out, preferred_element_type=F32)
    return lax.psum_scatter(partial_out.astype(BF16), "head", scatter_dimension=1, tiled=True)


def solution(mesh):
    in_specs = (
        P("ctx", "head"),
        P(),
        P(),
        P(None, "head"),
        P(None, "head"),
        P(None, "head"),
        P("head", None),
    )

    def per_device(tokens, block_order, block_mask, w_query, w_key, w_value, w_out):
        args = (tokens, block_order, block_mask, w_query, w_key, w_value, w_out)
        heads = w_query.shape[1] // HEAD_DIM
        fits = mesh.shape["ctx"] == Z * X * C and mesh.shape["head"] == 2 and heads % Z == 0
        return split_heads(*args) if fits else gather_all(*args)

    return jax.shard_map(
        per_device, mesh=mesh, in_specs=in_specs, out_specs=P("ctx", "head"), check_vma=False
    )
```

```python
import functools
import math

import jax
import jax.numpy as jnp
from jax import lax
from jax.experimental import pallas as pl
from jax.experimental.pallas import tpu as pltpu
from jax.sharding import PartitionSpec as P

HEAD_DIM = 128
BLOCK = 128
Z, X, C = 4, 2, 2
RETURN_ORDER = (0, 3, 2, 1)
MIB = 1 << 20
BF16, F32 = jnp.bfloat16, jnp.float32
LIGHT = pl.CostEstimate(flops=1024, bytes_accessed=1024, transcendentals=0)
SOME = pl.CostEstimate(flops=1024, bytes_accessed=1 << 20, transcendentals=0)


def place(z, x, c):
    return (z * X + x) * C + c


def hop(dz, dx, dc):
    return [
        (place(z, x, c), place(z ^ dz, x ^ dx, c ^ dc))
        for z in range(Z)
        for x in range(X)
        for c in range(C)
    ]


def params(mib):
    return pltpu.CompilerParams(vmem_limit_bytes=mib * MIB)


def after(value, *others):
    return lax.optimization_barrier((value, *others))[0]


def whole(count):
    return [pl.BlockSpec(memory_space=pltpu.VMEM)] * count


def fetch(where, weights, width, groups, fence, beside=None):
    depth = weights[0].shape[0]
    half = depth // 2
    kinds = len(weights)
    extra = list(beside or ())

    def body(s, *refs):
        out, sems = refs[kinds + 1 + len(extra)], refs[-1]
        copies = []
        for g in range(2):
            columns = pl.ds(pl.multiple_of((s[1] ^ groups[g]) * width, width), width)
            for k in range(kinds):
                for part in range(2):
                    rows = pl.ds(pl.multiple_of((s[0] ^ part) * half, half), half)
                    copies.append(
                        pltpu.make_async_copy(
                            refs[k].at[rows, columns],
                            out.at[g * kinds + k, pl.ds(part * half, half)],
                            sems.at[len(copies)],
                        )
                    )
        for copy in copies:
            copy.start()
        if extra:
            tokens_ref, held_ref = refs[kinds + 1 : kinds + 3]
            for i in range(2 * kinds):
                refs[-2][i] = jnp.dot(
                    tokens_ref[...], held_ref[i, :half], preferred_element_type=F32
                )
        for copy in copies:
            copy.wait()

    out_shape = [pltpu.VMEM((2 * kinds, depth, width), BF16)]
    if extra:
        out_shape.append(pltpu.VMEM((2 * kinds, extra[0].shape[0], width), F32))
    return pl.pallas_call(
        body,
        grid_spec=pltpu.PrefetchScalarGridSpec(
            num_scalar_prefetch=1,
            grid=(),
            in_specs=[pl.BlockSpec(memory_space=pl.ANY)] * (kinds + 1) + whole(len(extra)),
            out_specs=whole(len(out_shape)),
            scratch_shapes=[pltpu.SemaphoreType.DMA((4 * kinds,))],
        ),
        out_shape=out_shape,
        compiler_params=params(4),
        cost_estimate=LIGHT,
    )(where, *weights, fence, *extra)


def project(own, other, held, outputs, start=0, partial=None):
    rows = own.shape[0] - start
    kinds = held.shape[0] // 2
    flat = [block for blocks in outputs for block in blocks]

    def body(*refs):
        held_ref, outs = refs[2], refs[3:]
        tokens, low = jnp.concatenate([refs[0][start:], refs[1][start:]], axis=1), 0
        if partial is not None:
            tokens, low, outs = refs[1][start:], own.shape[1], refs[4:]
        at = [(o, i) for o, blocks in enumerate(outputs) for i in range(len(blocks))]
        for first in range(0, len(flat), 2):
            pair = flat[first : first + 2]
            weight = [
                held_ref[g * kinds + k, low:, h * HEAD_DIM : (h + 1) * HEAD_DIM] for g, k, h in pair
            ]
            total = jnp.dot(
                tokens, jnp.concatenate(weight, axis=1), preferred_element_type=F32
            )
            if partial is not None:
                done = [
                    refs[3][g * kinds + k, :, h * HEAD_DIM : (h + 1) * HEAD_DIM] for g, k, h in pair
                ]
                total = total + jnp.concatenate(done, axis=1)
            total = total.astype(BF16)
            for i in range(len(pair)):
                o, place_in = at[first + i]
                outs[o][place_in] = total[:, i * HEAD_DIM : (i + 1) * HEAD_DIM]

    more = [] if partial is None else [partial]
    return pl.pallas_call(
        body,
        in_specs=whole(3 + len(more)),
        out_specs=whole(len(outputs)),
        out_shape=[jax.ShapeDtypeStruct((len(b), rows, HEAD_DIM), BF16) for b in outputs],
        compiler_params=params(8),
        cost_estimate=LIGHT,
    )(own, other, held, *more)


def take(array, ranges):
    def body(in_ref, *outs):
        for out, (first, last) in zip(outs, ranges):
            out[...] = in_ref[first:last]

    return pl.pallas_call(
        body,
        in_specs=whole(1),
        out_specs=whole(len(ranges)),
        out_shape=[
            jax.ShapeDtypeStruct((last - first,) + array.shape[1:], array.dtype)
            for first, last in ranges
        ],
        compiler_params=params(4),
        cost_estimate=LIGHT,
    )(array)


def pack(sides, picks):
    arrays = [a for side in sides for half in side for a in half]
    rows = sum(half[0].shape[1] for half in sides[0])

    def body(*refs):
        ins, outs = list(refs[: len(arrays)]), refs[len(arrays) :]
        blocks = []
        for side in sides:
            for half in side:
                blocks.append([])
                for a in half:
                    ref = ins.pop(0)
                    blocks[-1] += [(ref, b) for b in range(a.shape[0])]
        for out, wanted in zip(outs, picks):
            for n, (side, upper, lower) in enumerate(wanted):
                ref, b = blocks[2 * side][upper]
                size = ref.shape[1]
                out[n, :size] = ref[b]
                ref, b = blocks[2 * side + 1][lower]
                out[n, size:] = ref[b]

    return pl.pallas_call(
        body,
        in_specs=whole(len(arrays)),
        out_specs=whole(len(picks)),
        out_shape=[jax.ShapeDtypeStruct((len(p), rows, HEAD_DIM), BF16) for p in picks],
        compiler_params=params(4),
        cost_estimate=LIGHT,
    )(*arrays)


def mask_rows(where, block_order, block_mask, rows):
    blocks = block_order.shape[0]
    per = rows // BLOCK
    keys = blocks * BLOCK

    def body(s, order_ref, mask_ref, out_ref):
        def ids(shape, axis, shift):
            at = lax.broadcasted_iota(jnp.int32, shape, axis) >> shift
            piece = at >> (per.bit_length() - 1)
            return at & (per - 1), piece

        hot = (order_ref[...] == lax.broadcasted_iota(jnp.int32, (blocks, blocks), 0)).astype(F32)
        low, piece = ids((Z * per, blocks), 0, 0)
        want = (place(s[1] ^ piece, s[2], s[3])) * per + low
        query = (want == lax.broadcasted_iota(jnp.int32, (Z * per, blocks), 1)).astype(F32)
        low, piece = ids((blocks, keys), 1, BLOCK.bit_length() - 1)
        want = place(s[1] ^ (piece >> 2), s[2] ^ (piece & 1), s[3] ^ ((piece >> 1) & 1)) * per + low
        key = (want == lax.broadcasted_iota(jnp.int32, (blocks, keys), 0)).astype(F32)
        frames = lax.dot_general(query, hot, (((1,), (1,)), ((), ())), preferred_element_type=F32)
        live = jnp.dot(frames, mask_ref[...].astype(F32), preferred_element_type=F32)
        live = jnp.dot(live, hot, preferred_element_type=F32)
        live = jnp.dot(live, key, preferred_element_type=F32)
        out_ref[...] = jnp.where(live > 0.5, 0.0, -1e30)

    return pl.pallas_call(
        body,
        grid_spec=pltpu.PrefetchScalarGridSpec(
            num_scalar_prefetch=1, grid=(), in_specs=whole(2), out_specs=whole(1)[0]
        ),
        out_shape=jax.ShapeDtypeStruct((Z * per, keys), F32),
        compiler_params=params(8),
        cost_estimate=LIGHT,
    )(where, block_order[None, :], block_mask)


def attend(steps, parts, stride, bias, mask_at, mask_stride, key_at, outputs, earlier, fences):
    tile = parts[0][0].shape[1]
    n, count = len(parts), len(steps)
    scale = math.log2(math.e) / math.sqrt(HEAD_DIM)
    every = sum(q[3] for q in steps[0][0])
    width = n * tile
    carried = bool(steps[0][1])
    arrays = []

    def index_of(array):
        for i, known in enumerate(arrays):
            if known is array:
                return i
        arrays.append(array)
        return len(arrays) - 1

    plan = [
        (
            [(index_of(q), *rest) for q, *rest in queries],
            [([index_of(a) for a in held], *rest) for held, *rest in states],
            results,
        )
        for queries, states, results in steps
    ]
    part_plan = [(index_of(p[0]), p[1], index_of(p[2]), p[3]) for p in parts]
    earlier_plan = [(index_of(a), low, out) for a, low, out in earlier]
    bias_index = index_of(bias)
    total_arrays = len(arrays)

    def body(*refs):
        ins = refs[:total_arrays]
        outs = refs[total_arrays + len(fences) :]
        q_ref = outs[-1 - (3 if carried else 0)]
        held_refs = outs[len(outs) - 3 :]
        step = pl.program_id(0)
        for i, (queries, states, _) in enumerate(plan):

            @pl.when(step == i)
            def _(i=i, queries=queries, states=states):
                at = 0
                for q, block, low, size in queries:
                    q_ref[at : at + size] = ins[q][block, low : low + size]
                    at += size
                at = 0
                for held, block, low, size in states:
                    for k in range(3):
                        held_refs[k][at : at + size] = ins[held[k]][block, low : low + size]
                    at += size
                if i == 0:
                    for a, low, out in earlier_plan:
                        outs[out][:, :HEAD_DIM] = ins[a][low : low + outs[out].shape[0]]

        shift = step * stride
        key = jnp.concatenate([ins[k][at + shift] for k, at, _, _ in part_plan], axis=0)
        value = jnp.concatenate([ins[v][at + shift] for _, _, v, at in part_plan], axis=0)
        if carried:
            top, total, accum = held_refs[0][:, :1], held_refs[1][...], held_refs[2][...]
        else:
            top = jnp.full((every, 1), -1e30, F32)
            total = jnp.zeros((every, HEAD_DIM), F32)
            accum = jnp.zeros((every, HEAD_DIM), F32)
        score = lax.dot_general(
            q_ref[...], key, (((1,), (1,)), ((), ())), preferred_element_type=F32
        )
        columns = slice(key_at * tile, key_at * tile + width)
        keep = [
            jnp.broadcast_to(
                ins[bias_index][pl.ds(row + step * mask_stride, 1), columns], (BLOCK, width)
            )
            for row in mask_at
        ]
        score = score + jnp.concatenate(keep, axis=0)
        best = score[:, :HEAD_DIM]
        for u in range(HEAD_DIM, width, HEAD_DIM):
            best = jnp.maximum(best, score[:, u : u + HEAD_DIM])
        top_next = jnp.maximum(top, jnp.max(best, axis=1, keepdims=True))
        factor = jnp.exp2((top - top_next) * scale)
        weight = jnp.exp2((score - top_next) * scale)
        add = weight[:, :HEAD_DIM]
        for u in range(HEAD_DIM, width, HEAD_DIM):
            add = add + weight[:, u : u + HEAD_DIM]
        total = total * factor + add
        accum = accum * factor + jnp.dot(weight.astype(BF16), value, preferred_element_type=F32)
        if outputs is None:
            outs[0][step] = jnp.broadcast_to(top_next, (every, HEAD_DIM))
            outs[1][step] = total
            outs[2][step] = accum
            return
        result = (accum / jnp.sum(total, axis=1, keepdims=True)).astype(BF16)
        for i, (queries, _, results) in enumerate(plan):

            @pl.when(step == i)
            def _(queries=queries, results=results):
                at = 0
                for (_, _, _, size), (out, head) in zip(queries, results):
                    lanes = slice(head * HEAD_DIM, (head + 1) * HEAD_DIM)
                    outs[out][:, lanes] = result[at : at + size]
                    at += size

    if outputs is None:
        out_shape = [jax.ShapeDtypeStruct((count, every, HEAD_DIM), F32)] * 3
    else:
        out_shape = [jax.ShapeDtypeStruct(shape, BF16) for shape in outputs]
    return pl.pallas_call(
        body,
        grid=(count,),
        in_specs=whole(total_arrays) + [pl.BlockSpec(memory_space=pl.ANY)] * len(fences),
        out_specs=whole(len(out_shape)),
        out_shape=out_shape,
        scratch_shapes=[pltpu.VMEM((every, HEAD_DIM), BF16)]
        + [pltpu.VMEM((every, HEAD_DIM), F32)] * (3 if carried else 0),
        compiler_params=params(24),
        cost_estimate=LIGHT,
    )(*arrays, *fences)


def fetch_out(where, w_out, fence):
    depth, width = w_out.shape
    group, half = depth // Z, width // 2

    def body(s, w_ref, fence_ref, out, sems):
        copies = []
        for row, dz in enumerate(RETURN_ORDER):
            rows = pl.ds(pl.multiple_of((s[1] ^ dz) * group, group), group)
            for part in range(2):
                columns = pl.ds(pl.multiple_of((1 - s[0] if part == 0 else s[0]) * half, half), half)
                copies.append(
                    pltpu.make_async_copy(
                        w_ref.at[rows, columns],
                        out.at[pl.ds(row * group, group), pl.ds(part * half, half)],
                        sems.at[len(copies)],
                    )
                )
        for copy in copies:
            copy.start()
        for copy in copies:
            copy.wait()

    return pl.pallas_call(
        body,
        grid_spec=pltpu.PrefetchScalarGridSpec(
            num_scalar_prefetch=1,
            grid=(),
            in_specs=[pl.BlockSpec(memory_space=pl.ANY)] * 2,
            out_specs=whole(1)[0],
            scratch_shapes=[pltpu.SemaphoreType.DMA((2 * Z,))],
        ),
        out_shape=pltpu.VMEM((depth, width), BF16),
        compiler_params=params(4),
        cost_estimate=LIGHT,
    )(where, w_out, fence)


def mix(attended, held, part):
    rows = attended[0].shape[0]
    half = held.shape[1] // 2
    count = len(attended)
    step = half // 3

    def body(*refs):
        rows_all = jnp.concatenate([r[...] for r in refs[:count]], axis=1)
        for i in range(3):
            weight = refs[count][:, part * half + i * step : part * half + (i + 1) * step]
            refs[-1][:, i * step : (i + 1) * step] = jnp.dot(
                rows_all, weight, preferred_element_type=F32
            ).astype(BF16)

    return pl.pallas_call(
        body,
        in_specs=whole(count + 1),
        out_specs=whole(1)[0],
        out_shape=jax.ShapeDtypeStruct((rows, half), BF16),
        compiler_params=params(16),
        cost_estimate=LIGHT,
    )(*attended, held)


def finish(home, arrived, above, cost):
    rows, width = home.shape
    first = 0 if above is None else above.shape[0]

    def body(*refs):
        total = refs[0][...].astype(F32) + refs[1][...].astype(F32)
        if above is not None:
            refs[-1][:first] = refs[2][...]
        refs[-1][first:] = total.astype(BF16)

    more = [] if above is None else [above]
    return pl.pallas_call(
        body,
        in_specs=whole(2 + len(more)),
        out_specs=whole(1)[0],
        out_shape=jax.ShapeDtypeStruct((first + rows, width), BF16),
        compiler_params=params(8),
        cost_estimate=cost,
    )(home, arrived, *more)


def split_heads(tokens, block_order, block_mask, w_query, w_key, w_value, w_out):
    rows, half = tokens.shape
    group_heads = w_query.shape[1] // HEAD_DIM // Z
    per = rows // BLOCK
    cut = rows * 9 // 16
    ctx = lax.axis_index("ctx")
    y = lax.axis_index("head")
    where = jnp.stack([y, ctx // (X * C), (ctx // C) % X, ctx % C]).astype(jnp.int32)
    weights = [pltpu.with_memory_space_constraint(w, pltpu.HBM) for w in (w_query, w_key, w_value)]
    w_out = pltpu.with_memory_space_constraint(w_out, pltpu.HBM)
    heads = range(group_heads)
    span = group_heads * HEAD_DIM

    def over_y(a):
        return lax.ppermute(a, "head", [(0, 1), (1, 0)])

    def over(a, dz, dx, dc):
        return lax.ppermute(a, "ctx", hop(dz, dx, dc))

    def pairs(group, wanted):
        return [(group, kind, h) for kind in (1, 2) for h in wanted]

    def singles(group):
        return [(group, 0, h) for h in heads]

    other = over_y(tokens)
    far = over(tokens[:cut], 2, 0, 0)
    (held,) = fetch(where, weights, span, (0, 1), where)
    held_far, partial = fetch(where, weights, span, (2, 3), where, (tokens, held))

    other = after(other, held_far)
    own_kv, sent = project(
        tokens,
        other,
        held,
        [pairs(0, heads), singles(1) + pairs(1, heads)],
        partial=partial,
    )
    came = over(sent, 1, 0, 0)
    own_across = over(own_kv, 0, 1, 0)
    own_core = over(own_kv, 0, 0, 1)
    far = after(far, sent)
    far_other = over_y(far)
    low2, low3 = project(
        after(tokens, far),
        other,
        held_far,
        [singles(0) + pairs(0, heads), singles(1) + pairs(1, heads)],
        cut,
    )
    (own_q,) = project(
        after(tokens, own_core, low2), other, held, [singles(0)], partial=partial
    )
    low2 = over(low2, 2, 0, 0)
    low3 = over(low3, 3, 0, 0)
    bias = mask_rows(after(where, own_q), block_order, block_mask, rows)
    out_held = fetch_out(where, w_out, bias)
    own_across = after(own_across, out_held)
    own_across_core = over(own_across, 0, 0, 1)

    far_sent_q, far_sent, far_kept = project(
        far,
        after(far_other, out_held),
        held,
        [singles(1), pairs(1, heads), singles(0) + pairs(0, heads)],
    )
    far_came_q = over(far_sent_q, 1, 0, 0)
    far_came = over(far_sent, 1, 0, 0)
    came = after(came, far_sent, own_across)
    n = group_heads
    came_kv, came_k, came_v = take(came, [(n, 3 * n), (n, 2 * n), (2 * n, 3 * n)])
    across_k = over(came_k, 0, 1, 0)
    across_v = over(came_v, 0, 1, 0)
    came_core = over(came_kv, 0, 0, 1)
    far_came = after(far_came, low2, low3)
    across_k, across_v = after(across_k, far_came), after(across_v, far_came)
    across_core_k = over(across_k, 0, 0, 1)
    across_core_v = over(across_v, 0, 0, 1)

    first, rest = (0,), tuple(heads)[1:]
    sides = [[[far_kept], [low2]], [[far_came], [low3]]]

    def picks(chunk):
        kept = [(0, k * n + h, k * n + h) for k in (1, 2) for h in chunk]
        return kept + [(1, (k - 1) * n + h, k * n + h) for k in (1, 2) for h in chunk]

    far_first, far_rest, far_q = pack(
        sides, [picks(first), picks(rest), [(0, h, h) for h in heads]]
    )
    first_across = over(far_first, 0, 1, 0)
    first_core = over(far_first, 0, 0, 1)
    rest_across = over(far_rest, 0, 1, 0)
    rest_core = over(far_rest, 0, 0, 1)

    near = [(a, 0, a, n) for a in (own_kv, own_across, own_core, own_across_core)]
    near += [
        (came_kv, 0, came_kv, n),
        (across_k, 0, across_v, 0),
        (came_core, 0, came_core, n),
        (across_core_k, 0, across_core_v, 0),
    ]

    def whole_rows(arrays, j):
        return [(a, j, 0, rows) for a in arrays]

    state_near = attend(
        [(whole_rows([own_q, came], j), [], []) for j in heads],
        near,
        1,
        bias,
        range(2 * per),
        0,
        0,
        None,
        [],
        [far_first],
    )
    (far_came_q,) = pack(
        [[[after(far_came_q, state_near[0])], [low3]]], [[(0, h, h) for h in heads]]
    )
    state_far = attend(
        [(whole_rows([far_q, far_came_q], j), [], []) for j in heads],
        near,
        1,
        bias,
        range(2 * per, 4 * per),
        0,
        0,
        None,
        [],
        [state_near[0]],
    )
    first_across = after(first_across, state_far[0])
    first_across_core = over(first_across, 0, 0, 1)

    def far_parts(arrays, size):
        return [(a, 2 * i * size, a, (2 * i + 1) * size) for i in range(2) for a in arrays]

    first_rows = attend(
        [
            (whole_rows([own_q, came], 0), [(state_near, 0, 0, 2 * rows)], [(0, 0), (1, 0)]),
            (whole_rows([far_q, far_came_q], 0), [(state_far, 0, 0, 2 * rows)], [(2, 0), (3, 0)]),
        ],
        far_parts([far_first, first_across, first_core, first_across_core], 1),
        0,
        bias,
        range(2 * per),
        2 * per,
        len(near),
        [(rows, HEAD_DIM)] * Z,
        [],
        [],
    )
    rest_across = after(rest_across, first_rows[0])
    rest_across_core = over(rest_across, 0, 0, 1)
    rest_parts = far_parts([far_rest, rest_across, rest_core, rest_across_core], len(rest))
    homes, arrived, fences = [], [], []
    for low in range(0, rows, BLOCK):
        steps = [
            (
                [(a, j, low, BLOCK) for a in (own_q, came, far_q, far_came_q)],
                [(s, j, i * rows + low, BLOCK) for s in (state_near, state_far) for i in range(2)],
                [(i, j) for i in range(Z)],
            )
            for j in rest
        ]
        done = attend(
            steps,
            rest_parts,
            1,
            bias,
            [i * per + low // BLOCK for i in range(Z)],
            0,
            len(near),
            [(BLOCK, span)] * Z,
            [(first_rows[i], low, i) for i in range(Z)],
            fences,
        )
        fences = [done[0]]
        back = [done[0]] + [over(done[dz], dz, 0, 0) for dz in RETURN_ORDER[1:]]
        if arrived:
            back[-1] = after(back[-1], homes[0])
        away = mix(back, out_held, 0)
        arrived.append(over_y(away))
        homes.append(mix(back[:-1] + [after(back[-1], away)], out_held, 1))
    upper = finish(homes[0], arrived[0], None, SOME)
    return finish(homes[1], after(arrived[1], upper), upper, LIGHT)


def gather_all(tokens, block_order, block_mask, w_query, w_key, w_value, w_out):
    row_count = tokens.shape[0]
    local_width = w_query.shape[1]
    local_heads = local_width // HEAD_DIM
    block_count = block_order.shape[0]
    portion = lax.all_gather(tokens, "head", axis=1, tiled=True)
    query_rows, key_rows, value_rows = [
        jnp.dot(portion, weight, preferred_element_type=F32)
        .astype(BF16)
        .reshape(row_count, local_heads, HEAD_DIM)
        for weight in (w_query, w_key, w_value)
    ]
    cycle_live = block_mask[block_order][:, block_order]
    row_blocks = (
        lax.axis_index("ctx") * row_count + jnp.arange(row_count, dtype=jnp.int32)
    ) // BLOCK
    live_columns = cycle_live[row_blocks].T
    inv_root = 1.0 / HEAD_DIM**0.5

    def advance(state, inputs):
        key_tile, value_tile, offset = inputs
        keep = lax.dynamic_index_in_dim(live_columns, offset, 0, keepdims=False) > 0
        top_now, total_now, accum = state
        scores = (
            jnp.einsum("qhd,khd->hqk", query_rows, key_tile, preferred_element_type=F32)
            * inv_root
        )
        allowed = keep[None, :, None]
        top_next = jnp.maximum(top_now, jnp.max(jnp.where(allowed, scores, -1e30), axis=-1))
        factor = jnp.exp(top_now - top_next)
        weights = jnp.where(allowed, jnp.exp(scores - top_next[..., None]), 0.0)
        total_next = total_now * factor + jnp.sum(weights, axis=-1)
        accum = accum * factor[..., None] + jnp.einsum(
            "hqk,khd->hqd", weights.astype(BF16), value_tile, preferred_element_type=F32
        )
        return (top_next, total_next, accum), None

    initial = (
        jnp.full((local_heads, row_count), -1e30, F32),
        jnp.zeros((local_heads, row_count), F32),
        jnp.zeros((local_heads, row_count, HEAD_DIM), F32),
    )
    tiles = [
        lax.all_gather(part, "ctx", axis=0, tiled=True).reshape(
            block_count, BLOCK, local_heads, HEAD_DIM
        )
        for part in (key_rows, value_rows)
    ]
    (_, total, accum), _ = lax.scan(
        advance, initial, (*tiles, jnp.arange(block_count, dtype=jnp.int32))
    )
    attended = (
        (accum / total[..., None]).transpose(1, 0, 2).reshape(row_count, local_width).astype(BF16)
    )
    partial_out = jnp.dot(attended, w_out, preferred_element_type=F32)
    return lax.psum_scatter(partial_out.astype(BF16), "head", scatter_dimension=1, tiled=True)


def solution(mesh):
    in_specs = (
        P("ctx", "head"),
        P(),
        P(),
        P(None, "head"),
        P(None, "head"),
        P(None, "head"),
        P("head", None),
    )

    def per_device(tokens, block_order, block_mask, w_query, w_key, w_value, w_out):
        args = (tokens, block_order, block_mask, w_query, w_key, w_value, w_out)
        heads = w_query.shape[1] // HEAD_DIM
        fits = mesh.shape["ctx"] == Z * X * C and mesh.shape["head"] == 2 and heads % Z == 0
        return split_heads(*args) if fits else gather_all(*args)

    return jax.shard_map(
        per_device, mesh=mesh, in_specs=in_specs, out_specs=P("ctx", "head"), check_vma=False
    )
```

```python
import functools
import math

import jax
import jax.numpy as jnp
from jax import lax
from jax.experimental import pallas as pl
from jax.experimental.pallas import tpu as pltpu
from jax.sharding import PartitionSpec as P

HEAD_DIM = 128
BLOCK = 128
Z, X, C = 4, 2, 2
MIB = 1 << 20
BF16, F32 = jnp.bfloat16, jnp.float32
LIGHT = pl.CostEstimate(flops=1024, bytes_accessed=1024, transcendentals=0)
SOME = pl.CostEstimate(flops=1024, bytes_accessed=1 << 20, transcendentals=0)


def place(z, x, c):
    return (z * X + x) * C + c


def hop(dz, dx, dc):
    return [
        (place(z, x, c), place(z ^ dz, x ^ dx, c ^ dc))
        for z in range(Z)
        for x in range(X)
        for c in range(C)
    ]


def params(mib):
    return pltpu.CompilerParams(vmem_limit_bytes=mib * MIB)


def after(value, *others):
    return lax.optimization_barrier((value, *others))[0]


def whole(count):
    return [pl.BlockSpec(memory_space=pltpu.VMEM)] * count


def fetch(where, weights, width, groups, fence, beside=None):
    depth = weights[0].shape[0]
    half = depth // 2
    kinds = len(weights)
    extra = list(beside or ())

    def body(s, *refs):
        out, sems = refs[kinds + 1 + len(extra)], refs[-1]
        copies = []
        for g in range(2):
            columns = pl.ds(pl.multiple_of((s[1] ^ groups[g]) * width, width), width)
            for k in range(kinds):
                for part in range(2):
                    rows = pl.ds(pl.multiple_of((s[0] ^ part) * half, half), half)
                    copies.append(
                        pltpu.make_async_copy(
                            refs[k].at[rows, columns],
                            out.at[g * kinds + k, pl.ds(part * half, half)],
                            sems.at[len(copies)],
                        )
                    )
        for copy in copies:
            copy.start()
        if extra:
            tokens_ref, held_ref = refs[kinds + 1 : kinds + 3]
            for i in range(2 * kinds):
                refs[-2][i] = jnp.dot(
                    tokens_ref[...], held_ref[i, :half], preferred_element_type=F32
                )
        for copy in copies:
            copy.wait()

    out_shape = [pltpu.VMEM((2 * kinds, depth, width), BF16)]
    if extra:
        out_shape.append(pltpu.VMEM((2 * kinds, extra[0].shape[0], width), F32))
    return pl.pallas_call(
        body,
        grid_spec=pltpu.PrefetchScalarGridSpec(
            num_scalar_prefetch=1,
            grid=(),
            in_specs=[pl.BlockSpec(memory_space=pl.ANY)] * (kinds + 1) + whole(len(extra)),
            out_specs=whole(len(out_shape)),
            scratch_shapes=[pltpu.SemaphoreType.DMA((4 * kinds,))],
        ),
        out_shape=out_shape,
        compiler_params=params(4),
        cost_estimate=LIGHT,
    )(where, *weights, fence, *extra)


def project(own, other, held, outputs, start=0, partial=None):
    rows = own.shape[0] - start
    kinds = held.shape[0] // 2
    flat = [block for blocks in outputs for block in blocks]

    def body(*refs):
        held_ref, outs = refs[2], refs[3:]
        tokens, low = jnp.concatenate([refs[0][start:], refs[1][start:]], axis=1), 0
        if partial is not None:
            tokens, low, outs = refs[1][start:], own.shape[1], refs[4:]
        at = [(o, i) for o, blocks in enumerate(outputs) for i in range(len(blocks))]
        for first in range(0, len(flat), 2):
            pair = flat[first : first + 2]
            weight = [
                held_ref[g * kinds + k, low:, h * HEAD_DIM : (h + 1) * HEAD_DIM] for g, k, h in pair
            ]
            total = jnp.dot(
                tokens, jnp.concatenate(weight, axis=1), preferred_element_type=F32
            )
            if partial is not None:
                done = [
                    refs[3][g * kinds + k, :, h * HEAD_DIM : (h + 1) * HEAD_DIM] for g, k, h in pair
                ]
                total = total + jnp.concatenate(done, axis=1)
            total = total.astype(BF16)
            for i in range(len(pair)):
                o, place_in = at[first + i]
                outs[o][place_in] = total[:, i * HEAD_DIM : (i + 1) * HEAD_DIM]

    more = [] if partial is None else [partial]
    return pl.pallas_call(
        body,
        in_specs=whole(3 + len(more)),
        out_specs=whole(len(outputs)),
        out_shape=[jax.ShapeDtypeStruct((len(b), rows, HEAD_DIM), BF16) for b in outputs],
        compiler_params=params(8),
        cost_estimate=LIGHT,
    )(own, other, held, *more)


def take(array, ranges):
    def body(in_ref, *outs):
        for out, (first, last) in zip(outs, ranges):
            out[...] = in_ref[first:last]

    return pl.pallas_call(
        body,
        in_specs=whole(1),
        out_specs=whole(len(ranges)),
        out_shape=[
            jax.ShapeDtypeStruct((last - first,) + array.shape[1:], array.dtype)
            for first, last in ranges
        ],
        compiler_params=params(4),
        cost_estimate=LIGHT,
    )(array)


def pack(sides, picks):
    arrays = [a for side in sides for half in side for a in half]
    rows = sum(half[0].shape[1] for half in sides[0])

    def body(*refs):
        ins, outs = list(refs[: len(arrays)]), refs[len(arrays) :]
        blocks = []
        for side in sides:
            for half in side:
                blocks.append([])
                for a in half:
                    ref = ins.pop(0)
                    blocks[-1] += [(ref, b) for b in range(a.shape[0])]
        for out, wanted in zip(outs, picks):
            for n, (side, upper, lower) in enumerate(wanted):
                ref, b = blocks[2 * side][upper]
                size = ref.shape[1]
                out[n, :size] = ref[b]
                ref, b = blocks[2 * side + 1][lower]
                out[n, size:] = ref[b]

    return pl.pallas_call(
        body,
        in_specs=whole(len(arrays)),
        out_specs=whole(len(picks)),
        out_shape=[jax.ShapeDtypeStruct((len(p), rows, HEAD_DIM), BF16) for p in picks],
        compiler_params=params(4),
        cost_estimate=LIGHT,
    )(*arrays)


def mask_rows(where, block_order, block_mask, rows):
    blocks = block_order.shape[0]
    per = rows // BLOCK
    keys = blocks * BLOCK

    def body(s, order_ref, mask_ref, out_ref):
        def ids(shape, axis, shift):
            at = lax.broadcasted_iota(jnp.int32, shape, axis) >> shift
            piece = at >> (per.bit_length() - 1)
            return at & (per - 1), piece

        hot = (order_ref[...] == lax.broadcasted_iota(jnp.int32, (blocks, blocks), 0)).astype(F32)
        low, piece = ids((Z * per, blocks), 0, 0)
        want = (place(s[1] ^ piece, s[2], s[3])) * per + low
        query = (want == lax.broadcasted_iota(jnp.int32, (Z * per, blocks), 1)).astype(F32)
        low, piece = ids((blocks, keys), 1, BLOCK.bit_length() - 1)
        want = place(s[1] ^ (piece >> 2), s[2] ^ (piece & 1), s[3] ^ ((piece >> 1) & 1)) * per + low
        key = (want == lax.broadcasted_iota(jnp.int32, (blocks, keys), 0)).astype(F32)
        frames = lax.dot_general(query, hot, (((1,), (1,)), ((), ())), preferred_element_type=F32)
        live = jnp.dot(frames, mask_ref[...].astype(F32), preferred_element_type=F32)
        live = jnp.dot(live, hot, preferred_element_type=F32)
        live = jnp.dot(live, key, preferred_element_type=F32)
        out_ref[...] = jnp.where(live > 0.5, 0.0, -1e30)

    return pl.pallas_call(
        body,
        grid_spec=pltpu.PrefetchScalarGridSpec(
            num_scalar_prefetch=1, grid=(), in_specs=whole(2), out_specs=whole(1)[0]
        ),
        out_shape=jax.ShapeDtypeStruct((Z * per, keys), F32),
        compiler_params=params(8),
        cost_estimate=LIGHT,
    )(where, block_order[None, :], block_mask)


def attend(steps, parts, stride, bias, mask_at, mask_stride, key_at, outputs, earlier, fences):
    tile = parts[0][0].shape[1]
    n, count = len(parts), len(steps)
    scale = math.log2(math.e) / math.sqrt(HEAD_DIM)
    every = sum(q[3] for q in steps[0][0])
    width = n * tile
    carried = bool(steps[0][1])
    arrays = []

    def index_of(array):
        for i, known in enumerate(arrays):
            if known is array:
                return i
        arrays.append(array)
        return len(arrays) - 1

    plan = [
        (
            [(index_of(q), *rest) for q, *rest in queries],
            [([index_of(a) for a in held], *rest) for held, *rest in states],
            results,
        )
        for queries, states, results in steps
    ]
    part_plan = [(index_of(p[0]), p[1], index_of(p[2]), p[3]) for p in parts]
    earlier_plan = [(index_of(a), low, out) for a, low, out in earlier]
    bias_index = index_of(bias)
    total_arrays = len(arrays)

    def body(*refs):
        ins = refs[:total_arrays]
        outs = refs[total_arrays + len(fences) :]
        q_ref = outs[-1 - (3 if carried else 0)]
        held_refs = outs[len(outs) - 3 :]
        step = pl.program_id(0)
        for i, (queries, states, _) in enumerate(plan):

            @pl.when(step == i)
            def _(i=i, queries=queries, states=states):
                at = 0
                for q, block, low, size in queries:
                    q_ref[at : at + size] = ins[q][block, low : low + size]
                    at += size
                at = 0
                for held, block, low, size in states:
                    for k in range(3):
                        held_refs[k][at : at + size] = ins[held[k]][block, low : low + size]
                    at += size
                if i == 0:
                    for a, low, out in earlier_plan:
                        outs[out][:, :HEAD_DIM] = ins[a][low : low + outs[out].shape[0]]

        shift = step * stride
        key = jnp.concatenate([ins[k][at + shift] for k, at, _, _ in part_plan], axis=0)
        value = jnp.concatenate([ins[v][at + shift] for _, _, v, at in part_plan], axis=0)
        if carried:
            top, total, accum = held_refs[0][:, :1], held_refs[1][...], held_refs[2][...]
        else:
            top = jnp.full((every, 1), -1e30, F32)
            total = jnp.zeros((every, HEAD_DIM), F32)
            accum = jnp.zeros((every, HEAD_DIM), F32)
        score = lax.dot_general(
            q_ref[...], key, (((1,), (1,)), ((), ())), preferred_element_type=F32
        )
        columns = slice(key_at * tile, key_at * tile + width)
        keep = [
            jnp.broadcast_to(
                ins[bias_index][pl.ds(row + step * mask_stride, 1), columns], (BLOCK, width)
            )
            for row in mask_at
        ]
        score = score + jnp.concatenate(keep, axis=0)
        best = score[:, :HEAD_DIM]
        for u in range(HEAD_DIM, width, HEAD_DIM):
            best = jnp.maximum(best, score[:, u : u + HEAD_DIM])
        top_next = jnp.maximum(top, jnp.max(best, axis=1, keepdims=True))
        factor = jnp.exp2((top - top_next) * scale)
        weight = jnp.exp2((score - top_next) * scale)
        add = weight[:, :HEAD_DIM]
        for u in range(HEAD_DIM, width, HEAD_DIM):
            add = add + weight[:, u : u + HEAD_DIM]
        total = total * factor + add
        accum = accum * factor + jnp.dot(weight.astype(BF16), value, preferred_element_type=F32)
        if outputs is None:
            outs[0][step] = jnp.broadcast_to(top_next, (every, HEAD_DIM))
            outs[1][step] = total
            outs[2][step] = accum
            return
        result = (accum / jnp.sum(total, axis=1, keepdims=True)).astype(BF16)
        for i, (queries, _, results) in enumerate(plan):

            @pl.when(step == i)
            def _(queries=queries, results=results):
                at = 0
                for (_, _, _, size), (out, head) in zip(queries, results):
                    lanes = slice(head * HEAD_DIM, (head + 1) * HEAD_DIM)
                    outs[out][:, lanes] = result[at : at + size]
                    at += size

    if outputs is None:
        out_shape = [jax.ShapeDtypeStruct((count, every, HEAD_DIM), F32)] * 3
    else:
        out_shape = [jax.ShapeDtypeStruct(shape, BF16) for shape in outputs]
    return pl.pallas_call(
        body,
        grid=(count,),
        in_specs=whole(total_arrays) + [pl.BlockSpec(memory_space=pl.ANY)] * len(fences),
        out_specs=whole(len(out_shape)),
        out_shape=out_shape,
        scratch_shapes=[pltpu.VMEM((every, HEAD_DIM), BF16)]
        + [pltpu.VMEM((every, HEAD_DIM), F32)] * (3 if carried else 0),
        compiler_params=params(24),
        cost_estimate=LIGHT,
    )(*arrays, *fences)


def fetch_out(where, w_out, fence):
    depth, width = w_out.shape
    group, half = depth // Z, width // 2

    def body(s, w_ref, fence_ref, out, sems):
        copies = []
        for dz in range(Z):
            rows = pl.ds(pl.multiple_of((s[1] ^ dz) * group, group), group)
            for part in range(2):
                columns = pl.ds(pl.multiple_of((1 - s[0] if part == 0 else s[0]) * half, half), half)
                copies.append(
                    pltpu.make_async_copy(
                        w_ref.at[rows, columns],
                        out.at[pl.ds(dz * group, group), pl.ds(part * half, half)],
                        sems.at[len(copies)],
                    )
                )
        for copy in copies:
            copy.start()
        for copy in copies:
            copy.wait()

    return pl.pallas_call(
        body,
        grid_spec=pltpu.PrefetchScalarGridSpec(
            num_scalar_prefetch=1,
            grid=(),
            in_specs=[pl.BlockSpec(memory_space=pl.ANY)] * 2,
            out_specs=whole(1)[0],
            scratch_shapes=[pltpu.SemaphoreType.DMA((2 * Z,))],
        ),
        out_shape=pltpu.VMEM((depth, width), BF16),
        compiler_params=params(4),
        cost_estimate=LIGHT,
    )(where, w_out, fence)


def mix(attended, held, part):
    rows = attended[0].shape[0]
    half = held.shape[1] // 2
    count = len(attended)
    step = half // 3

    def body(*refs):
        rows_all = jnp.concatenate([r[...] for r in refs[:count]], axis=1)
        for i in range(3):
            weight = refs[count][:, part * half + i * step : part * half + (i + 1) * step]
            refs[-1][:, i * step : (i + 1) * step] = jnp.dot(
                rows_all, weight, preferred_element_type=F32
            ).astype(BF16)

    return pl.pallas_call(
        body,
        in_specs=whole(count + 1),
        out_specs=whole(1)[0],
        out_shape=jax.ShapeDtypeStruct((rows, half), BF16),
        compiler_params=params(16),
        cost_estimate=LIGHT,
    )(*attended, held)


def finish(home, arrived, above, cost):
    rows, width = home.shape
    low = 0 if above is None else rows
    more = [] if above is None else [above]

    def body(*refs):
        total_ref, sem = refs[-2:]
        total = refs[0][...].astype(F32) + refs[1][...].astype(F32)
        total_ref[...] = total.astype(BF16)
        copy = pltpu.make_async_copy(total_ref, refs[-3].at[pl.ds(low, rows)], sem)
        copy.start()
        copy.wait()

    return pl.pallas_call(
        body,
        in_specs=whole(2) + [pl.BlockSpec(memory_space=pl.ANY)] * len(more),
        out_specs=pl.BlockSpec(memory_space=pl.ANY),
        out_shape=jax.ShapeDtypeStruct((2 * rows, width), BF16),
        scratch_shapes=[pltpu.VMEM((rows, width), BF16), pltpu.SemaphoreType.DMA(())],
        input_output_aliases={} if above is None else {2: 0},
        compiler_params=params(8),
        cost_estimate=cost,
    )(home, arrived, *more)


def split_heads(tokens, block_order, block_mask, w_query, w_key, w_value, w_out):
    rows, half = tokens.shape
    group_heads = w_query.shape[1] // HEAD_DIM // Z
    per = rows // BLOCK
    cut = rows * 9 // 16
    ctx = lax.axis_index("ctx")
    y = lax.axis_index("head")
    where = jnp.stack([y, ctx // (X * C), (ctx // C) % X, ctx % C]).astype(jnp.int32)
    weights = [pltpu.with_memory_space_constraint(w, pltpu.HBM) for w in (w_query, w_key, w_value)]
    w_out = pltpu.with_memory_space_constraint(w_out, pltpu.HBM)
    heads = range(group_heads)
    span = group_heads * HEAD_DIM

    def over_y(a):
        return lax.ppermute(a, "head", [(0, 1), (1, 0)])

    def over(a, dz, dx, dc):
        return lax.ppermute(a, "ctx", hop(dz, dx, dc))

    def pairs(group, wanted):
        return [(group, kind, h) for kind in (1, 2) for h in wanted]

    def singles(group):
        return [(group, 0, h) for h in heads]

    other = over_y(tokens)
    far = over(tokens[:cut], 2, 0, 0)
    (held,) = fetch(where, weights, span, (0, 1), where)
    held_far, partial = fetch(where, weights, span, (2, 3), where, (tokens, held))

    other = after(other, held_far)
    own_kv, sent = project(
        tokens,
        other,
        held,
        [pairs(0, heads), singles(1) + pairs(1, heads)],
        partial=partial,
    )
    came = over(sent, 1, 0, 0)
    own_across = over(own_kv, 0, 1, 0)
    own_core = over(own_kv, 0, 0, 1)
    far = after(far, sent)
    far_other = over_y(far)
    low2, low3 = project(
        after(tokens, far),
        other,
        held_far,
        [singles(0) + pairs(0, heads), singles(1) + pairs(1, heads)],
        cut,
    )
    (own_q,) = project(
        after(tokens, own_core, low2), other, held, [singles(0)], partial=partial
    )
    low2 = over(low2, 2, 0, 0)
    low3 = over(low3, 3, 0, 0)
    bias = mask_rows(after(where, own_q), block_order, block_mask, rows)
    out_held = fetch_out(where, w_out, bias)
    own_across = after(own_across, out_held)
    own_across_core = over(own_across, 0, 0, 1)

    far_sent_q, far_sent, far_kept = project(
        far,
        after(far_other, out_held),
        held,
        [singles(1), pairs(1, heads), singles(0) + pairs(0, heads)],
    )
    far_came_q = over(far_sent_q, 1, 0, 0)
    far_came = over(far_sent, 1, 0, 0)
    came = after(came, far_sent, own_across)
    n = group_heads
    came_kv, came_k, came_v = take(came, [(n, 3 * n), (n, 2 * n), (2 * n, 3 * n)])
    across_k = over(came_k, 0, 1, 0)
    across_v = over(came_v, 0, 1, 0)
    came_core = over(came_kv, 0, 0, 1)
    far_came = after(far_came, low2, low3)
    across_k, across_v = after(across_k, far_came), after(across_v, far_came)
    across_core_k = over(across_k, 0, 0, 1)
    across_core_v = over(across_v, 0, 0, 1)

    first, rest = (0,), tuple(heads)[1:]
    sides = [[[far_kept], [low2]], [[far_came], [low3]]]

    def picks(chunk):
        kept = [(0, k * n + h, k * n + h) for k in (1, 2) for h in chunk]
        return kept + [(1, (k - 1) * n + h, k * n + h) for k in (1, 2) for h in chunk]

    far_first, far_rest, far_q = pack(
        sides, [picks(first), picks(rest), [(0, h, h) for h in heads]]
    )
    first_across = over(far_first, 0, 1, 0)
    first_core = over(far_first, 0, 0, 1)
    rest_across = over(far_rest, 0, 1, 0)
    rest_core = over(far_rest, 0, 0, 1)

    near = [(a, 0, a, n) for a in (own_kv, own_across, own_core, own_across_core)]
    near += [
        (came_kv, 0, came_kv, n),
        (across_k, 0, across_v, 0),
        (came_core, 0, came_core, n),
        (across_core_k, 0, across_core_v, 0),
    ]

    def whole_rows(arrays, j):
        return [(a, j, 0, rows) for a in arrays]

    state_near = attend(
        [(whole_rows([own_q, came], j), [], []) for j in heads],
        near,
        1,
        bias,
        range(2 * per),
        0,
        0,
        None,
        [],
        [far_first],
    )
    (far_came_q,) = pack(
        [[[after(far_came_q, state_near[0])], [low3]]], [[(0, h, h) for h in heads]]
    )
    state_far = attend(
        [(whole_rows([far_q, far_came_q], j), [], []) for j in heads],
        near,
        1,
        bias,
        range(2 * per, 4 * per),
        0,
        0,
        None,
        [],
        [state_near[0]],
    )
    first_across = after(first_across, state_far[0])
    first_across_core = over(first_across, 0, 0, 1)

    def far_parts(arrays, size):
        return [(a, 2 * i * size, a, (2 * i + 1) * size) for i in range(2) for a in arrays]

    first_rows = attend(
        [
            (whole_rows([own_q, came], 0), [(state_near, 0, 0, 2 * rows)], [(0, 0), (1, 0)]),
            (whole_rows([far_q, far_came_q], 0), [(state_far, 0, 0, 2 * rows)], [(2, 0), (3, 0)]),
        ],
        far_parts([far_first, first_across, first_core, first_across_core], 1),
        0,
        bias,
        range(2 * per),
        2 * per,
        len(near),
        [(rows, HEAD_DIM)] * Z,
        [],
        [],
    )
    rest_across = after(rest_across, first_rows[0])
    rest_across_core = over(rest_across, 0, 0, 1)
    rest_parts = far_parts([far_rest, rest_across, rest_core, rest_across_core], len(rest))
    homes, arrived, fences = [], [], []
    for low in range(0, rows, BLOCK):
        steps = [
            (
                [(a, j, low, BLOCK) for a in (own_q, came, far_q, far_came_q)],
                [(s, j, i * rows + low, BLOCK) for s in (state_near, state_far) for i in range(2)],
                [(i, j) for i in range(Z)],
            )
            for j in rest
        ]
        done = attend(
            steps,
            rest_parts,
            1,
            bias,
            [i * per + low // BLOCK for i in range(Z)],
            0,
            len(near),
            [(BLOCK, span)] * Z,
            [(first_rows[i], low, i) for i in range(Z)],
            fences,
        )
        fences = [done[0]]
        back = [done[0]] + [over(done[dz], dz, 0, 0) for dz in range(1, Z)]
        if arrived:
            back[-1] = after(back[-1], homes[0])
        away = mix(back, out_held, 0)
        arrived.append(over_y(away))
        homes.append(mix(back[:-1] + [after(back[-1], away)], out_held, 1))
    upper = finish(homes[0], arrived[0], None, SOME)
    return finish(homes[1], after(arrived[1], upper), upper, LIGHT)


def gather_all(tokens, block_order, block_mask, w_query, w_key, w_value, w_out):
    row_count = tokens.shape[0]
    local_width = w_query.shape[1]
    local_heads = local_width // HEAD_DIM
    block_count = block_order.shape[0]
    portion = lax.all_gather(tokens, "head", axis=1, tiled=True)
    query_rows, key_rows, value_rows = [
        jnp.dot(portion, weight, preferred_element_type=F32)
        .astype(BF16)
        .reshape(row_count, local_heads, HEAD_DIM)
        for weight in (w_query, w_key, w_value)
    ]
    cycle_live = block_mask[block_order][:, block_order]
    row_blocks = (
        lax.axis_index("ctx") * row_count + jnp.arange(row_count, dtype=jnp.int32)
    ) // BLOCK
    live_columns = cycle_live[row_blocks].T
    inv_root = 1.0 / HEAD_DIM**0.5

    def advance(state, inputs):
        key_tile, value_tile, offset = inputs
        keep = lax.dynamic_index_in_dim(live_columns, offset, 0, keepdims=False) > 0
        top_now, total_now, accum = state
        scores = (
            jnp.einsum("qhd,khd->hqk", query_rows, key_tile, preferred_element_type=F32)
            * inv_root
        )
        allowed = keep[None, :, None]
        top_next = jnp.maximum(top_now, jnp.max(jnp.where(allowed, scores, -1e30), axis=-1))
        factor = jnp.exp(top_now - top_next)
        weights = jnp.where(allowed, jnp.exp(scores - top_next[..., None]), 0.0)
        total_next = total_now * factor + jnp.sum(weights, axis=-1)
        accum = accum * factor[..., None] + jnp.einsum(
            "hqk,khd->hqd", weights.astype(BF16), value_tile, preferred_element_type=F32
        )
        return (top_next, total_next, accum), None

    initial = (
        jnp.full((local_heads, row_count), -1e30, F32),
        jnp.zeros((local_heads, row_count), F32),
        jnp.zeros((local_heads, row_count, HEAD_DIM), F32),
    )
    tiles = [
        lax.all_gather(part, "ctx", axis=0, tiled=True).reshape(
            block_count, BLOCK, local_heads, HEAD_DIM
        )
        for part in (key_rows, value_rows)
    ]
    (_, total, accum), _ = lax.scan(
        advance, initial, (*tiles, jnp.arange(block_count, dtype=jnp.int32))
    )
    attended = (
        (accum / total[..., None]).transpose(1, 0, 2).reshape(row_count, local_width).astype(BF16)
    )
    partial_out = jnp.dot(attended, w_out, preferred_element_type=F32)
    return lax.psum_scatter(partial_out.astype(BF16), "head", scatter_dimension=1, tiled=True)


def solution(mesh):
    in_specs = (
        P("ctx", "head"),
        P(),
        P(),
        P(None, "head"),
        P(None, "head"),
        P(None, "head"),
        P("head", None),
    )

    def per_device(tokens, block_order, block_mask, w_query, w_key, w_value, w_out):
        args = (tokens, block_order, block_mask, w_query, w_key, w_value, w_out)
        heads = w_query.shape[1] // HEAD_DIM
        fits = mesh.shape["ctx"] == Z * X * C and mesh.shape["head"] == 2 and heads % Z == 0
        return split_heads(*args) if fits else gather_all(*args)

    return jax.shard_map(
        per_device, mesh=mesh, in_specs=in_specs, out_specs=P("ctx", "head"), check_vma=False
    )
```
